32 devices in a mesh: grp: 2 (over x), seq: 16 (over z, y, core).
Axes of the slice: x: 2, y: 2, z: 4, core: 2. Of those that a mesh axis runs over, the one named last changes fastest.
Arguments:
- layer_input: bfloat16 [2, 8192, 1024], P('grp', 'seq'), may hold values from -6 to 6
- segment_ids: int32 [2, 8192], P('grp', 'seq'), may hold values from 0 to 15, never falling along the last dimension, each value on 1 to 2048 neighbouring positions
- context_mask: int32 [2, 16, 128], P('grp', 'seq'), may hold values 0 or 1
- first_gain: float32 [1024], replicated, may hold values from 0.5 to 1.5
- attention_in: bfloat16 [1024, 3072], replicated, may hold values from -0.1875 to 0.1875
- kernel_weight: float32 [1024, 16], replicated, may hold values from -1.5 to 1.5
- kernel_decay: float32 [1024, 16], replicated, may hold values from -1 to 7
- attention_out: bfloat16 [1024, 1024], replicated, may hold values from -0.75 to 0.75
- second_gain: float32 [1024], replicated, may hold values from 0.5 to 1.5
- expand_weight: bfloat16 [1024, 4096], replicated, may hold values from -0.1875 to 0.1875
- reduce_weight: bfloat16 [4096, 1024], replicated, may hold values from -0.09375 to 0.09375
- cotangent: bfloat16 [2, 8192, 1024], P('grp', 'seq'), may hold values from -6 to 6
Outputs:
- layer_output: bfloat16 [2, 8192, 1024], P('grp', 'seq')
- input_grad: float32 [2, 8192, 1024], P('grp', 'seq')
- first_gain_grad: float32 [1024], P('seq')
- attention_in_grad: float32 [1024, 3072], P('seq')
- kernel_weight_grad: float32 [1024, 16], P('seq')
- kernel_decay_grad: float32 [1024, 16], P('seq')
- attention_out_grad: float32 [1024, 1024], P('seq')
- second_gain_grad: float32 [1024], P('seq')
- expand_weight_grad: float32 [1024, 4096], P('seq')
- reduce_weight_grad: float32 [4096, 1024], P('seq')
The draws below stay inside these ranges and needn't reach their ends.
Inputs may be any that keep to these rules, and one draw needn't show every extreme that they name: `segment_ids`: within a sequence segment numbers never fall; each document has 1 to 2048 positions, and one has exactly that many.
All inputs are finite; a program needn't handle non-finite values. No bound on the sum of `context_mask` on one device may be relied on, other than what follows from the above.
Results may differ from the reference program's by a relative error of at most 0.015.
Values may be sent and summed in bfloat16 or wider, within the bound.
A program may use at most 256 MiB of HBM per device.

```python
import math
import jax
import jax.numpy as jnp
import numpy as np
from jax import lax

D = 1024
HEADS = 8
HEAD_DIM = 128
FF = 4096
NST = 16
BLK = 512
CTX = 128
SEQLEN = 8192
ROWS = 2


def place_ends(values, key, smallest, largest):
    longest = values.shape.index(max(values.shape))
    spots = []
    for shift in (0, 1):
        where = [jax.random.randint(jax.random.fold_in(key, axis), (), 0, length) for axis, length in enumerate(values.shape)]
        where[longest] = (where[longest] + shift) % values.shape[longest]
        spots.append(tuple(where))
    return values.at[spots[0]].set(smallest).at[spots[1]].set(largest)


def block_scale(key, shape, cuts, low, high):
    level = 1.0
    for axis_at, shards_of in cuts:
        heights = jax.random.uniform(jax.random.fold_in(jax.random.fold_in(key, 6), axis_at), (shards_of,), jnp.float32, low / len(cuts), high / len(cuts))
        level = level * jnp.repeat(jnp.exp(heights), shape[axis_at] // shards_of).reshape((-1,) + (1,) * (len(shape) - 1 - axis_at))
    return level


def split_up(amount, total, limit, skew):
    weights = [(1 << 20) // math.isqrt(rank ** skew) + 1 for rank in range(2, amount + 1)]
    surplus, counts = total - limit - (amount - 1), [1] * (amount - 1)
    while surplus > 0:
        movable = [i for i in range(amount - 1) if counts[i] < limit]
        whole, remaining = sum([weights[i] for i in movable]), surplus
        for i in movable:
            more = min(limit - counts[i], max(1, remaining * weights[i] // whole), surplus)
            counts[i] = counts[i] + more
            surplus = surplus - more
    return np.array([limit] + counts)


def uneven_parts(key, amount, total, reach, skew):
    if amount == 2:
        one = jax.random.randint(key, (), max(1, total - reach), min(reach, total - 1) + 1)
        return jnp.stack([one, total - one])
    lengths = jnp.asarray(split_up(amount, total, reach, skew), jnp.int32)
    couples = (amount - 1) // 2
    source_of, sink = lengths[1:1 + 2 * couples:2], lengths[2:2 + 2 * couples:2]
    margin = jnp.minimum(source_of - 1, reach - sink)
    shifted = jax.random.randint(jax.random.fold_in(key, 1), (couples,), 0, 1 << 20) % (margin + 1)
    lengths = lengths.at[1:1 + 2 * couples:2].set(source_of - shifted).at[2:2 + 2 * couples:2].set(sink + shifted)
    return lengths[jax.random.permutation(jax.random.fold_in(key, 2), amount)]


def noise(key, shape, scale, limit, cuts=(), kind=jnp.bfloat16):
    entries = scale * jax.random.normal(key, shape, jnp.float32)
    if cuts:
        entries = entries * block_scale(key, shape, cuts, -0.22, 0.18)
    return jnp.clip(entries, -limit, limit).astype(kind)


def setup_inputs(seed: int = 0) -> dict:
    arg_keys = jax.random.split(jax.random.key(seed), 13)
    layer_input = noise(arg_keys[0], (ROWS, SEQLEN, D), 1.0, 6.0, ((0, 2), (1, 16)))
    segment_ids = jax.vmap(lambda own: jnp.searchsorted(jnp.cumsum(uneven_parts(own, SEQLEN // BLK, SEQLEN, 4 * BLK, 2)), jnp.arange(SEQLEN), side="right"))(jax.random.split(arg_keys[1], ROWS)).reshape((ROWS, SEQLEN)).astype(jnp.int32)
    context_mask = place_ends((jax.random.randint(arg_keys[2], (ROWS, SEQLEN // BLK, CTX), 0, 4) < 3).astype(jnp.int32), jax.random.fold_in(arg_keys[2], 1), 0, 1)
    first_gain = jnp.clip(1.0 + 0.1 * jax.random.normal(arg_keys[3], (D,), jnp.float32), 0.5, 1.5)
    attention_in = noise(arg_keys[4], (D, 3 * D), D ** -0.5, 0.1875)
    kernel_weight = noise(arg_keys[5], (D, NST), NST ** -0.5, 1.5, (), jnp.float32)
    kernel_decay = jnp.clip(jax.random.uniform(arg_keys[6], (D, NST), jnp.float32, -1.0, 7.0), -1.0, 7.0)
    attention_out = noise(arg_keys[7], (D, D), (D // 16) ** -0.5, 0.75)
    second_gain = jnp.clip(1.0 + 0.1 * jax.random.normal(arg_keys[8], (D,), jnp.float32), 0.5, 1.5)
    expand_weight = noise(arg_keys[9], (D, FF), D ** -0.5, 0.1875)
    reduce_weight = noise(arg_keys[10], (FF, D), FF ** -0.5, 0.09375)
    cotangent = noise(arg_keys[11], (ROWS, SEQLEN, D), 1.0, 6.0, ((0, 2), (1, 16)))
    return {"layer_input": layer_input, "segment_ids": segment_ids, "context_mask": context_mask, "first_gain": first_gain, "attention_in": attention_in, "kernel_weight": kernel_weight, "kernel_decay": kernel_decay, "attention_out": attention_out, "second_gain": second_gain, "expand_weight": expand_weight, "reduce_weight": reduce_weight, "cotangent": cotangent}


@jax.custom_vjp
def low(v):
    return lax.optimization_barrier(v.astype(jnp.bfloat16)).astype(jnp.float32)

@jax.custom_vjp
def low_back(v):
    return v

def low_keep(v):
    return (low(v), None)

def low_pass(kept, grad):
    return (grad,)

def back_keep(v):
    return (v, None)

def back_low(kept, grad):
    return (low(grad),)
low.defvjp(low_keep, low_pass)
low_back.defvjp(back_keep, back_low)
epsilon = 1e-05
highest = lax.Precision.HIGHEST
masked_score = -1e+30

def layer_norm(matrix, scales):
    centre = matrix - lax.optimization_barrier(jnp.mean(matrix, axis=-1, keepdims=True))
    spread = lax.optimization_barrier(jnp.mean(centre * centre, axis=-1, keepdims=True))
    return centre * lax.rsqrt(spread + epsilon) * scales

def exact_product(operand, partner):
    return jnp.dot(operand, partner, precision=highest, preferred_element_type=jnp.float32)

def activation(values_in):
    return jax.nn.gelu(values_in, approximate=True)

def lag_kernel(weights, decays):
    decay_rates = jnp.exp(decays) / SEQLEN
    lag_steps = jnp.arange(SEQLEN, dtype=jnp.float32)
    return jnp.einsum('cn,cnl->cl', weights * jnp.sqrt(decay_rates), jnp.exp(-decay_rates[:, :, None] * lag_steps), precision=highest)

def causal_convolution(signal, kernel_rows):
    padded_length = 2 * SEQLEN
    spectrum = jnp.fft.rfft(signal, n=padded_length, axis=0) * jnp.fft.rfft(kernel_rows.T, n=padded_length, axis=0)
    return jnp.fft.irfft(spectrum, n=padded_length, axis=0)[:SEQLEN]

def attend_block(pieces):
    queries, keys_all, values_all, segments, visible_row, block_index = pieces
    offsets = jnp.arange(BLK)
    inside = (offsets[None, :] <= offsets[:, None]) & (segments[None, :] == segments[:, None])
    visible = (visible_row == 1) & (block_index > 0)
    allowed = jnp.concatenate([inside, jnp.broadcast_to(visible[None, :], (BLK, CTX))], axis=1)
    heads_query = queries.reshape(BLK, HEADS, HEAD_DIM)
    heads_key = keys_all.reshape(BLK + CTX, HEADS, HEAD_DIM)
    heads_value = values_all.reshape(BLK + CTX, HEADS, HEAD_DIM)
    raw_scores = low_back(jnp.einsum('qhd,khd->hqk', heads_query, heads_key, precision=highest) / math.sqrt(HEAD_DIM))
    scores = jnp.where(allowed[None], raw_scores, masked_score)
    row_top = lax.optimization_barrier(jnp.max(scores, axis=-1, keepdims=True))
    exponent = jnp.exp(scores - row_top)
    probabilities = low(exponent / lax.optimization_barrier(jnp.sum(exponent, axis=-1, keepdims=True)))
    mixture = jnp.einsum('hqk,khd->qhd', probabilities, heads_value, precision=highest)
    return mixture.reshape(BLK, HEADS * HEAD_DIM)

def row_forward(row_input, segment_row, mask_row, kernel_rows, params):
    block_count = SEQLEN // BLK
    first_low = low(layer_norm(row_input, params[0]))
    packed = low(low_back(exact_product(first_low, params[1])))
    convolved = causal_convolution(low_back(first_low), kernel_rows)
    states = low(low_back(convolved))
    tail_rows = states.reshape(block_count, BLK, D)[:, BLK - CTX:]
    context = jnp.concatenate([jnp.zeros((1, CTX, D), jnp.float32), tail_rows[:-1]], axis=0)
    context_pairs = low(low_back(exact_product(context.reshape(block_count * CTX, D), params[1][:, D:])))
    context_pairs = context_pairs.reshape(block_count, CTX, 2 * D)
    grouped = packed.reshape(block_count, BLK, 3 * D)
    keys_all = jnp.concatenate([grouped[:, :, D:2 * D], context_pairs[:, :, :D]], axis=1)
    values_all = jnp.concatenate([grouped[:, :, 2 * D:], context_pairs[:, :, D:]], axis=1)
    block_numbers = jnp.arange(block_count, dtype=jnp.int32)
    attended = lax.map(jax.checkpoint(attend_block), (grouped[:, :, :D], keys_all, values_all, segment_row.reshape(block_count, BLK), mask_row, block_numbers))
    attended = low(low_back(attended.reshape(SEQLEN, D)))
    residual = row_input + low_back(exact_product(attended, params[4]))
    second_low = low(layer_norm(residual, params[5]))
    activated = low(activation(low_back(exact_product(second_low, params[6]))))
    return low(residual + exact_product(activated, params[7]))

def reference(layer_input, segment_ids, context_mask, first_gain, attention_in, kernel_weight, kernel_decay, attention_out, second_gain, expand_weight, reduce_weight, cotangent):
    weights = (first_gain, attention_in.astype(jnp.float32), kernel_weight, kernel_decay, attention_out.astype(jnp.float32), second_gain, expand_weight.astype(jnp.float32), reduce_weight.astype(jnp.float32))

    def forward(inputs, params):
        kernel_rows = lag_kernel(params[2], params[3])

        def one_row(pieces):
            return row_forward(pieces[0], pieces[1], pieces[2], kernel_rows, params)
        return lax.map(one_row, (inputs, segment_ids, context_mask))
    output, pullback = jax.vjp(forward, layer_input.astype(jnp.float32), weights)
    input_grad, weight_grads = pullback(cotangent.astype(jnp.float32))
    return (output.astype(jnp.bfloat16), input_grad, weight_grads[0], weight_grads[1], weight_grads[2], weight_grads[3], weight_grads[4], weight_grads[5], weight_grads[6], weight_grads[7])
```

```python
import functools
import heapq
import itertools
import math

import jax
import jax.numpy as jnp
from jax import lax
from jax.experimental import pallas as pl
from jax.experimental.pallas import tpu as pltpu
from jax.sharding import PartitionSpec as P


MESH=pl.DeviceIdType.MESH
BF=jnp.bfloat16

def sizes(nx, ns):
    ny = nx if ns % (2*nx)==0 else 1
    return {"x":nx,"y":ny,"z":ns//(2*ny)}

class Place:
    def __init__(s, n):
        s.n=n; q=lax.axis_index("seq")
        s.i=dict(x=lax.axis_index("grp"), y=lax.rem(lax.div(q,2),n["y"]), z=lax.div(q,2*n["y"])); s.c=lax.rem(q,2)
    def at(s, ax, k):
        return lax.rem(s.i[ax]+k, s.n[ax])
    def device(s, ax, k):
        j=dict(s.i); j[ax]=s.at(ax,k)
        return {"grp":j["x"],"seq":(j["z"]*s.n["y"]+j["y"])*2+s.c}
    def sibling(s):
        return {"seq":(s.i["z"]*s.n["y"]+s.i["y"])*2+1-s.c}
    def partners(s):
        return [s.device(ax,k) for ax in "xyz" for k in range(1,s.n[ax])]

def stage_shapes(n, order, rows, cw):
    left=dict(n); out=[]
    for ax in order:
        del left[ax]
        out.append(tuple(left[a] for a in "zy" if a in left)+(rows, cw*(left["x"] if "x" in left else 1)))
    return out

def piece_scratch(n, order, rows, cw):
    sh=stage_shapes(n,order,rows,cw)
    res=[]
    for ax,s in zip(order,sh):
        res.append(pltpu.VMEM((n[ax]-1,)+s,BF)); res.append(pltpu.VMEM(s,BF))
    most=max(n.values())-1
    res+= [pltpu.SemaphoreType.DMA((4,most)),pltpu.SemaphoreType.DMA((4,most))]
    return res

class Piece:
    def __init__(s, place, order, rows, cw, src, out, scratch):
        s.p,s.order,s.rows,s.cw,s.src,s.out=place,order,rows,cw,src,out
        s.recv=[scratch[0],scratch[2],scratch[4]]; s.sum=[scratch[1],scratch[3],scratch[5]]
        s.ss,s.rs=scratch[6],scratch[7]
        s.copies={}
    def view(s, stage, fixed):
        if stage==0:
            ref=s.src; lead=[fixed.get(a,slice(None)) for a in "zy"]; left=["z","y","x"]
        else:
            ref=s.sum[stage-1]; left=[a for a in "zyx" if a not in s.order[:stage]]
            lead=[fixed.get(a,slice(None)) for a in "zy" if a in left]
        cols=slice(None)
        if "x" in fixed and "x" in left: cols=pl.ds(pl.multiple_of(fixed["x"]*s.cw,128),s.cw)
        return ref, tuple(lead)+(slice(None),cols)
    def start(s, stage):
        if stage<3:
            ax=s.order[stage]
            for k in range(1,s.p.n[ax]):
                if stage==0: src=s.src(ax,s.p.at(ax,k))
                else:
                    ref,ix=s.view(stage,{ax:s.p.at(ax,k)}); src=ref.at[ix]
                cp=pltpu.make_async_remote_copy(src_ref=src,dst_ref=s.recv[stage].at[k-1],send_sem=s.ss.at[stage,k-1],recv_sem=s.rs.at[stage,k-1],device_id=s.p.device(ax,k),device_id_type=MESH)
                cp.start(); s.copies[stage,k]=cp
        else:
            for k in range(1,s.p.n["x"]):
                cp=pltpu.make_async_remote_copy(src_ref=s.sum[2],dst_ref=s.out.at[:,pl.ds(pl.multiple_of(s.p.i["x"]*s.cw,128),s.cw)],send_sem=s.ss.at[3,k-1],recv_sem=s.rs.at[3,k-1],device_id=s.p.device("x",k),device_id_type=MESH)
                cp.start(); s.copies[3,k]=cp
    def wait_send(s, stage):
        for (st,k),cp in s.copies.items():
            if st==stage: cp.wait_send()
    def finish(s, stage):
        for (st,k),cp in s.copies.items():
            if st==stage: cp.wait_recv()
        if stage==3: return
        ax=s.order[stage]; n=s.p.n
        left=[a for a in "zy" if a not in s.order[:stage+1]]
        R=s.recv[stage]; T=s.sum[stage]
        step=min(s.rows,32)
        for lead in itertools.product(*[range(n[a]) for a in left]):
            fixed=dict(zip(left,lead)); fixed[ax]=s.p.i[ax]
            if stage==0: own=s.src(None,None,fixed)
            else:
                ref,ix=s.view(stage,fixed); own=ref.at[ix]
            def body(r,_):
                rr=pl.ds(pl.multiple_of(r*step,16),step)
                v=own[rr,:].astype(jnp.float32)
                for k in range(n[ax]-1):
                    v=v+R[(k,)+lead+(rr,slice(None))].astype(jnp.float32)
                T[lead+(rr,slice(None))]=v.astype(BF)
                if stage==2:
                    s.out[rr,pl.ds(pl.multiple_of(s.p.i["x"]*s.cw,128),s.cw)]=v.astype(BF)
                return 0
            if s.rows==step: body(0,0)
            else: lax.fori_loop(0,s.rows//step,body,0)

def source(ref, place, rows0, rows, col0, cw):
    n=place.n
    def src(ax,j,fixed=None):
        fixed=dict(fixed or {})
        if ax: fixed[ax]=j
        lead=[fixed.get(a,slice(None)) for a in "zy"]
        if "x" in fixed: cols=pl.ds(pl.multiple_of(col0+fixed["x"]*cw,128),cw)
        else: cols=pl.ds(col0,cw*n["x"])
        return ref.at[tuple(lead)+(pl.ds(rows0,rows),cols)]
    return src

def barrier(place, extra=()):
    sem=pltpu.get_barrier_semaphore()
    ps=place.partners()+list(extra)
    for d in ps: pl.semaphore_signal(sem,inc=1,device_id=d,device_id_type=MESH)
    pl.semaphore_wait(sem,len(ps))

EPS=1e-5
BLK=512; CTX=128; HEADS=8; HD=128
F32=jnp.float32

def norm_rows(src, gain, dst, rows, step=64):
    def body(i,_):
        rr=pl.ds(pl.multiple_of(i*step,16),step)
        x=src[rr,:].astype(F32)
        x=x-jnp.mean(x,axis=-1,keepdims=True)
        v=jnp.mean(x*x,axis=-1,keepdims=True)
        dst[rr,:]=(x*lax.rsqrt(v+EPS)*gain).astype(BF)
        return 0
    lax.fori_loop(0,rows//step,body,0)

def rates(decay, length):
    return jnp.exp(decay)*(1.0/length)

def block_state(low, rate3, row0, rows, put):
    nst=rate3.shape[0]
    back=7.0-lax.broadcasted_iota(jnp.int32,(8,128),0).astype(F32)
    for lt in range(low.shape[1]//128):
        lanes=pl.ds(lt*128,128)
        r=[jnp.broadcast_to(rate3[n,lt:lt+1,:],(8,128)) for n in range(nst)]
        a8=[jnp.exp(-8.0*v) for v in r]
        def body(g,acc):
            u=low[pl.ds(pl.multiple_of(row0+g*16,16),16),lanes].astype(F32)
            lo,hi=u[:8],u[8:]
            acc=tuple(a*c+lo for a,c in zip(a8,acc))
            return tuple(a*c+hi for a,c in zip(a8,acc))
        acc=lax.fori_loop(0,rows//16,body,tuple(jnp.zeros((8,128),F32) for _ in range(nst)),unroll=2)
        for n in range(nst):
            put(n,lt,jnp.sum(acc[n]*jnp.exp(-back*r[n]),axis=0,keepdims=True))

def split_lanes(src, dst, rows):
    def body(g,_):
        for lt in range(src.shape[1]//128):
            v=src[pl.ds(pl.multiple_of(g*16,16),16),lt*128:(lt+1)*128].astype(F32)
            dst[pl.ds(g*16,16),lt,:]=v
        return 0
    lax.fori_loop(0,rows//16,body,0)

def join_lanes(src, dst, rows):
    def body(g,_):
        for lt in range(dst.shape[1]//128):
            dst[pl.ds(pl.multiple_of(g*16,16),16),lt*128:(lt+1)*128]=src[pl.ds(g*16,16),lt,:].astype(dst.dtype)
        return 0
    lax.fori_loop(0,rows//16,body,0)

class Scan:
    def __init__(s, ns, nst, s3, gather, spread, h3, sem, forward):
        s.ns,s.nst,s.s3,s.gather,s.spread,s.h3=ns,nst,s3,gather,spread,h3
        s.sem=sem; s.forward=forward; s.q=lax.axis_index("seq"); s.stride=ns//nst
        s.n=lax.div(s.q,s.stride); s.scans=lax.rem(s.q,s.stride)==0
    def to_scanner(s, n):
        return pltpu.make_async_remote_copy(src_ref=s.s3.at[n],dst_ref=s.gather.at[s.q],send_sem=s.sem[0].at[n],recv_sem=s.sem[1].at[s.q],device_id={"seq":n*s.stride},device_id_type=MESH)
    def from_block(s, b):
        return pltpu.make_async_remote_copy(src_ref=s.s3.at[0],dst_ref=s.gather.at[b],send_sem=s.sem[0].at[0],recv_sem=s.sem[1].at[b],device_id={"seq":b},device_id_type=MESH)
    def to_block(s, b):
        return pltpu.make_async_remote_copy(src_ref=s.spread.at[b],dst_ref=s.h3.at[s.n],send_sem=s.sem[2].at[b],recv_sem=s.sem[3].at[s.n],device_id={"seq":b},device_id_type=MESH)
    def from_scanner(s, n):
        return pltpu.make_async_remote_copy(src_ref=s.spread.at[0],dst_ref=s.h3.at[n],send_sem=s.sem[2].at[0],recv_sem=s.sem[3].at[n],device_id={"seq":n*s.stride},device_id_type=MESH)
    def each(s, count, fn, skip):
        def body(i,_):
            @pl.when(i!=skip)
            def _(): fn(i)
            return 0
        lax.fori_loop(0,count,body,0)
    def collect(s):
        mine=jnp.where(s.scans,s.n,s.nst)
        s.each(s.nst,lambda n:s.to_scanner(n).start(),mine)
    def scan(s, decay_block):
        mine=jnp.where(s.scans,s.n,s.nst)
        @pl.when(s.scans)
        def _():
            s.gather[s.q]=s.s3[s.n]
            s.each(s.ns,lambda b:s.from_block(b).wait_recv(),s.q)
            a=decay_block[s.n]
            def body(i,h):
                b=i if s.forward else s.ns-1-i
                s.spread[b]=h
                return a*h+s.gather[b]
            lax.fori_loop(0,s.ns,body,jnp.zeros((8,128),F32))
            s.each(s.ns,lambda b:s.to_block(b).start(),s.q)
            s.h3[s.n]=s.spread[s.q]
    def receive(s):
        mine=jnp.where(s.scans,s.n,s.nst)
        s.each(s.nst,lambda n:s.from_scanner(n).wait_recv(),mine)
    def drain(s):
        mine=jnp.where(s.scans,s.n,s.nst)
        s.each(s.nst,lambda n:s.to_scanner(n).wait_send(),mine)
        @pl.when(s.scans)
        def _(): s.each(s.ns,lambda b:s.to_block(b).wait_send(),s.q)

def scan_scratch(ns,nst):
    return [pltpu.VMEM((nst,8,128),F32),pltpu.VMEM((ns,8,128),F32),pltpu.VMEM((ns,8,128),F32),
      pltpu.SemaphoreType.DMA((nst,)),pltpu.SemaphoreType.DMA((ns,)),pltpu.SemaphoreType.DMA((ns,)),pltpu.SemaphoreType.DMA((nst,))]

def front_kernel(ns, length, x, cot, gain, decay3, weight3, w_hbm, low, tail_low, packed, ctx, pairs, h3, own3, cot_sib,
                 w, tail_x, rate3, dec3, u3, y3, s3, gather, spread, e0, e1, e2, e3, wsem, tsem, csem):
    q=lax.axis_index("seq"); c=lax.rem(q,2); g=lax.axis_index("grp")
    nst=decay3.shape[0]
    sem=pltpu.get_barrier_semaphore()
    def sig(i,_):
        @pl.when(i!=q)
        def _(): pl.semaphore_signal(sem,inc=1,device_id={"seq":i},device_id_type=MESH)
        return 0
    lax.fori_loop(0,ns,sig,0)
    wcp=pltpu.make_async_copy(w_hbm,w,wsem); wcp.start()
    pl.semaphore_wait(sem,ns-1)
    tail=pltpu.make_async_remote_copy(src_ref=x.at[pl.ds(BLK-CTX,CTX),:],dst_ref=tail_x,send_sem=tsem.at[0],recv_sem=tsem.at[1],device_id={"seq":jnp.minimum(q+1,ns-1)},device_id_type=MESH)
    @pl.when(q<ns-1)
    def _(): tail.start()
    cc=pltpu.make_async_remote_copy(src_ref=cot,dst_ref=cot_sib,send_sem=csem.at[0],recv_sem=csem.at[1],device_id={"seq":q+1-2*c},device_id_type=MESH)
    cc.start()
    rate3[...]=rates(decay3[...],length)
    dec3[...]=jnp.exp(-float(BLK)*rate3[...])
    norm_rows(x,gain[...],low,BLK)
    def put_own(n,lt,v): own3[n,lt:lt+1,:]=v
    block_state(low,rate3,0,BLK-CTX,put_own)
    @pl.when(q>0)
    def _(): tail.wait_recv()
    @pl.when(q==0)
    def _(): tail_x[...]=jnp.zeros_like(tail_x)
    norm_rows(tail_x,gain[...],tail_low,CTX)
    def put_tail(n,lt,v): s3[n,lt:lt+1,:]=v
    block_state(tail_low,rate3,0,CTX,put_tail)
    for n in range(nst):
        s3[n]=jnp.exp(-float(BLK-CTX)*rate3[n])*s3[n]+own3[n]
    ex=Scan(ns,nst,s3,gather,spread,h3,[e0,e1,e2,e3],True)
    ex.collect()
    wcp.wait()
    def mm(i,_):
        cols=pl.ds(pl.multiple_of(i*256,128),256)
        packed[:,cols]=jnp.dot(low[...],w[:,cols],preferred_element_type=F32).astype(BF)
        return 0
    tiles=packed.shape[1]//256
    lax.fori_loop(0,tiles//2,mm,0)
    ex.scan(dec3)
    split_lanes(tail_low,u3,CTX)
    lax.fori_loop(tiles//2,tiles,mm,0)
    ex.receive()
    a=[jnp.exp(-rate3[n]) for n in range(nst)]
    k=[weight3[n]*jnp.sqrt(rate3[n]) for n in range(nst)]
    def step(t,h):
        u=u3[t]
        h=tuple(p*v+u for p,v in zip(a,h))
        ys=[p*v for p,v in zip(k,h)]
        while len(ys)>1: ys=[ys[i]+ys[i+1] if i+1<len(ys) else ys[i] for i in range(0,len(ys),2)]
        y3[t]=ys[0]
        return h
    lax.fori_loop(0,CTX,step,tuple(h3[n] for n in range(nst)),unroll=2)
    join_lanes(y3,ctx,CTX)
    d=low.shape[1]
    def pm(i,_):
        cols=pl.ds(pl.multiple_of(i*256,128),256)
        pairs[:,cols]=jnp.dot(ctx[...],w[:,pl.ds(pl.multiple_of(d+i*256,128),256)],preferred_element_type=F32).astype(BF)
        return 0
    lax.fori_loop(0,pairs.shape[1]//256,pm,0)
    ex.drain()
    @pl.when(q<ns-1)
    def _(): tail.wait_send()
    cc.wait()

def front(ns, x, cot, gain, decay3, weight3, w):
    nst=decay3.shape[0]; d=x.shape[1]
    V=pl.BlockSpec(memory_space=pltpu.VMEM); A=pl.BlockSpec(memory_space=pl.ANY)
    S=lambda *s,t=BF: jax.ShapeDtypeStruct(s,t)
    return pl.pallas_call(functools.partial(front_kernel,ns,x.shape[0]*ns),
        out_shape=[S(BLK,d),S(CTX,d),S(BLK,3*d),S(CTX,d),S(CTX,2*d),S(nst,8,128,t=F32),S(nst,8,128,t=F32),S(BLK,d)],
        in_specs=[V,A,V,V,V,A],out_specs=[V]*7+[A],
        scratch_shapes=[pltpu.VMEM((d,3*d),BF),pltpu.VMEM((CTX,d),BF),pltpu.VMEM((nst,8,128),F32),pltpu.VMEM((nst,8,128),F32),
          pltpu.VMEM((CTX,8,128),F32),pltpu.VMEM((CTX,8,128),F32)]+scan_scratch(ns,nst)+[pltpu.SemaphoreType.DMA,pltpu.SemaphoreType.DMA((2,)),pltpu.SemaphoreType.DMA((2,))],
        compiler_params=pltpu.CompilerParams(collective_id=0,has_side_effects=True,vmem_limit_bytes=60*2**20),
        name="front")(x,cot,gain,decay3,weight3,w)

NEG=-1e30
NT=(((1,),(1,)),((),()))
TN=(((0,),(0,)),((),()))
NN=(((1,),(0,)),((),()))
def mm(a,b,dims=NN): return lax.dot_general(a,b,dims,preferred_element_type=F32)

def attention_kernel(q,k,v,ck,cv,seg,vis,x,wo,gain,probs,attended,residual,low2,bias):
    h=pl.program_id(0)
    @pl.when(h==0)
    def _():
        row=jnp.broadcast_to(seg[...].astype(F32),(128,BLK))
        col=jnp.transpose(row)
        def body(i,_):
            rr=pl.ds(pl.multiple_of(i*128,128),128)
            qi=i*128+lax.broadcasted_iota(jnp.int32,(128,BLK),0)
            kj=lax.broadcasted_iota(jnp.int32,(128,BLK),1)
            return 0
        for i in range(BLK//128):
            ci=col[i*128:(i+1)*128]
            for j in range(BLK//128):
                if j>i:
                    bias[i*128:(i+1)*128,j*128:(j+1)*128]=jnp.full((128,128),NEG,F32); continue
                ok=ci==row[:,j*128:(j+1)*128]
                if i==j: ok=ok&(lax.broadcasted_iota(jnp.int32,(128,128),0)>=lax.broadcasted_iota(jnp.int32,(128,128),1))
                bias[i*128:(i+1)*128,j*128:(j+1)*128]=jnp.where(ok,0.0,NEG)
        bias[:,BLK:]=jnp.broadcast_to(vis[...],(BLK,CTX))
    scale=1.0/math.sqrt(HD)
    half=BLK//2
    for r in range(2):
        rows=slice(r*half,(r+1)*half); n=(r+1)*half
        s1=mm(q[rows,:],k[:n,:],NT)*scale+bias[rows,:n]
        s2=mm(q[rows,:],ck[...],NT)*scale+bias[rows,BLK:]
        top=jnp.maximum(jnp.max(s1,axis=-1,keepdims=True),jnp.max(s2,axis=-1,keepdims=True))
        e1=jnp.exp(s1-top); e2=jnp.exp(s2-top)
        inv=1.0/(jnp.sum(e1,axis=-1,keepdims=True)+jnp.sum(e2,axis=-1,keepdims=True))
        p1=(e1*inv).astype(BF); p2=(e2*inv).astype(BF)
        probs[0,rows,:n]=p1; probs[0,rows,BLK:]=p2
        if n<BLK: probs[0,rows,n:BLK]=jnp.zeros((half,BLK-n),BF)
        o=mm(p1,v[:n,:])+mm(p2,cv[...])
        attended[rows,pl.ds(pl.multiple_of(h*HD,HD),HD)]=o.astype(BF)
    @pl.when(h==HEADS-1)
    def _():
        def body(i,_):
            rr=pl.ds(pl.multiple_of(i*128,128),128)
            res=x[rr,:].astype(F32)+mm(attended[rr,:],wo[...])
            residual[rr,:]=res
            m=res-jnp.mean(res,axis=-1,keepdims=True)
            var=jnp.mean(m*m,axis=-1,keepdims=True)
            low2[rr,:]=(m*lax.rsqrt(var+EPS)*gain[...]).astype(BF)
            return 0
        lax.fori_loop(0,BLK//128,body,0)

def attention(packed,pairs,seg,vis,x,wo,gain):
    d=x.shape[1]
    S=lambda *s,t=BF: jax.ShapeDtypeStruct(s,t)
    full=lambda a: pl.BlockSpec(a.shape,lambda h:(0,)*a.ndim)
    return pl.pallas_call(attention_kernel,grid=(HEADS,),
      in_specs=[pl.BlockSpec((BLK,HD),lambda h:(0,h)),pl.BlockSpec((BLK,HD),lambda h:(0,HEADS+h)),pl.BlockSpec((BLK,HD),lambda h:(0,2*HEADS+h)),
        pl.BlockSpec((CTX,HD),lambda h:(0,h)),pl.BlockSpec((CTX,HD),lambda h:(0,HEADS+h)),full(seg),full(vis),full(x),full(wo),full(gain)],
      out_specs=[pl.BlockSpec((1,BLK,BLK+CTX),lambda h:(h,0,0)),pl.BlockSpec((BLK,d),lambda h:(0,0)),pl.BlockSpec((BLK,d),lambda h:(0,0)),pl.BlockSpec((BLK,d),lambda h:(0,0))],
      out_shape=[S(HEADS,BLK,BLK+CTX),S(BLK,d),S(BLK,d,t=F32),S(BLK,d)],
      scratch_shapes=[pltpu.VMEM((BLK,BLK+CTX),F32)],
      compiler_params=pltpu.CompilerParams(vmem_limit_bytes=48*2**20),
      cost_estimate=pl.CostEstimate(flops=4*10**9,bytes_accessed=2*10**7,transcendentals=3*10**6),
      name="attention")(packed,packed,packed,pairs,pairs,seg,vis,x,wo,gain)

G0=math.sqrt(2/math.pi); G1=0.044715
def gelu_pair(h):
    h2=h*h
    th=jnp.tanh(h*(G0+G0*G1*h2))
    p=0.5*(1.0+th)
    return h*p, p+h*(0.5*(1.0-th*th))*(G0+3*G0*G1*h2)

def ffn_kernel(n, nff, xo, coto, cots, w1, w2, A, B, out_own, out_rec, dx_own, dx_rec,
               x2, x2t, cot2, w1s, w2s, act, dexp, sbuf, wsem1, wsem2, xsem, osem, dsem):
    place=Place(n); c=place.c; sib=place.sibling()
    tiles=w1s.shape[1]//256; d=xo.shape[1]; rf=A.shape[2]
    sem=pltpu.get_barrier_semaphore()
    pl.semaphore_signal(sem,inc=1,device_id=sib,device_id_type=MESH)
    if rf%128==0:
        per=256//rf if rf<256 else 1; wd=min(rf,256)
        def cp(i):
            j=i*wd
            src=lax.div(j,rf)*(2*rf)+c*rf+lax.rem(j,rf)
            return (pltpu.make_async_copy(w1.at[:,pl.ds(pl.multiple_of(src,128),wd)],w1s.at[:,pl.ds(pl.multiple_of(j,128),wd)],wsem1.at[i]),
                    pltpu.make_async_copy(w2.at[pl.ds(pl.multiple_of(src,16),wd),:],w2s.at[pl.ds(pl.multiple_of(j,16),wd),:],wsem2.at[i]))
    else:
        per=1; wd=256
        def cp(i):
            j=i*wd
            return (pltpu.make_async_copy(w1.at[:,pl.ds(pl.multiple_of(j,128),wd)],w1s.at[:,pl.ds(pl.multiple_of(j,128),wd)],wsem1.at[i]),
                    pltpu.make_async_copy(w2.at[pl.ds(pl.multiple_of(j,16),wd),:],w2s.at[pl.ds(pl.multiple_of(j,16),wd),:],wsem2.at[i]))
    count=tiles*256//wd
    def go(i,_):
        a,b=cp(i); a.start(); b.start(); return 0
    lax.fori_loop(0,count,go,0)
    pl.semaphore_wait(sem,1)
    xs=pltpu.make_async_remote_copy(src_ref=xo,dst_ref=x2.at[pl.ds(BLK,BLK),:],send_sem=xsem.at[0],recv_sem=xsem.at[1],device_id=sib,device_id_type=MESH)
    xs.start()
    x2[0:BLK,:]=xo[...]
    cot2[0:BLK,:]=coto[...]; cot2[BLK:,:]=cots[...]
    for i in range(d//256): x2t[i*256:(i+1)*256,0:BLK]=jnp.transpose(xo[:,i*256:(i+1)*256])
    xs.wait()
    for i in range(d//256): x2t[i*256:(i+1)*256,BLK:]=jnp.transpose(x2[BLK:,i*256:(i+1)*256])
    def tile(t,_):
        for j in range(per):
            a,b=cp(t*per+j); a.wait(); b.wait()
        cols=pl.ds(pl.multiple_of(t*256,256),256)
        def part(r,_):
            rr=pl.ds(pl.multiple_of(r*256,256),256)
            h=mm(x2[rr,:],w1s[:,cols]); u=mm(cot2[rr,:],w2s[cols,:],NT)
            a,g=gelu_pair(h)
            act[rr,cols]=a.astype(BF); dexp[rr,cols]=(u*g).astype(BF)
            return 0
        lax.fori_loop(0,2*BLK//256,part,0)
        def ga(k,_):
            kc=pl.ds(pl.multiple_of(k*256,256),256)
            v=mm(act[:,cols],cot2[:,kc],TN).astype(BF)
            for j in range(max(1,256//rf)):
                zy=lax.div(t*256,rf)+j; w=min(rf,256)
                A[lax.div(zy,n["y"]),lax.rem(zy,n["y"]),pl.ds(pl.multiple_of(lax.rem(t*256,rf),16),w) if rf>256 else slice(None),kc]=v[j*w:(j+1)*w]
            return 0
        lax.fori_loop(0,d//256,ga,0)
        rb=B.shape[2]; nzy=n["z"]*n["y"]; group=max(1,256//rb)
        def gb(k,_):
            rr=pl.ds(pl.multiple_of(k*group*rb,16),group*rb)
            v=mm(x2t[rr,:],dexp[:,cols]).astype(BF)
            for j in range(group):
                zy=k*group+j
                B[lax.div(zy,n["y"]),lax.rem(zy,n["y"]),:,cols]=v[j*rb:(j+1)*rb]
            return 0
        lax.fori_loop(0,nzy//group,gb,0)
        return 0
    lax.fori_loop(0,tiles,tile,0)
    def dx(r,dst):
        rr=pl.ds(pl.multiple_of(r*256,256),256)
        return mm(dexp[rr,:],w1s[...],NT)
    def ou(r):
        rr=pl.ds(pl.multiple_of(r*256,256),256)
        return mm(act[rr,:],w2s[...])
    for r in range(2):
        sbuf[0,r*256:(r+1)*256,:]=dx(2+r,None).astype(BF)
    dc=pltpu.make_async_remote_copy(src_ref=sbuf.at[0],dst_ref=dx_rec,send_sem=dsem.at[0],recv_sem=dsem.at[1],device_id=sib,device_id_type=MESH); dc.start()
    for r in range(2):
        sbuf[1,r*256:(r+1)*256,:]=ou(2+r).astype(BF)
    oc=pltpu.make_async_remote_copy(src_ref=sbuf.at[1],dst_ref=out_rec,send_sem=osem.at[0],recv_sem=osem.at[1],device_id=sib,device_id_type=MESH); oc.start()
    for r in range(2):
        dx_own[r*256:(r+1)*256,:]=dx(r,None)
        out_own[r*256:(r+1)*256,:]=ou(r)
    dc.wait(); oc.wait()

def ffn(n, xo, coto, cots, w1, w2):
    d=xo.shape[1]; ff=w1.shape[1]; zy=n["z"]*n["y"]; own=ff//2; rf=own//zy; rb=d//zy
    V=pl.BlockSpec(memory_space=pltpu.VMEM); Y=pl.BlockSpec(memory_space=pl.ANY)
    S=lambda *s,t=BF: jax.ShapeDtypeStruct(s,t)
    if rf%128:
        c=lax.rem(lax.axis_index("seq"),2)
        w1=lax.dynamic_index_in_dim(w1.reshape(d,zy,2,rf),c,2,keepdims=False).reshape(d,own)
        w2=lax.dynamic_index_in_dim(w2.reshape(zy,2,rf,d),c,1,keepdims=False).reshape(own,d)
    D=pltpu.SemaphoreType.DMA; nc=own//min(max(rf,128),256) if rf%128==0 else own//256
    return pl.pallas_call(functools.partial(ffn_kernel,n,ff),
      out_shape=[S(n["z"],n["y"],rf,d),S(n["z"],n["y"],rb,own),S(BLK,d,t=F32),S(BLK,d),S(BLK,d,t=F32),S(BLK,d)],
      in_specs=[V,V,V,Y,Y],out_specs=[V]*6,
      scratch_shapes=[pltpu.VMEM((2*BLK,d),BF),pltpu.VMEM((d,2*BLK),BF),pltpu.VMEM((2*BLK,d),BF),pltpu.VMEM((d,own),BF),pltpu.VMEM((own,d),BF),
        pltpu.VMEM((2*BLK,own),BF),pltpu.VMEM((2*BLK,own),BF),pltpu.VMEM((2,BLK,d),BF),D((nc,)),D((nc,)),D((2,)),D((2,)),D((2,))],
      compiler_params=pltpu.CompilerParams(collective_id=1,has_side_effects=True,vmem_limit_bytes=60*2**20),
      cost_estimate=pl.CostEstimate(flops=26*10**9,bytes_accessed=3*10**7,transcendentals=2*10**6),
      name="ffn")(xo,coto,cots,w1,w2)


def norm_back(v, gain, dy):
    x=v-jnp.mean(v,axis=-1,keepdims=True)
    s=lax.rsqrt(jnp.mean(x*x,axis=-1,keepdims=True)+EPS)
    nrm=x*s
    dn=dy*gain
    dv=(dn-jnp.mean(dn,axis=-1,keepdims=True)-nrm*jnp.mean(dn*nrm,axis=-1,keepdims=True))*s
    return dv, dy*nrm
def fold(v):
    return jnp.sum(v.reshape(v.shape[0]//8,8,v.shape[1]),axis=0)

def middle_kernel(dx_own,dx_rec,residual,gain,cot,attended,wo,out_own,out_rec, out,rgrad,branch,ggrad,agrad):
    ggrad[...]=jnp.zeros_like(ggrad)
    def body(i,_):
        rr=pl.ds(pl.multiple_of(i*64,64),64)
        dy=dx_own[rr,:]+dx_rec[rr,:].astype(F32)
        dv,g=norm_back(residual[rr,:],gain[...],dy)
        r=cot[rr,:].astype(F32)+dv
        rgrad[rr,:]=r; b=r.astype(BF); branch[rr,:]=b
        ggrad[...]+=fold(g)
        out[rr,:]=(residual[rr,:]+out_own[rr,:]+out_rec[rr,:].astype(F32)).astype(BF)
        return 0
    lax.fori_loop(0,BLK//64,body,0)
    def ag(i,_):
        rr=pl.ds(pl.multiple_of(i*256,256),256)
        agrad[rr,:]=mm(branch[rr,:],wo[...],NT).astype(BF)
        return 0
    lax.fori_loop(0,BLK//256,ag,0)

def call(kernel, ins, outs, scratch=(), name=None, flops=10**9, **kw):
    V=pl.BlockSpec(memory_space=pltpu.VMEM)
    return pl.pallas_call(kernel,out_shape=outs,in_specs=[V]*len(ins),out_specs=[V]*len(outs),scratch_shapes=list(scratch),
      compiler_params=pltpu.CompilerParams(vmem_limit_bytes=60*2**20,**kw),cost_estimate=pl.CostEstimate(flops=flops,bytes_accessed=2*10**7,transcendentals=0),name=name)(*ins)
def S(*s,t=BF): return jax.ShapeDtypeStruct(s,t)

def attention_back_kernel(q,k,v,ck,cv,p,o,do,dq,dk,dv,dck,dcv):
    scale=1.0/math.sqrt(HD)
    half=BLK//2
    for r in range(2):
        rows=slice(r*half,(r+1)*half); n=(r+1)*half
        g=do[rows,:]
        dot=jnp.sum(g.astype(F32)*o[rows,:].astype(F32),axis=-1,keepdims=True)
        p1=p[0,rows,:n]; p2=p[0,rows,BLK:]
        s1=(p1.astype(F32)*(mm(g,v[:n,:],NT)-dot)).astype(BF)
        s2=(p2.astype(F32)*(mm(g,cv[...],NT)-dot)).astype(BF)
        dq[rows,:]=((mm(s1,k[:n,:])+mm(s2,ck[...]))*scale).astype(BF)
        qr=q[rows,:]
        a1=mm(s1,qr,TN)*scale; a2=mm(s2,qr,TN)*scale; b1=mm(p1,g,TN); b2=mm(p2,g,TN)
        if r==0: first=(a1,a2,b1,b2)
    dk[0:half,:]=(first[0]+a1[:half]).astype(BF); dk[half:,:]=a1[half:].astype(BF)
    dv[0:half,:]=(first[2]+b1[:half]).astype(BF); dv[half:,:]=b1[half:].astype(BF)
    dck[...]=(first[1]+a2).astype(BF); dcv[...]=(first[3]+b2).astype(BF)

def attention_back(packed,pairs,probs,attended,agrad):
    d=attended.shape[1]
    col=lambda n,o: pl.BlockSpec((n,HD),lambda h,o=o:(0,o+h))
    return pl.pallas_call(attention_back_kernel,grid=(HEADS,),
      in_specs=[col(BLK,0),col(BLK,HEADS),col(BLK,2*HEADS),col(CTX,0),col(CTX,HEADS),pl.BlockSpec((1,BLK,BLK+CTX),lambda h:(h,0,0)),col(BLK,0),col(BLK,0)],
      out_specs=[col(BLK,0)]*3+[col(CTX,0)]*2,out_shape=[S(BLK,d)]*3+[S(CTX,d)]*2,
      compiler_params=pltpu.CompilerParams(vmem_limit_bytes=48*2**20),
      cost_estimate=pl.CostEstimate(flops=4*10**9,bytes_accessed=2*10**7,transcendentals=0),
      name="attention_back")(packed,packed,packed,pairs,pairs,probs,attended,agrad)

def grads_kernel(low,ctx,dq,dk,dv,dck,dcv,attended,branch,w, C,G,dn, lt,ct,at):
    d=low.shape[1]; nz,ny=C.shape[0],C.shape[1]; rb=C.shape[3]; per=256//rb
    def tr(i,_):
        cols=pl.ds(pl.multiple_of(i*256,256),256)
        lt[cols,:]=jnp.transpose(low[:,cols]); ct[cols,:]=jnp.transpose(ctx[:,cols]); at[cols,:]=jnp.transpose(attended[:,cols])
        return 0
    lax.fori_loop(0,d//256,tr,0)
    def put(i,v,col0):
        for j in range(per):
            b=i*per+j; zy=lax.div(b,2)
            C[lax.div(zy,ny),lax.rem(zy,ny),lax.rem(b,2),:,col0:col0+d]=v[j*rb:(j+1)*rb].astype(BF)
    def rows(i,_):
        rr=pl.ds(pl.multiple_of(i*256,256),256)
        put(i,mm(lt[rr,:],dq[...]),0)
        put(i,mm(lt[rr,:],dk[...])+mm(ct[rr,:],dck[...]),d)
        put(i,mm(lt[rr,:],dv[...])+mm(ct[rr,:],dcv[...]),2*d)
        put(i,mm(at[rr,:],branch[...]),3*d)
        return 0
    lax.fori_loop(0,d//256,rows,0)
    G[...]=(mm(dck[...],w[:,d:2*d],NT)+mm(dcv[...],w[:,2*d:],NT)).astype(BF)
    def back(i,_):
        rr=pl.ds(pl.multiple_of(i*256,256),256)
        dn[rr,:]=mm(dq[rr,:],w[:,:d],NT)+mm(dk[rr,:],w[:,d:2*d],NT)+mm(dv[rr,:],w[:,2*d:],NT)
        return 0
    lax.fori_loop(0,BLK//256,back,0)

def conv_back_kernel(ns,length,G,tail_low,low,decay3,weight3,h3, sig,kwg,kdg, rate3,dec3,u3,g3,y3,hb,sp3,d0,d1,tailb,tail_in,s3,gather,spread,e0,e1,e2,e3,tsem):
    q=lax.axis_index("seq"); nst=decay3.shape[0]
    sem=pltpu.get_barrier_semaphore()
    def sg(i,_):
        @pl.when(i!=q)
        def _(): pl.semaphore_signal(sem,inc=1,device_id={"seq":i},device_id_type=MESH)
        return 0
    lax.fori_loop(0,ns,sg,0)
    rate3[...]=rates(decay3[...],length)
    dec3[...]=jnp.exp(-float(BLK)*rate3[...])
    split_lanes(G,g3,CTX)
    a=[jnp.exp(-rate3[n]) for n in range(nst)]
    k=[weight3[n]*jnp.sqrt(rate3[n]) for n in range(nst)]
    def back(i,g):
        t=CTX-1-i
        v=g3[t]
        g=tuple(p*x+v for p,x in zip(a,g))
        ys=[p*x for p,x in zip(k,g)]
        while len(ys)>1: ys=[ys[i]+ys[i+1] for i in range(0,len(ys),2)]
        y3[t]=ys[0]
        return g
    g=lax.fori_loop(0,CTX,back,tuple(jnp.zeros((8,128),F32) for _ in range(nst)),unroll=2)
    for n in range(nst): s3[n]=g[n]
    pl.semaphore_wait(sem,ns-1)
    ex=Scan(ns,nst,s3,gather,spread,hb,[e0,e1,e2,e3],False)
    ex.collect()
    split_lanes(tail_low,u3,CTX)
    up=lax.broadcasted_iota(jnp.int32,(8,128),0).astype(F32)
    for lt in range(low.shape[1]//128):
        lanes=pl.ds(lt*128,128)
        for part in range(0,nst,8):
            r=[jnp.broadcast_to(rate3[n,lt:lt+1,:],(8,128)) for n in range(part,part+8)]
            a8=[jnp.exp(-8.0*v) for v in r]
            def body(i,cr):
                acc,der=cr
                u=low[pl.ds(pl.multiple_of(i*16,16),16),lanes].astype(F32)
                for w in (u[:8],u[8:]):
                    der=tuple(p*(x+y) for p,x,y in zip(a8,der,acc))
                    acc=tuple(p*y+w for p,y in zip(a8,acc))
                return acc,der
            z=tuple(jnp.zeros((8,128),F32) for _ in range(8))
            acc,der=lax.fori_loop(0,(BLK-CTX)//16,body,(z,z))
            for i,n in enumerate(range(part,part+8)):
                j=7.0-up
                sp3[n,lt:lt+1,:]=jnp.sum(jnp.exp(-j*r[i])*(8.0*der[i]+j*acc[i]),axis=0,keepdims=True)
    ex.scan(dec3)
    for part in range(0,nst,4):
        z=tuple(jnp.zeros((8,128),F32) for _ in range(4))
        def fwd(t,cr):
            h,hp,s0,s1=cr
            u=u3[t]; gg=g3[t]; aa=a[part:part+4]
            hp=tuple(p*(x+y) for p,x,y in zip(aa,hp,h))
            h=tuple(p*x+u for p,x in zip(aa,h))
            s0=tuple(x+gg*y for x,y in zip(s0,h)); s1=tuple(x+gg*y for x,y in zip(s1,hp))
            return h,hp,s0,s1
        h,hp,s0,s1=lax.fori_loop(0,CTX,fwd,(tuple(h3[n] for n in range(part,part+4)),z,z,z),unroll=2)
        for i,n in enumerate(range(part,part+4)):
            d0[n]=s0[i]; d1[n]=s1[i]
            m=float(BLK-CTX)
            am=jnp.exp(-m*rate3[n])
            sp3[n]=a[n]*(am*hp[i]+m*am*h[i]+sp3[n])
    ex.receive()
    for n in range(nst):
        r=rate3[n]; D1=d1[n]+hb[n]*sp3[n]; sq=jnp.sqrt(r)
        kwg[n]=sq*d0[n]
        kdg[n]=weight3[n]*sq*(0.5*d0[n]-r*D1)
    for lt in range(low.shape[1]//128):
        lanes=slice(lt*128,(lt+1)*128)
        r=[jnp.broadcast_to(rate3[n,lt:lt+1,:],(8,128)) for n in range(nst)]
        a8=[jnp.exp(-8.0*x) for x in r]
        v=tuple(jnp.broadcast_to((weight3[n,lt:lt+1,:]*jnp.sqrt(rate3[n,lt:lt+1,:]))*hb[n,lt:lt+1,:],(8,128))*jnp.exp(-(8.0-up)*r[n]) for n in range(nst))
        def total(v):
            ys=list(v)
            while len(ys)>1: ys=[ys[i]+ys[i+1] for i in range(0,len(ys),2)]
            return ys[0]
        def own(i,v):
            b=total(v); v=tuple(p*x for p,x in zip(a8,v))
            t=total(v); v=tuple(p*x for p,x in zip(a8,v))
            sig[pl.ds(pl.multiple_of(BLK-CTX-16-i*16,16),16),lanes]=jnp.concatenate([t,b],axis=0).astype(BF)
            return v
        v=lax.fori_loop(0,(BLK-CTX)//16,own,v)
        def tl(i,v):
            b=total(v); v=tuple(p*x for p,x in zip(a8,v))
            t=total(v); v=tuple(p*x for p,x in zip(a8,v))
            row=pl.multiple_of(CTX-16-i*16,16)
            tailb[pl.ds(row,16),lanes]=(jnp.concatenate([t,b],axis=0)+y3[pl.ds(row,16),lt,:]).astype(BF)
            return v
        lax.fori_loop(0,CTX//16,tl,v)
    back_copy=pltpu.make_async_remote_copy(src_ref=tailb,dst_ref=tail_in,send_sem=tsem.at[0],recv_sem=tsem.at[1],device_id={"seq":jnp.maximum(q-1,0)},device_id_type=MESH)
    @pl.when(q>0)
    def _(): back_copy.start()
    @pl.when(q==ns-1)
    def _(): tail_in[...]=jnp.zeros_like(tail_in)
    @pl.when(q<ns-1)
    def _(): back_copy.wait_recv()
    sig[BLK-CTX:,:]=tail_in[...]
    @pl.when(q>0)
    def _(): back_copy.wait_send()
    ex.drain()

def conv_back(ns,G,tail_low,low,decay3,weight3,h3):
    nst=decay3.shape[0]; d=low.shape[1]; M=pltpu.VMEM; st=(nst,8,128)
    return call(functools.partial(conv_back_kernel,ns,BLK*ns),[G,tail_low,low,decay3,weight3,h3],[S(BLK,d),S(*st,t=F32),S(*st,t=F32)],
      [M(st,F32),M(st,F32),M((CTX,8,128),F32),M((CTX,8,128),F32),M((CTX,8,128),F32),M(st,F32),M(st,F32),M(st,F32),M(st,F32),M((CTX,d),BF),M((CTX,d),BF)]+scan_scratch(ns,nst)+[pltpu.SemaphoreType.DMA((2,))],
      name="conv_back",collective_id=2,has_side_effects=True)

def last_kernel(x,gain,dn,sig,rgrad, igrad,ggrad):
    ggrad[...]=jnp.zeros_like(ggrad)
    def body(i,_):
        rr=pl.ds(pl.multiple_of(i*64,64),64)
        dv,g=norm_back(x[rr,:].astype(F32),gain[...],dn[rr,:]+sig[rr,:].astype(F32))
        igrad[rr,:]=rgrad[rr,:]+dv
        ggrad[...]+=fold(g)
        return 0
    lax.fori_loop(0,BLK//64,body,0)

def rs_kernel(n, plan, sched, A,B,Cf, OA,OB,OC, C,crec,csem,*scr):
    place=Place(n); c=place.c
    barrier(place,[place.sibling()])
    cps=[]
    nz,ny=n["z"],n["y"]
    for z in range(nz):
        cp=pltpu.make_async_remote_copy(src_ref=Cf.at[z,:,1-c],dst_ref=crec.at[z],send_sem=csem.at[0,z],recv_sem=csem.at[1,z],device_id=place.sibling(),device_id_type=MESH)
        cp.start(); cps.append(cp)
    T=[A,B,C]; O=[OA,OB,OC]
    pieces=[Piece(place,o,r,cw,source(T[t],place,r0,r,c0,cw),O[t].at[pl.ds(r0,r),pl.ds(c0,cw*n["x"])],scr[8*i:8*i+8]) for i,(t,r0,r,c0,cw,o) in enumerate(plan)]
    for i,p in enumerate(plan):
        if p[0]<2: pieces[i].start(0)
    rb=C.shape[2]
    for z in range(nz):
        cps[z].wait_recv()
        def add(y,_):
            for h in range(rb//16):
                rr=slice(h*16,h*16+16)
                C[z,y,rr,:]=(Cf[z,y,c,rr,:].astype(F32)+crec[z,y,rr,:].astype(F32)).astype(BF)
            return 0
        lax.fori_loop(0,ny,add,0)
    for i,p in enumerate(plan):
        if p[0]==2: pieces[i].start(0)
    for i,s in sched:
        pieces[i].finish(s)
        if s<3: pieces[i].start(s+1)
    for p in pieces:
        for s in range(4): p.wait_send(s)
    for cp in cps: cp.wait_send()

def simulate(n, plan, ready):
    free=dict(x=0.,y=0.,z=0.); res={}
    ev=[(ready[p[0]],i,0) for i,p in enumerate(plan)]; heapq.heapify(ev)
    while ev:
        t,i,s=heapq.heappop(ev)
        (_,r0,r,c0,cw,order)=plan[i]
        if s<3:
            ax=order[s]; shape=stage_shapes(n,order,r,cw)[s]; vol=math.prod(shape)*4*(n[ax]**2/4 if n[ax]>2 else 1)
        else: ax="x"; vol=r*cw*4
        st=max(t,free[ax]); en=st+vol/91e3; free[ax]=en
        res[i,s]=en+1.5
        if s<3: heapq.heappush(ev,(en+2.5,i,s+1))
    return sorted(res,key=lambda k:(res[k],k[1])), max(free.values())

def make_plan(n, ra, rb, rc, d, own, tot):
    nx=n["x"]; plan=[]
    def cut(t,rows,cols,orders):
        parts=len(orders)
        while rows//parts<16: parts//=2
        r=rows//parts
        for i in range(parts): plan.append((t,i*r,r,0,cols//nx,orders[i]))
    cut(0,ra,d,["xyz"]*4); cut(1,rb,own,["yxz"]*4); cut(2,rc,tot,["zxy","xyz","yxz","zxy"])
    return plan

def reduce_all(n, A,B,Cf):
    nz,ny=n["z"],n["y"]; ra,d=A.shape[2:]; rb,own=B.shape[2:]; rc,tot=Cf.shape[3:]
    plan=make_plan(n,ra,rb,rc,d,own,tot)
    sched,_=simulate(n,plan,[0.,0.,12.])
    scr=[pltpu.VMEM((nz,ny,rc,tot),BF),pltpu.VMEM((nz,ny,rc,tot),BF),pltpu.SemaphoreType.DMA((2,nz))]
    for (t,r0,r,c0,cw,o) in plan: scr+=piece_scratch(n,o,r,cw)
    return call(functools.partial(rs_kernel,n,plan,sched),[A,B,Cf],[S(ra,d),S(rb,own),S(rc,tot)],scr,name="reduce_all",collective_id=3,has_side_effects=True)

def local(layer_input,segment_ids,context_mask,first_gain,attention_in,kernel_weight,kernel_decay,attention_out,second_gain,expand_weight,reduce_weight,cotangent):
    ns=lax.axis_size("seq"); nx=lax.axis_size("grp"); nst=kernel_decay.shape[1]; n=sizes(nx,ns)
    q=lax.axis_index("seq"); c=lax.rem(q,2)
    x=layer_input[0]; cot=cotangent[0]; d=x.shape[1]; ff=expand_weight.shape[1]
    decay3=kernel_decay.T.reshape(nst,8,128); weight3=kernel_weight.T.reshape(nst,8,128)
    low,tail_low,packed,ctx,pairs,h3,own3,cot_sib=front(ns,x,cot,first_gain[None],decay3,weight3,attention_in)
    vis=jnp.where((context_mask[0]==1)&(q>0),0.0,NEG).astype(F32)
    probs,attended,residual,low2=attention(packed,pairs,segment_ids,vis,x,attention_out,second_gain[None])
    A,B,oo,orr,do,dr=ffn(n,low2,cot,cot_sib,expand_weight,reduce_weight)
    out,rgrad,branch,g2,agrad=call(middle_kernel,[do,dr,residual,second_gain[None],cot,attended,attention_out,oo,orr],[S(BLK,d),S(BLK,d,t=F32),S(BLK,d),S(8,d,t=F32),S(BLK,d)],name="middle")
    dq,dk,dv,dck,dcv=attention_back(packed,pairs,probs,attended,agrad)
    nz,ny=n["z"],n["y"]
    Cf,G,dn=call(grads_kernel,[low,ctx,dq,dk,dv,dck,dcv,attended,branch,attention_in],[S(nz,ny,2,d//ns,4*d),S(CTX,d),S(BLK,d,t=F32)],
       [pltpu.VMEM((d,BLK),BF),pltpu.VMEM((d,CTX),BF),pltpu.VMEM((d,BLK),BF)],name="grads")
    sig,kwg,kdg=conv_back(ns,G,tail_low,low,decay3,weight3,h3)
    igrad,g1=call(last_kernel,[x,first_gain[None],dn,sig,rgrad],[S(BLK,d,t=F32),S(8,d,t=F32)],name="last")
    OA,OB,OC=reduce_all(n,A,B,Cf)
    small=jnp.concatenate([kwg.reshape(nst,d),kdg.reshape(nst,d),jnp.sum(g1,0,keepdims=True),jnp.sum(g2,0,keepdims=True)],0)
    small=lax.psum(small,("grp","seq"))
    rows=d//ns
    mine=lax.dynamic_slice_in_dim(small,q*rows,rows,1)
    rd=d//ns; own=ff//2; rf=own//(nz*ny)
    keep=lax.dynamic_slice_in_dim(OB,c*rd,rd,0); send=lax.dynamic_slice_in_dim(OB,(1-c)*rd,rd,0)
    other=lax.ppermute(send,"seq",[(i,i^1) for i in range(ns)])
    keep=keep.reshape(rd,nz*ny,rf); other=other.reshape(rd,nz*ny,rf)
    eg=jnp.stack([jnp.where(c==0,keep,other),jnp.where(c==0,other,keep)],2).reshape(rd,ff).astype(F32)
    OC=OC.astype(F32)
    return (out[None],igrad[None],mine[2*nst],OC[:,:3*d],mine[:nst].T,mine[nst:2*nst].T,OC[:,3*d:],mine[2*nst+1],eg,OA.astype(F32))

def solution(mesh):
    ins=(P("grp","seq",None),P("grp","seq"),P("grp","seq",None))+(P(),)*8+(P("grp","seq",None),)
    outs=(P("grp","seq",None),)*2+(P("seq"),)+(P("seq",None),)*4+(P("seq"),)+(P("seq",None),)*2
    return jax.shard_map(local,mesh=mesh,in_specs=ins,out_specs=outs,check_vma=False)
```

```python
import functools
import heapq
import itertools
import math

import jax
import jax.numpy as jnp
from jax import lax
from jax.experimental import pallas as pl
from jax.experimental.pallas import tpu as pltpu
from jax.sharding import PartitionSpec as P

MESH=pl.DeviceIdType.MESH
BF=jnp.bfloat16

def sizes(nx, ns):
    ny = nx if ns % (2*nx)==0 else 1
    return {"x":nx,"y":ny,"z":ns//(2*ny)}

class Place:
    def __init__(s, n):
        s.n=n; q=lax.axis_index("seq")
        s.i=dict(x=lax.axis_index("grp"), y=lax.rem(lax.div(q,2),n["y"]), z=lax.div(q,2*n["y"])); s.c=lax.rem(q,2)
    def at(s, ax, k):
        return lax.rem(s.i[ax]+k, s.n[ax])
    def device(s, ax, k):
        j=dict(s.i); j[ax]=s.at(ax,k)
        return {"grp":j["x"],"seq":(j["z"]*s.n["y"]+j["y"])*2+s.c}
    def sibling(s):
        return {"seq":(s.i["z"]*s.n["y"]+s.i["y"])*2+1-s.c}
    def partners(s):
        return [s.device(ax,k) for ax in "xyz" for k in range(1,s.n[ax])]

def stage_shapes(n, order, rows, cw):
    left=dict(n); out=[]
    for ax in order:
        del left[ax]
        out.append(tuple(left[a] for a in "zy" if a in left)+(rows, cw*(left["x"] if "x" in left else 1)))
    return out


EPS=1e-5
BLK=512; CTX=128; HEADS=8; HD=128
F32=jnp.float32

def norm_rows(src, gain, dst, rows, step=64):
    def body(i,_):
        rr=pl.ds(pl.multiple_of(i*step,16),step)
        x=src[rr,:].astype(F32)
        x=x-jnp.mean(x,axis=-1,keepdims=True)
        v=jnp.mean(x*x,axis=-1,keepdims=True)
        dst[rr,:]=(x*lax.rsqrt(v+EPS)*gain).astype(BF)
        return 0
    lax.fori_loop(0,rows//step,body,0)

def rates(decay, length):
    return jnp.exp(decay)*(1.0/length)

def block_state(low, rate3, row0, rows, put):
    nst=rate3.shape[0]
    back=7.0-lax.broadcasted_iota(jnp.int32,(8,128),0).astype(F32)
    for lt in range(low.shape[1]//128):
        lanes=pl.ds(lt*128,128)
        r=[jnp.broadcast_to(rate3[n,lt:lt+1,:],(8,128)) for n in range(nst)]
        a8=[jnp.exp(-8.0*v) for v in r]
        def body(g,acc):
            u=low[pl.ds(pl.multiple_of(row0+g*16,16),16),lanes].astype(F32)
            lo,hi=u[:8],u[8:]
            acc=tuple(a*c+lo for a,c in zip(a8,acc))
            return tuple(a*c+hi for a,c in zip(a8,acc))
        acc=lax.fori_loop(0,rows//16,body,tuple(jnp.zeros((8,128),F32) for _ in range(nst)),unroll=2)
        for n in range(nst):
            put(n,lt,jnp.sum(acc[n]*jnp.exp(-back*r[n]),axis=0,keepdims=True))

def split_lanes(src, dst, rows):
    def body(g,_):
        for lt in range(src.shape[1]//128):
            v=src[pl.ds(pl.multiple_of(g*16,16),16),lt*128:(lt+1)*128].astype(F32)
            dst[pl.ds(g*16,16),lt,:]=v
        return 0
    lax.fori_loop(0,rows//16,body,0)

def join_lanes(src, dst, rows):
    def body(g,_):
        for lt in range(dst.shape[1]//128):
            dst[pl.ds(pl.multiple_of(g*16,16),16),lt*128:(lt+1)*128]=src[pl.ds(g*16,16),lt,:].astype(dst.dtype)
        return 0
    lax.fori_loop(0,rows//16,body,0)

class Scan:
    def __init__(s, ns, nst, s3, gather, spread, h3, sem, forward):
        s.ns,s.nst,s.s3,s.gather,s.spread,s.h3=ns,nst,s3,gather,spread,h3
        s.sem=sem; s.forward=forward; s.q=lax.axis_index("seq"); s.stride=ns//nst
        s.n=lax.div(s.q,s.stride); s.scans=lax.rem(s.q,s.stride)==0
    def to_scanner(s, n):
        return pltpu.make_async_remote_copy(src_ref=s.s3.at[n],dst_ref=s.gather.at[s.q],send_sem=s.sem[0].at[n],recv_sem=s.sem[1].at[s.q],device_id={"seq":n*s.stride},device_id_type=MESH)
    def from_block(s, b):
        return pltpu.make_async_remote_copy(src_ref=s.s3.at[0],dst_ref=s.gather.at[b],send_sem=s.sem[0].at[0],recv_sem=s.sem[1].at[b],device_id={"seq":b},device_id_type=MESH)
    def to_block(s, b):
        return pltpu.make_async_remote_copy(src_ref=s.spread.at[b],dst_ref=s.h3.at[s.n],send_sem=s.sem[2].at[b],recv_sem=s.sem[3].at[s.n],device_id={"seq":b},device_id_type=MESH)
    def from_scanner(s, n):
        return pltpu.make_async_remote_copy(src_ref=s.spread.at[0],dst_ref=s.h3.at[n],send_sem=s.sem[2].at[0],recv_sem=s.sem[3].at[n],device_id={"seq":n*s.stride},device_id_type=MESH)
    def each(s, count, fn, skip):
        def body(i,_):
            @pl.when(i!=skip)
            def _(): fn(i)
            return 0
        lax.fori_loop(0,count,body,0)
    def collect(s):
        mine=jnp.where(s.scans,s.n,s.nst)
        s.each(s.nst,lambda n:s.to_scanner(n).start(),mine)
    def scan(s, decay_block):
        mine=jnp.where(s.scans,s.n,s.nst)
        @pl.when(s.scans)
        def _():
            s.gather[s.q]=s.s3[s.n]
            s.each(s.ns,lambda b:s.from_block(b).wait_recv(),s.q)
            a=decay_block[s.n]
            def body(i,h):
                b=i if s.forward else s.ns-1-i
                s.spread[b]=h
                return a*h+s.gather[b]
            lax.fori_loop(0,s.ns,body,jnp.zeros((8,128),F32))
            s.each(s.ns,lambda b:s.to_block(b).start(),s.q)
            s.h3[s.n]=s.spread[s.q]
    def receive(s):
        mine=jnp.where(s.scans,s.n,s.nst)
        s.each(s.nst,lambda n:s.from_scanner(n).wait_recv(),mine)
    def drain(s):
        mine=jnp.where(s.scans,s.n,s.nst)
        s.each(s.nst,lambda n:s.to_scanner(n).wait_send(),mine)
        @pl.when(s.scans)
        def _(): s.each(s.ns,lambda b:s.to_block(b).wait_send(),s.q)

def scan_scratch(ns,nst):
    return [pltpu.VMEM((nst,8,128),F32),pltpu.VMEM((ns,8,128),F32),pltpu.VMEM((ns,8,128),F32),
      pltpu.SemaphoreType.DMA((nst,)),pltpu.SemaphoreType.DMA((ns,)),pltpu.SemaphoreType.DMA((ns,)),pltpu.SemaphoreType.DMA((nst,))]

def front_kernel(ns, length, x, cot, gain, decay3, weight3, w_hbm, low, tail_low, packed, ctx, pairs, h3, own3, cot_sib,
                 w, tail_x, rate3, dec3, u3, y3, s3, gather, spread, e0, e1, e2, e3, wsem, tsem, csem):
    q=lax.axis_index("seq"); c=lax.rem(q,2); g=lax.axis_index("grp")
    nst=decay3.shape[0]
    sem=pltpu.get_barrier_semaphore()
    def sig(i,_):
        @pl.when(i!=q)
        def _(): pl.semaphore_signal(sem,inc=1,device_id={"seq":i},device_id_type=MESH)
        return 0
    lax.fori_loop(0,ns,sig,0)
    wcp=pltpu.make_async_copy(w_hbm,w,wsem); wcp.start()
    pl.semaphore_wait(sem,ns-1)
    tail=pltpu.make_async_remote_copy(src_ref=x.at[pl.ds(BLK-CTX,CTX),:],dst_ref=tail_x,send_sem=tsem.at[0],recv_sem=tsem.at[1],device_id={"seq":jnp.minimum(q+1,ns-1)},device_id_type=MESH)
    @pl.when(q<ns-1)
    def _(): tail.start()
    cc=pltpu.make_async_remote_copy(src_ref=cot,dst_ref=cot_sib,send_sem=csem.at[0],recv_sem=csem.at[1],device_id={"seq":q+1-2*c},device_id_type=MESH)
    cc.start()
    rate3[...]=rates(decay3[...],length)
    dec3[...]=jnp.exp(-float(BLK)*rate3[...])
    norm_rows(x,gain[...],low,BLK)
    def put_own(n,lt,v): own3[n,lt:lt+1,:]=v
    block_state(low,rate3,0,BLK-CTX,put_own)
    @pl.when(q>0)
    def _(): tail.wait_recv()
    @pl.when(q==0)
    def _(): tail_x[...]=jnp.zeros_like(tail_x)
    norm_rows(tail_x,gain[...],tail_low,CTX)
    def put_tail(n,lt,v): s3[n,lt:lt+1,:]=v
    block_state(tail_low,rate3,0,CTX,put_tail)
    for n in range(nst):
        s3[n]=jnp.exp(-float(BLK-CTX)*rate3[n])*s3[n]+own3[n]
    ex=Scan(ns,nst,s3,gather,spread,h3,[e0,e1,e2,e3],True)
    ex.collect()
    wcp.wait()
    def mm(i,_):
        cols=pl.ds(pl.multiple_of(i*256,128),256)
        packed[:,cols]=jnp.dot(low[...],w[:,cols],preferred_element_type=F32).astype(BF)
        return 0
    tiles=packed.shape[1]//256
    lax.fori_loop(0,tiles//2,mm,0)
    ex.scan(dec3)
    split_lanes(tail_low,u3,CTX)
    lax.fori_loop(tiles//2,tiles,mm,0)
    ex.receive()
    a=[jnp.exp(-rate3[n]) for n in range(nst)]
    k=[weight3[n]*jnp.sqrt(rate3[n]) for n in range(nst)]
    def step(t,h):
        u=u3[t]
        h=tuple(p*v+u for p,v in zip(a,h))
        ys=[p*v for p,v in zip(k,h)]
        while len(ys)>1: ys=[ys[i]+ys[i+1] if i+1<len(ys) else ys[i] for i in range(0,len(ys),2)]
        y3[t]=ys[0]
        return h
    lax.fori_loop(0,CTX,step,tuple(h3[n] for n in range(nst)),unroll=2)
    join_lanes(y3,ctx,CTX)
    d=low.shape[1]
    def pm(i,_):
        cols=pl.ds(pl.multiple_of(i*256,128),256)
        pairs[:,cols]=jnp.dot(ctx[...],w[:,pl.ds(pl.multiple_of(d+i*256,128),256)],preferred_element_type=F32).astype(BF)
        return 0
    lax.fori_loop(0,pairs.shape[1]//256,pm,0)
    ex.drain()
    @pl.when(q<ns-1)
    def _(): tail.wait_send()
    cc.wait()

def front(ns, x, cot, gain, decay3, weight3, w):
    nst=decay3.shape[0]; d=x.shape[1]
    V=pl.BlockSpec(memory_space=pltpu.VMEM); A=pl.BlockSpec(memory_space=pl.ANY)
    S=lambda *s,t=BF: jax.ShapeDtypeStruct(s,t)
    return pl.pallas_call(functools.partial(front_kernel,ns,x.shape[0]*ns),
        out_shape=[S(BLK,d),S(CTX,d),S(BLK,3*d),S(CTX,d),S(CTX,2*d),S(nst,8,128,t=F32),S(nst,8,128,t=F32),S(BLK,d)],
        in_specs=[V,A,V,V,V,A],out_specs=[V]*7+[A],
        scratch_shapes=[pltpu.VMEM((d,3*d),BF),pltpu.VMEM((CTX,d),BF),pltpu.VMEM((nst,8,128),F32),pltpu.VMEM((nst,8,128),F32),
          pltpu.VMEM((CTX,8,128),F32),pltpu.VMEM((CTX,8,128),F32)]+scan_scratch(ns,nst)+[pltpu.SemaphoreType.DMA,pltpu.SemaphoreType.DMA((2,)),pltpu.SemaphoreType.DMA((2,))],
        compiler_params=pltpu.CompilerParams(collective_id=0,has_side_effects=True,vmem_limit_bytes=60*2**20),
        name="front")(x,cot,gain,decay3,weight3,w)

NEG=-1e30
NT=(((1,),(1,)),((),()))
TN=(((0,),(0,)),((),()))
NN=(((1,),(0,)),((),()))
def mm(a,b,dims=NN): return lax.dot_general(a,b,dims,preferred_element_type=F32)

def attention_kernel(q,k,v,ck,cv,seg,vis,x,wo,gain,probs,attended,residual,low2,bias):
    h=pl.program_id(0)
    @pl.when(h==0)
    def _():
        row=jnp.broadcast_to(seg[...].astype(F32),(128,BLK))
        col=jnp.transpose(row)
        def body(i,_):
            rr=pl.ds(pl.multiple_of(i*128,128),128)
            qi=i*128+lax.broadcasted_iota(jnp.int32,(128,BLK),0)
            kj=lax.broadcasted_iota(jnp.int32,(128,BLK),1)
            return 0
        for i in range(BLK//128):
            ci=col[i*128:(i+1)*128]
            for j in range(BLK//128):
                if j>i:
                    bias[i*128:(i+1)*128,j*128:(j+1)*128]=jnp.full((128,128),NEG,F32); continue
                ok=ci==row[:,j*128:(j+1)*128]
                if i==j: ok=ok&(lax.broadcasted_iota(jnp.int32,(128,128),0)>=lax.broadcasted_iota(jnp.int32,(128,128),1))
                bias[i*128:(i+1)*128,j*128:(j+1)*128]=jnp.where(ok,0.0,NEG)
        bias[:,BLK:]=jnp.broadcast_to(vis[...],(BLK,CTX))
    scale=1.0/math.sqrt(HD)
    half=BLK//2
    for r in range(2):
        rows=slice(r*half,(r+1)*half); n=(r+1)*half
        s1=mm(q[rows,:],k[:n,:],NT)*scale+bias[rows,:n]
        s2=mm(q[rows,:],ck[...],NT)*scale+bias[rows,BLK:]
        top=jnp.maximum(jnp.max(s1,axis=-1,keepdims=True),jnp.max(s2,axis=-1,keepdims=True))
        e1=jnp.exp(s1-top); e2=jnp.exp(s2-top)
        inv=1.0/(jnp.sum(e1,axis=-1,keepdims=True)+jnp.sum(e2,axis=-1,keepdims=True))
        p1=(e1*inv).astype(BF); p2=(e2*inv).astype(BF)
        probs[0,rows,:n]=p1; probs[0,rows,BLK:]=p2
        if n<BLK: probs[0,rows,n:BLK]=jnp.zeros((half,BLK-n),BF)
        o=mm(p1,v[:n,:])+mm(p2,cv[...])
        attended[rows,pl.ds(pl.multiple_of(h*HD,HD),HD)]=o.astype(BF)
    @pl.when(h==HEADS-1)
    def _():
        def body(i,_):
            rr=pl.ds(pl.multiple_of(i*128,128),128)
            res=x[rr,:].astype(F32)+mm(attended[rr,:],wo[...])
            residual[rr,:]=res
            m=res-jnp.mean(res,axis=-1,keepdims=True)
            var=jnp.mean(m*m,axis=-1,keepdims=True)
            low2[rr,:]=(m*lax.rsqrt(var+EPS)*gain[...]).astype(BF)
            return 0
        lax.fori_loop(0,BLK//128,body,0)

def attention(packed,pairs,seg,vis,x,wo,gain):
    d=x.shape[1]
    S=lambda *s,t=BF: jax.ShapeDtypeStruct(s,t)
    full=lambda a: pl.BlockSpec(a.shape,lambda h:(0,)*a.ndim)
    return pl.pallas_call(attention_kernel,grid=(HEADS,),
      in_specs=[pl.BlockSpec((BLK,HD),lambda h:(0,h)),pl.BlockSpec((BLK,HD),lambda h:(0,HEADS+h)),pl.BlockSpec((BLK,HD),lambda h:(0,2*HEADS+h)),
        pl.BlockSpec((CTX,HD),lambda h:(0,h)),pl.BlockSpec((CTX,HD),lambda h:(0,HEADS+h)),full(seg),full(vis),full(x),full(wo),full(gain)],
      out_specs=[pl.BlockSpec((1,BLK,BLK+CTX),lambda h:(h,0,0)),pl.BlockSpec((BLK,d),lambda h:(0,0)),pl.BlockSpec((BLK,d),lambda h:(0,0)),pl.BlockSpec((BLK,d),lambda h:(0,0))],
      out_shape=[S(HEADS,BLK,BLK+CTX),S(BLK,d),S(BLK,d,t=F32),S(BLK,d)],
      scratch_shapes=[pltpu.VMEM((BLK,BLK+CTX),F32)],
      compiler_params=pltpu.CompilerParams(vmem_limit_bytes=48*2**20),
      cost_estimate=pl.CostEstimate(flops=4*10**9,bytes_accessed=2*10**7,transcendentals=3*10**6),
      name="attention")(packed,packed,packed,pairs,pairs,seg,vis,x,wo,gain)

G0=math.sqrt(2/math.pi); G1=0.044715
def gelu_pair(h):
    h2=h*h
    th=jnp.tanh(h*(G0+G0*G1*h2))
    p=0.5*(1.0+th)
    return h*p, p+h*(0.5*(1.0-th*th))*(G0+3*G0*G1*h2)


def norm_back(v, gain, dy):
    x=v-jnp.mean(v,axis=-1,keepdims=True)
    s=lax.rsqrt(jnp.mean(x*x,axis=-1,keepdims=True)+EPS)
    nrm=x*s
    dn=dy*gain
    dv=(dn-jnp.mean(dn,axis=-1,keepdims=True)-nrm*jnp.mean(dn*nrm,axis=-1,keepdims=True))*s
    return dv, dy*nrm
def fold(v):
    return jnp.sum(v.reshape(v.shape[0]//8,8,v.shape[1]),axis=0)


def S(*s,t=BF): return jax.ShapeDtypeStruct(s,t)


class Lane:
    def __init__(s, place, order, rows, cw, src, out, scratch):
        s.p,s.order,s.rows,s.cw,s.src,s.out=place,order,rows,cw,src,out
        s.recv=scratch[:3]; s.ss,s.rs=scratch[3],scratch[4]
        s.begun=[]
        s.mine=pl.ds(pl.multiple_of(place.i["x"]*cw,128),cw)
    def held(s, stage, fixed):
        if stage==0: return s.src(fixed)
        left=[a for a in "zyx" if a not in s.order[:stage]]
        cols=slice(None)
        if "x" in fixed and "x" in left: cols=pl.ds(pl.multiple_of(fixed["x"]*s.cw,128),s.cw)
        return s.recv[stage-1].at[(0,)+tuple(fixed.get(a,slice(None)) for a in "zy" if a in left)+(slice(None),cols)]
    def copy(s, stage, k):
        ax="x" if stage==3 else s.order[stage]
        if stage==3: src=s.out.at[:,s.mine]; dst=s.out.at[:,s.mine]
        else: src=s.held(stage,{ax:s.p.at(ax,k)}); dst=s.recv[stage].at[k-1]
        return pltpu.make_async_remote_copy(src_ref=src,dst_ref=dst,send_sem=s.ss.at[stage,k-1],recv_sem=s.rs.at[stage,k-1],device_id=s.p.device(ax,k),device_id_type=MESH)
    def start(s, stage):
        for k in range(1,s.p.n["x" if stage==3 else s.order[stage]]):
            s.copy(stage,k).start(); s.begun.append((stage,k))
    def drain(s):
        for stage,k in s.begun: s.copy(stage,k).wait_send()
    def finish(s, stage):
        for st,k in s.begun:
            if st==stage: s.copy(st,k).wait_recv()
        if stage==3: return
        ax=s.order[stage]; n=s.p.n
        left=[a for a in "zy" if a not in s.order[:stage+1]]
        R=s.recv[stage]; step=min(s.rows,32)
        for lead in itertools.product(*[range(n[a]) for a in left]):
            fixed=dict(zip(left,lead)); fixed[ax]=s.p.i[ax]
            own=s.held(stage,fixed)
            def body(r,_):
                rr=pl.ds(pl.multiple_of(r*step,16),step)
                v=own[rr,:].astype(F32)
                for k in range(n[ax]-1): v=v+R[(k,)+lead+(rr,slice(None))].astype(F32)
                if stage==2: s.out[rr,s.mine]=v.astype(BF)
                else: R[(0,)+lead+(rr,slice(None))]=v.astype(BF)
                return 0
            if s.rows==step: body(0,0)
            else: lax.fori_loop(0,s.rows//step,body,0)

def lane_scratch(n, order, rows, cw):
    most=max(n.values())-1
    return [pltpu.VMEM((n[ax]-1,)+sh,BF) for ax,sh in zip(order,stage_shapes(n,order,rows,cw))]+[pltpu.SemaphoreType.DMA((4,most)),pltpu.SemaphoreType.DMA((4,most))]

def cut(ref, place, row0, rows, col0, cw):
    def src(fixed):
        cols=pl.ds(pl.multiple_of(col0+fixed["x"]*cw,128),cw) if "x" in fixed else pl.ds(col0,cw*place.n["x"])
        return ref.at[tuple(fixed.get(a,slice(None)) for a in "zy")+(pl.ds(row0,rows),cols)]
    return src

class Agenda:
    def __init__(s): s.items=[]; s.count=0
    def add(s, when, fn):
        heapq.heappush(s.items,(when,s.count,fn)); s.count+=1
    def run(s, now):
        while s.items and s.items[0][0]<=now: heapq.heappop(s.items)[2]()

def plan_of(n, rf, rb, rc, d, own, orders):
    nx=n["x"]; J=max(1,rf//128); plan=[]; o=iter(orders)
    parts=4 if rf//4>=16 else rf//16
    for i in range(4):
        if i<parts: plan.append(("A",0,i*(rf//parts),rf//parts,0,d//nx,next(o)))
        else: next(o)
    for t in range(4): plan.append(("B",0,0,rb,t*512,512//nx,next(o)))
    for k in range(4): plan.append(("C",k,0,rc,0,d//nx,next(o)))
    plan.append(("S",0,0,rc,0,128,next(o)))
    return plan
ORDERS=["xyz"]*4+["yxz"]*4+["xyz","yxz","xyz","yxz"]+["xyz"]
RELEASE=dict(A=[13.,13.,24.,24.],B=[7.,13.,18.,24.],C=[43.,60.,62.,64.],S=[95.])

def forecast(n, plan):
    free=dict(x=0.,y=0.,z=0.); res={}; seen={}; ev=[]
    for i,p in enumerate(plan):
        j=seen.get(p[0],0); seen[p[0]]=j+1
        heapq.heappush(ev,(RELEASE[p[0]][j],i,0))
    while ev:
        t,i,s=heapq.heappop(ev)
        _,_,r0,r,c0,cw,order=plan[i]
        if s<3:
            ax=order[s]; vol=math.prod(stage_shapes(n,order,r,cw)[s])*4*(n[ax]**2/4 if n[ax]>2 else 1)
        else: ax="x"; vol=r*cw*4
        st=max(t,free[ax]); free[ax]=st+vol/91e3
        res[i,s]=free[ax]+2.0
        if s<3: heapq.heappush(ev,(res[i,s]+0.5,i,s+1))
    return res

def tree(ys):
    ys=list(ys)
    while len(ys)>1: ys=[ys[i]+ys[i+1] if i+1<len(ys) else ys[i] for i in range(0,len(ys),2)]
    return ys[0]

def main_kernel(n, ns, length, plan, packed_w, *refs):
    (low2,cot,cots,w1,w2,residual,gain2,attended,wo,packed,pairs,probs,low,tail_low,ctx,w_in,x,gain1,decay3,weight3,h3,
     out,igrad,OA,OBk,OBr,OC,OS,
     x2,cot2,A,B,Cf,crec,dx_rec,out_rec,OBf,small,small_rec,tailb,tail_in,
     wsem1,wsem2,lsem,xsem,dsem,osem,csem,bsem,tsem,psem,outsem,s3,gather,spread,hb,e0,e1,e2,e3)=refs[:60]
    scr=refs[60:]
    place=Place(n); c=place.c; sib=place.sibling(); q=lax.axis_index("seq"); g=lax.axis_index("grp")
    d=x2.shape[1]; nz,ny=n["z"],n["y"]; nzy=nz*ny; rf=A.shape[2]; rb=B.shape[2]; own=B.shape[3]; rc=crec.shape[3]
    nst=decay3.shape[0]; J=max(1,rf//128); rj=rf//J
    sem=pltpu.get_barrier_semaphore()
    def sg(i,_):
        @pl.when(i!=q)
        def _(): pl.semaphore_signal(sem,inc=1,device_id={"seq":i},device_id_type=MESH)
        return 0
    lax.fori_loop(0,ns,sg,0)
    for k in range(1,n["x"]): pl.semaphore_signal(sem,inc=1,device_id=place.device("x",k),device_id_type=MESH)
    agenda=Agenda(); when=forecast(n,plan)
    outs={"A":OA,"B":OBf,"C":OC,"S":OS}; srcs={"A":lambda k:A,"B":lambda k:B,"C":lambda k:crec.at[k],"S":lambda k:small_rec}
    lanes=[]
    for i,(t,k,r0,r,c0,cw,o) in enumerate(plan):
        oc=(k*d if t=="C" else c0)
        lanes.append(Lane(place,o,r,cw,cut(srcs[t](k),place,r0,r,c0,cw),outs[t].at[pl.ds(r0,r),pl.ds(oc,cw*n["x"])],scr[5*i:5*i+5]))
    index={}
    for i,p in enumerate(plan): index.setdefault(p[0],[]).append(i)
    bcopies=[]
    def bcopy(c0,w):
        h=rb//2; cs=pl.ds(c0,w)
        return pltpu.make_async_remote_copy(src_ref=OBf.at[pl.ds(pl.multiple_of((1-c)*h,16),h),cs],dst_ref=OBr.at[:,cs],send_sem=bsem.at[0,c0//512],recv_sem=bsem.at[1,c0//512],device_id=sib,device_id_type=MESH)
    def chain(i,s):
        def fn():
            lanes[i].finish(s)
            if s<3:
                lanes[i].start(s+1); agenda.add(when[i,s+1],chain(i,s+1))
            elif plan[i][0]=="B":
                c0,w=plan[i][4],plan[i][5]*n["x"]; cs=pl.ds(c0,w); h=rb//2
                bcopy(c0,w).start(); bcopies.append((c0,w))
                OBk[:,cs]=OBf[pl.ds(pl.multiple_of(c*h,16),h),cs]
        return fn
    def launch(i):
        lanes[i].start(0); agenda.add(when[i,0],chain(i,0))

    def forward_part(w1s,w2s,act,dexp):
        tiles=own//512; wd=rj if rj%128==0 else 512; per=512//wd
        def wcopy(b):
            if packed_w: s1=s2=b*wd
            else: s1=s2=lax.rem(b,nzy)*(2*rf)+c*rf+lax.div(b,nzy)*rj
            return (pltpu.make_async_copy(w1.at[:,pl.ds(pl.multiple_of(s1,128),wd)],w1s.at[:,pl.ds(pl.multiple_of(b*wd,128),wd)],wsem1.at[b]),
                    pltpu.make_async_copy(w2.at[pl.ds(pl.multiple_of(s2,16),wd),:],w2s.at[pl.ds(pl.multiple_of(b*wd,16),wd),:],wsem2.at[b]))
        cc=[pltpu.make_async_copy(cot,cot2.at[pl.ds(0,BLK),:],lsem.at[0]),pltpu.make_async_copy(cots,cot2.at[pl.ds(BLK,BLK),:],lsem.at[1]),pltpu.make_async_copy(low2,x2.at[pl.ds(0,BLK),:],lsem.at[2])]
        for v in cc: v.start()
        def go(b,_):
            u,v=wcopy(b); v.start(); u.start(); return 0
        lax.fori_loop(0,own//wd,go,0)
        pl.semaphore_wait(sem,ns-1+n["x"]-1)
        xs=pltpu.make_async_remote_copy(src_ref=low2,dst_ref=x2.at[pl.ds(BLK,BLK),:],send_sem=xsem.at[0],recv_sem=xsem.at[1],device_id=sib,device_id_type=MESH)
        xs.start()
        for v in cc: v.wait()
        for t in range(tiles):
            for b in range(t*per,(t+1)*per): wcopy(b)[1].wait()
            cs=slice(t*512,(t+1)*512)
            u=mm(cot2[...],w2s[cs,:],NT)
            for b in range(t*per,(t+1)*per): wcopy(b)[0].wait()
            if t==0: xs.wait()
            h=mm(x2[...],w1s[:,cs])
            a,gp=gelu_pair(h)
            act[:,cs]=a.astype(BF); dexp[:,cs]=(u*gp).astype(BF)
            v=mm(x2[...],dexp[:,cs],TN).astype(BF)
            for b in range(nzy): B[b//ny,b%ny,:,cs]=v[b*rb:(b+1)*rb]
            launch(index["B"][t])
            agenda.run(7.+5.5*t)
            v=mm(act[:,cs],cot2[...],TN).astype(BF)
            for b in range(512//rj):
                e=t*(512//rj)+b; j,zy=e//nzy,e%nzy
                A[zy//ny,zy%ny,j*rj:(j+1)*rj,:]=v[b*rj:(b+1)*rj]
            ready=((t+1)*512//rj)//nzy*rj
            for i in index["A"]:
                if t*512//rj//nzy*rj<plan[i][2]+plan[i][3]<=ready: launch(i)
            agenda.run(8.5+5.5*t)
        cot2[0:BLK,:]=mm(dexp[BLK:,:],w1s[...],NT).astype(BF)
        dc=pltpu.make_async_remote_copy(src_ref=cot2.at[pl.ds(0,BLK),:],dst_ref=dx_rec,send_sem=dsem.at[0],recv_sem=dsem.at[1],device_id=sib,device_id_type=MESH); dc.start()
        agenda.run(27.)
        cot2[BLK:,:]=mm(act[BLK:,:],w2s[...]).astype(BF)
        oc=pltpu.make_async_remote_copy(src_ref=cot2.at[pl.ds(BLK,BLK),:],dst_ref=out_rec,send_sem=osem.at[0],recv_sem=osem.at[1],device_id=sib,device_id_type=MESH); oc.start()
        agenda.run(29.5)
        x2[0:BLK,:]=mm(dexp[0:BLK,:],w1s[...],NT).astype(BF)
        agenda.run(32.)
        x2[BLK:,:]=mm(act[0:BLK,:],w2s[...]).astype(BF)
        agenda.run(34.5)
        dc.wait(); oc.wait()
    pl.run_scoped(forward_part,pltpu.VMEM((d,own),BF),pltpu.VMEM((own,d),BF),pltpu.VMEM((2*BLK,own),BF),pltpu.VMEM((2*BLK,own),BF))

    def ccopy(k):
        return pltpu.make_async_remote_copy(src_ref=Cf.at[k%2,:,:,1-c],dst_ref=crec.at[k],send_sem=csem.at[0,k],recv_sem=csem.at[1,k],device_id=sib,device_id_type=MESH)
    def send_half(k, part, slot):
        if k>=2: ccopy(k-2).wait_send()
        for r in range(2):
            v=part(slice(r*d//2,(r+1)*d//2)).astype(BF)
            for b in range(nzy):
                e=r*nzy+b
                Cf[slot,e//2//ny,e//2%ny,e%2]=v[b*rc:(b+1)*rc]
        ccopy(k).start()
    def join_half(k, slot):
        ccopy(k).wait_recv()
        def add(z,_):
            for y in range(ny):
                for h in range(rc//16):
                    rr=slice(h*16,h*16+16)
                    crec[k,z,y,rr,:]=(crec[k,z,y,rr,:].astype(F32)+Cf[slot,z,y,c,rr,:].astype(F32)).astype(BF)
            return 0
        lax.fori_loop(0,nz,add,0)
        launch(index["C"][k])

    def rest(res,dq,dk,dv,dck,dcv,lowv,ctxv,ggrad2):
        loads=[pltpu.make_async_copy(residual,res,lsem.at[0]),pltpu.make_async_copy(low,lowv,lsem.at[1]),pltpu.make_async_copy(ctx,ctxv,lsem.at[2])]
        for v in loads: v.start()
        def attention_part(attv,wov,pk,pr,pbuf,branch,agrad):
            more=[pltpu.make_async_copy(attended,attv,lsem.at[3]),pltpu.make_async_copy(wo,wov,lsem.at[4]),pltpu.make_async_copy(packed,pk,lsem.at[5]),pltpu.make_async_copy(pairs,pr,lsem.at[6])]
            for v in more: v.start()
            def pload(h): return pltpu.make_async_copy(probs.at[h],pbuf.at[lax.rem(h,2)],psem.at[lax.rem(h,2)])
            pload(0).start()
            for v in loads: v.wait()
            ggrad2[...]=jnp.zeros_like(ggrad2)
            for part in range(4):
                def body(i,_):
                    rr=pl.ds(pl.multiple_of(part*128+i*64,64),64)
                    dy=x2[rr,:].astype(F32)+dx_rec[rr,:].astype(F32)
                    dvv,gg=norm_back(res[rr,:],gain2[...],dy)
                    stage[rr,:]=(res[rr,:]+x2[pl.ds(pl.multiple_of(BLK+part*128+i*64,64),64),:].astype(F32)+out_rec[rr,:].astype(F32)).astype(BF)
                    r=cot_own[rr,:].astype(F32)+dvv
                    res[rr,:]=r; branch[rr,:]=r.astype(BF)
                    ggrad2[...]+=fold(gg)
                    return 0
                lax.fori_loop(0,2,body,0)
                agenda.run(36.5+1.2*part)
            oc=pltpu.make_async_copy(stage,out,outsem.at[0]); oc.start()
            for v in more: v.wait()
            send_half(0,lambda r: mm(attv[:,r],branch[...],TN),0)
            agenda.add(45.,lambda: join_half(0,0))
            agenda.run(42.)
            agrad[...]=mm(branch[...],wov[...],NT).astype(BF)
            agenda.run(44.)
            scale=1.0/math.sqrt(HD); half=BLK//2
            def head(h,_):
                @pl.when(h<HEADS-1)
                def _(): pload(h+1).start()
                pload(h).wait()
                slot=lax.rem(h,2)
                ql=pl.ds(pl.multiple_of(h*HD,128),HD); kl=pl.ds(pl.multiple_of(d+h*HD,128),HD); vl=pl.ds(pl.multiple_of(2*d+h*HD,128),HD)
                for r in range(2):
                    rows=slice(r*half,(r+1)*half); m=(r+1)*half
                    gr=agrad[rows,ql]
                    dot=jnp.sum(gr.astype(F32)*attv[rows,ql].astype(F32),axis=-1,keepdims=True)
                    p1=pbuf[slot,rows,:m]; p2=pbuf[slot,rows,BLK:]
                    s1=(p1.astype(F32)*(mm(gr,pk[:m,vl],NT)-dot)).astype(BF)
                    s2=(p2.astype(F32)*(mm(gr,pr[:,kl],NT)-dot)).astype(BF)
                    dq[rows,ql]=((mm(s1,pk[:m,kl])+mm(s2,pr[:,ql]))*scale).astype(BF)
                    qr=pk[rows,ql]
                    a1=mm(s1,qr,TN)*scale; a2=mm(s2,qr,TN)*scale; b1=mm(p1,gr,TN); b2=mm(p2,gr,TN)
                    if r==0: first=(a1,a2,b1,b2)
                dk[0:half,ql]=(first[0]+a1[:half]).astype(BF); dk[half:,ql]=a1[half:].astype(BF)
                dv[0:half,ql]=(first[2]+b1[:half]).astype(BF); dv[half:,ql]=b1[half:].astype(BF)
                dck[:,ql]=(first[1]+a2).astype(BF); dcv[:,ql]=(first[3]+b2).astype(BF)
                return 0
            for part in range(4):
                lax.fori_loop(2*part,2*part+2,head,0)
                agenda.run(46.5+2.5*part)
            oc.wait()
        def bigger(cot_,stage_):
            nonlocal cot_own,stage
            cot_own=cot_; stage=stage_
            cl=pltpu.make_async_copy(cot,cot_,lsem.at[7]); cl.start(); cl.wait()
            pl.run_scoped(attention_part,pltpu.VMEM((BLK,d),BF),pltpu.VMEM((d,d),BF),pltpu.VMEM((BLK,3*d),BF),pltpu.VMEM((CTX,2*d),BF),pltpu.VMEM((2,BLK,BLK+CTX),BF),pltpu.VMEM((BLK,d),BF),pltpu.VMEM((BLK,d),BF))
        cot_own=stage=None
        pl.run_scoped(bigger,pltpu.VMEM((BLK,d),BF),pltpu.VMEM((BLK,d),BF))
        def conv_part(w,dn,sig,u3,g3,y3,G,rate3,dec3,sp3,d0,d1,xv,tl,ggrad1,sm):
            loads=[pltpu.make_async_copy(w_in,w,lsem.at[0]),pltpu.make_async_copy(x,xv,lsem.at[1]),pltpu.make_async_copy(tail_low,tl,lsem.at[2])]
            for v in loads: v.start()
            def g1(): send_half(1,lambda r: mm(lowv[:,r],dq[...],TN),1); agenda.add(60.,lambda: join_half(1,1))
            def g2(): send_half(2,lambda r: mm(lowv[:,r],dk[...],TN)+mm(ctxv[:,r],dck[...],TN),0); agenda.add(62.,lambda: join_half(2,0))
            def g3_(): send_half(3,lambda r: mm(lowv[:,r],dv[...],TN)+mm(ctxv[:,r],dcv[...],TN),1); agenda.add(64.,lambda: join_half(3,1))
            g1(); agenda.run(58.); g2(); agenda.run(60.); g3_(); agenda.run(62.)
            for v in loads: v.wait()
            G[...]=(mm(dck[...],w[:,d:2*d],NT)+mm(dcv[...],w[:,2*d:],NT)).astype(BF)
            rate3[...]=rates(decay3[...],length)
            dec3[...]=jnp.exp(-float(BLK)*rate3[...])
            split_lanes(G,g3,CTX)
            a=lambda k: jnp.exp(-rate3[k]); kk=lambda k: weight3[k]*jnp.sqrt(rate3[k])
            av=[a(k) for k in range(nst)]; kv=[kk(k) for k in range(nst)]
            def back(i,gs):
                t=CTX-1-i; v=g3[t]
                gs=tuple(p*z+v for p,z in zip(av,gs))
                y3[t]=tree(p*z for p,z in zip(kv,gs))
                return gs
            gs=lax.fori_loop(0,CTX,back,tuple(jnp.zeros((8,128),F32) for _ in range(nst)),unroll=2)
            for k in range(nst): s3[k]=gs[k]
            ex=Scan(ns,nst,s3,gather,spread,hb,[e0,e1,e2,e3],False)
            ex.collect()
            agenda.run(66.)
            split_lanes(tl,u3,CTX)
            up=lax.broadcasted_iota(jnp.int32,(8,128),0).astype(F32)
            for lt in range(d//128):
                ls=slice(lt*128,(lt+1)*128)
                for part in range(0,nst,8):
                    r=[jnp.broadcast_to(rate3[k,lt:lt+1,:],(8,128)) for k in range(part,part+8)]
                    a8=[jnp.exp(-8.0*v) for v in r]
                    def body(i,cr):
                        acc,der=cr
                        u=lowv[pl.ds(pl.multiple_of(i*16,16),16),ls].astype(F32)
                        for w_ in (u[:8],u[8:]):
                            der=tuple(p*(z+y) for p,z,y in zip(a8,der,acc))
                            acc=tuple(p*y+w_ for p,y in zip(a8,acc))
                        return acc,der
                    zz=tuple(jnp.zeros((8,128),F32) for _ in range(8))
                    acc,der=lax.fori_loop(0,(BLK-CTX)//16,body,(zz,zz))
                    for i,k in enumerate(range(part,part+8)):
                        j=7.0-up
                        sp3[k,lt:lt+1,:]=jnp.sum(jnp.exp(-j*r[i])*(8.0*der[i]+j*acc[i]),axis=0,keepdims=True)
                if lt==2: ex.scan(dec3)
                if lt%2==1: agenda.run(67.+lt)
            for part in range(0,nst,4):
                zz=tuple(jnp.zeros((8,128),F32) for _ in range(4))
                aa=[a(k) for k in range(part,part+4)]
                def fwd(t,cr):
                    h,hp,q0,q1=cr
                    u=u3[t]; gg=g3[t]
                    hp=tuple(p*(z+y) for p,z,y in zip(aa,hp,h))
                    h=tuple(p*z+u for p,z in zip(aa,h))
                    return h,hp,tuple(z+gg*y for z,y in zip(q0,h)),tuple(z+gg*y for z,y in zip(q1,hp))
                h,hp,q0,q1=lax.fori_loop(0,CTX,fwd,(tuple(h3[k] for k in range(part,part+4)),zz,zz,zz),unroll=2)
                for i,k in enumerate(range(part,part+4)):
                    d0[k]=q0[i]; d1[k]=q1[i]
                    m=float(BLK-CTX); am=jnp.exp(-m*rate3[k])
                    sp3[k]=aa[i]*(am*hp[i]+m*am*h[i]+sp3[k])
                agenda.run(75.+.7*part)
            ex.receive()
            for lt in range(d//128):
                ls=slice(lt*128,(lt+1)*128)
                r=[jnp.broadcast_to(rate3[k,lt:lt+1,:],(8,128)) for k in range(nst)]
                a8=[jnp.exp(-8.0*z) for z in r]
                v=tuple(jnp.broadcast_to((weight3[k,lt:lt+1,:]*jnp.sqrt(rate3[k,lt:lt+1,:]))*hb[k,lt:lt+1,:],(8,128))*jnp.exp(-(8.0-up)*r[k]) for k in range(nst))
                def two(v):
                    b=tree(v); v=tuple(p*z for p,z in zip(a8,v))
                    t=tree(v); v=tuple(p*z for p,z in zip(a8,v))
                    return jnp.concatenate([t,b],axis=0),v
                def ownrows(i,v):
                    tb,v=two(v)
                    sig[pl.ds(pl.multiple_of(BLK-CTX-16-i*16,16),16),ls]=tb.astype(BF)
                    return v
                v=lax.fori_loop(0,(BLK-CTX)//16,ownrows,v)
                def tailrows(i,v):
                    tb,v=two(v)
                    row=pl.multiple_of(CTX-16-i*16,16)
                    tailb[pl.ds(row,16),ls]=(tb+y3[pl.ds(row,16),lt,:]).astype(BF)
                    return v
                lax.fori_loop(0,CTX//16,tailrows,v)
                agenda.run(80.+.5*lt)
            bc=pltpu.make_async_remote_copy(src_ref=tailb,dst_ref=tail_in,send_sem=tsem.at[0],recv_sem=tsem.at[1],device_id={"seq":jnp.maximum(q-1,0)},device_id_type=MESH)
            @pl.when(q>0)
            def _(): bc.start()
            def dnr(r):
                rr=slice(r*256,(r+1)*256)
                dn[rr,:]=mm(dq[rr,:],w[:,:d],NT)+mm(dk[rr,:],w[:,d:2*d],NT)+mm(dv[rr,:],w[:,2*d:],NT)
            dnr(0); agenda.run(87.); dnr(1); agenda.run(89.)
            ggrad1[...]=jnp.zeros_like(ggrad1)
            def lastrows(i,_):
                rr=pl.ds(pl.multiple_of(i*64,64),64)
                dvv,gg=norm_back(xv[rr,:].astype(F32),gain1[...],dn[rr,:]+sig[rr,:].astype(F32))
                res[rr,:]=res[rr,:]+dvv
                ggrad1[...]+=fold(gg)
                return 0
            lax.fori_loop(0,(BLK-CTX)//64,lastrows,0)
            agenda.run(92.)
            @pl.when(q==ns-1)
            def _(): tail_in[...]=jnp.zeros_like(tail_in)
            @pl.when(q<ns-1)
            def _(): bc.wait_recv()
            sig[BLK-CTX:,:]=tail_in[...]
            lax.fori_loop((BLK-CTX)//64,BLK//64,lastrows,0)
            ic=pltpu.make_async_copy(res,igrad,outsem.at[1]); ic.start()
            sm[...]=jnp.zeros_like(sm)
            for k in range(nst):
                r=rate3[k]; D1=d1[k]+hb[k]*sp3[k]; sq=jnp.sqrt(r)
                kw=sq*d0[k]; kd=weight3[k]*sq*(0.5*d0[k]-r*D1)
                for lt in range(d//128):
                    sm[k:k+1,lt*128:(lt+1)*128]=kw[lt:lt+1,:]; sm[nst+k:nst+k+1,lt*128:(lt+1)*128]=kd[lt:lt+1,:]
            sm[2*nst:2*nst+1,:]=jnp.sum(ggrad1[...],axis=0,keepdims=True)
            sm[2*nst+1:2*nst+2,:]=jnp.sum(ggrad2[...],axis=0,keepdims=True)
            for j in range(d//128):
                v=jnp.transpose(sm[:,j*128:(j+1)*128]).astype(BF)
                for b in range(128//rc):
                    e=j*(128//rc)+b
                    small[e//2//ny,e//2%ny,e%2,:,0:128]=v[b*rc:(b+1)*rc]
                    small[e//2//ny,e//2%ny,e%2,:,128:]=jnp.zeros((rc,small.shape[4]-128),BF)
            sc=pltpu.make_async_remote_copy(src_ref=small.at[:,:,1-c],dst_ref=small_rec,send_sem=csem.at[0,4],recv_sem=csem.at[1,4],device_id=sib,device_id_type=MESH)
            sc.start()
            def join_small():
                sc.wait_recv()
                for z in range(nz):
                    for y in range(ny):
                        small_rec[z,y]=(small_rec[z,y].astype(F32)+small[z,y,c].astype(F32)).astype(BF)
                launch(index["S"][0])
            agenda.add(97.,join_small)
            agenda.run(98.)
            ic.wait(); sc.wait_send(); ex.drain()
            @pl.when(q>0)
            def _(): bc.wait_send()
        M=pltpu.VMEM; st=(nst,8,128)
        pl.run_scoped(conv_part,M((d,3*d),BF),M((BLK,d),F32),M((BLK,d),BF),M((CTX,8,128),F32),M((CTX,8,128),F32),M((CTX,8,128),F32),M((CTX,d),BF),M(st,F32),M(st,F32),M(st,F32),M(st,F32),M(st,F32),M((BLK,d),BF),M((CTX,d),BF),M((8,d),F32),M((128,d),F32))
    M=pltpu.VMEM
    pl.run_scoped(rest,M((BLK,d),F32),M((BLK,d),BF),M((BLK,d),BF),M((BLK,d),BF),M((CTX,d),BF),M((CTX,d),BF),M((BLK,d),BF),M((CTX,d),BF),M((8,d),F32))
    agenda.run(1e9)
    for v in bcopies: bcopy(*v).wait()
    for v in lanes: v.drain()
    for k in (2,3): ccopy(k).wait_send()

def main(n, ns, low2,cot,cots,w1,w2,residual,gain2,attended,wo,packed,pairs,probs,low,tail_low,ctx,w_in,x,gain1,decay3,weight3,h3):
    d=x.shape[1]; ff=w1.shape[1]; nz,ny,nx=n["z"],n["y"],n["x"]; nzy=nz*ny; own=ff//2; rf=own//nzy; rb=d//nzy; rc=d//ns; nst=decay3.shape[0]
    J=max(1,rf//128); rj=rf//J
    packed_w=rj%128!=0
    if packed_w:
        c=lax.rem(lax.axis_index("seq"),2)
        w1=lax.dynamic_index_in_dim(w1.reshape(d,nzy,2,rf),c,2,keepdims=False).reshape(d,own)
        w2=lax.dynamic_index_in_dim(w2.reshape(nzy,2,rf,d),c,1,keepdims=False).reshape(own,d)
    plan=plan_of(n,rf,rb,rc,d,own,ORDERS)
    V=pl.BlockSpec(memory_space=pltpu.VMEM); Y=pl.BlockSpec(memory_space=pl.ANY); M=pltpu.VMEM; D=pltpu.SemaphoreType.DMA
    wd=rj if not packed_w else 512
    scr=[M((2*BLK,d),BF),M((2*BLK,d),BF),M((nz,ny,rf,d),BF),M((nz,ny,rb,own),BF),M((2,nz,ny,2,rc,d),BF),M((4,nz,ny,rc,d),BF),M((BLK,d),BF),M((BLK,d),BF),
         M((rb,own),BF),M((nz,ny,2,rc,128*nx),BF),M((nz,ny,rc,128*nx),BF),M((CTX,d),BF),M((CTX,d),BF),
         D((own//wd,)),D((own//wd,)),D((8,)),D((2,)),D((2,)),D((2,)),D((2,5)),D((2,4)),D((2,)),D((2,)),D((2,))]
    sc=scan_scratch(ns,nst)
    scr+=[sc[0],sc[1],sc[2],M((nst,8,128),F32)]+sc[3:]
    for (t,k,r0,r,c0,cw,o) in plan: scr+=lane_scratch(n,o,r,cw)
    ins=[low2,cot,cots,w1,w2,residual,gain2,attended,wo,packed,pairs,probs,low,tail_low,ctx,w_in,x,gain1,decay3,weight3,h3]
    small_in={6,17,18,19,20}
    return pl.pallas_call(functools.partial(main_kernel,n,ns,BLK*ns,plan,packed_w),
        out_shape=[S(BLK,d),S(BLK,d,t=F32),S(rf,d),S(rc,own),S(rc,own),S(rc,4*d),S(rc,128*nx)],
        in_specs=[V if i in small_in else Y for i in range(len(ins))],out_specs=[Y,Y]+[V]*5,scratch_shapes=scr,
        compiler_params=pltpu.CompilerParams(collective_id=1,has_side_effects=True,vmem_limit_bytes=63*10**6),
        cost_estimate=pl.CostEstimate(flops=45*10**9,bytes_accessed=6*10**7,transcendentals=2*10**6),name="main")(*ins)

def local(layer_input,segment_ids,context_mask,first_gain,attention_in,kernel_weight,kernel_decay,attention_out,second_gain,expand_weight,reduce_weight,cotangent):
    ns=lax.axis_size("seq"); nx=lax.axis_size("grp"); nst=kernel_decay.shape[1]; n=sizes(nx,ns)
    q=lax.axis_index("seq"); c=lax.rem(q,2)
    x=layer_input[0]; cot=cotangent[0]; d=x.shape[1]; ff=expand_weight.shape[1]
    decay3=kernel_decay.T.reshape(nst,8,128); weight3=kernel_weight.T.reshape(nst,8,128)
    low,tail_low,packed,ctx,pairs,h3,own3,cot_sib=front(ns,x,cot,first_gain[None],decay3,weight3,attention_in)
    vis=jnp.where((context_mask[0]==1)&(q>0),0.0,NEG).astype(F32)
    probs,attended,residual,low2=attention(packed,pairs,segment_ids,vis,x,attention_out,second_gain[None])
    out,igrad,OA,keep,other,OC,OS=main(n,ns,low2,cot,cot_sib,expand_weight,reduce_weight,residual,second_gain[None],attended,attention_out,packed,pairs,probs,low,tail_low,ctx,attention_in,x,first_gain[None],decay3,weight3,h3)
    nzy=n["z"]*n["y"]; rd=d//ns; rf=ff//2//nzy; J=max(1,rf//128); rj=rf//J
    keep=keep.reshape(rd,J,nzy,rj); other=other.reshape(rd,J,nzy,rj)
    eg=jnp.stack([jnp.where(c==0,keep,other),jnp.where(c==0,other,keep)],3)
    eg=eg.transpose(0,2,3,1,4).reshape(rd,ff).astype(F32)
    OS=OS.astype(F32)
    return (out[None],igrad[None],OS[:,2*nst],OC[:,d:].astype(F32),OS[:,:nst],OS[:,nst:2*nst],OC[:,:d].astype(F32),OS[:,2*nst+1],eg,OA.astype(F32))

def solution(mesh):
    ins=(P("grp","seq",None),P("grp","seq"),P("grp","seq",None))+(P(),)*8+(P("grp","seq",None),)
    outs=(P("grp","seq",None),)*2+(P("seq"),)+(P("seq",None),)*4+(P("seq"),)+(P("seq",None),)*2
    return jax.shard_map(local,mesh=mesh,in_specs=ins,out_specs=outs,check_vma=False)
```

```python
import functools
import heapq
import itertools
import math

import jax
import jax.numpy as jnp
from jax import lax
from jax.experimental import pallas as pl
from jax.experimental.pallas import tpu as pltpu
from jax.sharding import PartitionSpec as P

MESH=pl.DeviceIdType.MESH
BF=jnp.bfloat16

def sizes(nx, ns):
    ny = nx if ns % (2*nx)==0 else 1
    return {"x":nx,"y":ny,"z":ns//(2*ny)}

class Place:
    def __init__(s, n):
        s.n=n; q=lax.axis_index("seq")
        s.i=dict(x=lax.axis_index("grp"), y=lax.rem(lax.div(q,2),n["y"]), z=lax.div(q,2*n["y"])); s.c=lax.rem(q,2)
    def at(s, ax, k):
        return lax.rem(s.i[ax]+k, s.n[ax])
    def device(s, ax, k):
        j=dict(s.i); j[ax]=s.at(ax,k)
        return {"grp":j["x"],"seq":(j["z"]*s.n["y"]+j["y"])*2+s.c}
    def sibling(s):
        return {"seq":(s.i["z"]*s.n["y"]+s.i["y"])*2+1-s.c}
    def partners(s):
        return [s.device(ax,k) for ax in "xyz" for k in range(1,s.n[ax])]

def stage_shapes(n, order, rows, cw):
    left=dict(n); out=[]
    for ax in order:
        del left[ax]
        out.append(tuple(left[a] for a in "zy" if a in left)+(rows, cw*(left["x"] if "x" in left else 1)))
    return out


EPS=1e-5
BLK=512; CTX=128; HEADS=8; HD=128
F32=jnp.float32

def norm_rows(src, gain, dst, rows, step=64):
    def body(i,_):
        rr=pl.ds(pl.multiple_of(i*step,16),step)
        x=src[rr,:].astype(F32)
        x=x-jnp.mean(x,axis=-1,keepdims=True)
        v=jnp.mean(x*x,axis=-1,keepdims=True)
        dst[rr,:]=(x*lax.rsqrt(v+EPS)*gain).astype(BF)
        return 0
    lax.fori_loop(0,rows//step,body,0)

def rates(decay, length):
    return jnp.exp(decay)*(1.0/length)

def block_state(low, rate3, row0, rows, put):
    nst=rate3.shape[0]
    back=7.0-lax.broadcasted_iota(jnp.int32,(8,128),0).astype(F32)
    for lt in range(low.shape[1]//128):
        lanes=pl.ds(lt*128,128)
        r=[jnp.broadcast_to(rate3[n,lt:lt+1,:],(8,128)) for n in range(nst)]
        a8=[jnp.exp(-8.0*v) for v in r]
        def body(g,acc):
            u=low[pl.ds(pl.multiple_of(row0+g*16,16),16),lanes].astype(F32)
            lo,hi=u[:8],u[8:]
            acc=tuple(a*c+lo for a,c in zip(a8,acc))
            return tuple(a*c+hi for a,c in zip(a8,acc))
        acc=lax.fori_loop(0,rows//16,body,tuple(jnp.zeros((8,128),F32) for _ in range(nst)),unroll=2)
        for n in range(nst):
            put(n,lt,jnp.sum(acc[n]*jnp.exp(-back*r[n]),axis=0,keepdims=True))

def split_lanes(src, dst, rows):
    def body(g,_):
        for lt in range(src.shape[1]//128):
            v=src[pl.ds(pl.multiple_of(g*16,16),16),lt*128:(lt+1)*128].astype(F32)
            dst[pl.ds(g*16,16),lt,:]=v
        return 0
    lax.fori_loop(0,rows//16,body,0)

def join_lanes(src, dst, rows):
    def body(g,_):
        for lt in range(dst.shape[1]//128):
            dst[pl.ds(pl.multiple_of(g*16,16),16),lt*128:(lt+1)*128]=src[pl.ds(g*16,16),lt,:].astype(dst.dtype)
        return 0
    lax.fori_loop(0,rows//16,body,0)

class Scan:
    def __init__(s, ns, nst, s3, gather, spread, h3, sem, forward):
        s.ns,s.nst,s.s3,s.gather,s.spread,s.h3=ns,nst,s3,gather,spread,h3
        s.sem=sem; s.forward=forward; s.q=lax.axis_index("seq"); s.stride=ns//nst
        s.n=lax.div(s.q,s.stride); s.scans=lax.rem(s.q,s.stride)==0
    def to_scanner(s, n):
        return pltpu.make_async_remote_copy(src_ref=s.s3.at[n],dst_ref=s.gather.at[s.q],send_sem=s.sem[0].at[n],recv_sem=s.sem[1].at[s.q],device_id={"seq":n*s.stride},device_id_type=MESH)
    def from_block(s, b):
        return pltpu.make_async_remote_copy(src_ref=s.s3.at[0],dst_ref=s.gather.at[b],send_sem=s.sem[0].at[0],recv_sem=s.sem[1].at[b],device_id={"seq":b},device_id_type=MESH)
    def to_block(s, b):
        return pltpu.make_async_remote_copy(src_ref=s.spread.at[b],dst_ref=s.h3.at[s.n],send_sem=s.sem[2].at[b],recv_sem=s.sem[3].at[s.n],device_id={"seq":b},device_id_type=MESH)
    def from_scanner(s, n):
        return pltpu.make_async_remote_copy(src_ref=s.spread.at[0],dst_ref=s.h3.at[n],send_sem=s.sem[2].at[0],recv_sem=s.sem[3].at[n],device_id={"seq":n*s.stride},device_id_type=MESH)
    def each(s, count, fn, skip):
        def body(i,_):
            @pl.when(i!=skip)
            def _(): fn(i)
            return 0
        lax.fori_loop(0,count,body,0)
    def collect(s):
        mine=jnp.where(s.scans,s.n,s.nst)
        s.each(s.nst,lambda n:s.to_scanner(n).start(),mine)
    def scan(s, decay_block):
        mine=jnp.where(s.scans,s.n,s.nst)
        @pl.when(s.scans)
        def _():
            s.gather[s.q]=s.s3[s.n]
            s.each(s.ns,lambda b:s.from_block(b).wait_recv(),s.q)
            a=decay_block[s.n]
            def body(i,h):
                b=i if s.forward else s.ns-1-i
                s.spread[b]=h
                return a*h+s.gather[b]
            lax.fori_loop(0,s.ns,body,jnp.zeros((8,128),F32))
            s.each(s.ns,lambda b:s.to_block(b).start(),s.q)
            s.h3[s.n]=s.spread[s.q]
    def receive(s):
        mine=jnp.where(s.scans,s.n,s.nst)
        s.each(s.nst,lambda n:s.from_scanner(n).wait_recv(),mine)
    def drain(s):
        mine=jnp.where(s.scans,s.n,s.nst)
        s.each(s.nst,lambda n:s.to_scanner(n).wait_send(),mine)
        @pl.when(s.scans)
        def _(): s.each(s.ns,lambda b:s.to_block(b).wait_send(),s.q)

def scan_scratch(ns,nst):
    return [pltpu.VMEM((nst,8,128),F32),pltpu.VMEM((ns,8,128),F32),pltpu.VMEM((ns,8,128),F32),
      pltpu.SemaphoreType.DMA((nst,)),pltpu.SemaphoreType.DMA((ns,)),pltpu.SemaphoreType.DMA((ns,)),pltpu.SemaphoreType.DMA((nst,))]

def front_kernel(ns, length, x, cot, gain, decay, weight, w_hbm, low, tail_low, packed, ctx, pairs, h3, decay3, weight3, cot_sib,
                 w, own3, tail_x, rate3, dec3, u3, y3, s3, gather, spread, e0, e1, e2, e3, wsem, tsem, csem):
    q=lax.axis_index("seq"); c=lax.rem(q,2); g=lax.axis_index("grp")
    nst=decay.shape[0]
    sem=pltpu.get_barrier_semaphore()
    def sig(i,_):
        @pl.when(i!=q)
        def _(): pl.semaphore_signal(sem,inc=1,device_id={"seq":i},device_id_type=MESH)
        return 0
    lax.fori_loop(0,ns,sig,0)
    wcp=pltpu.make_async_copy(w_hbm,w,wsem); wcp.start()
    pl.semaphore_wait(sem,ns-1)
    tail=pltpu.make_async_remote_copy(src_ref=x.at[pl.ds(BLK-CTX,CTX),:],dst_ref=tail_x,send_sem=tsem.at[0],recv_sem=tsem.at[1],device_id={"seq":jnp.minimum(q+1,ns-1)},device_id_type=MESH)
    @pl.when(q<ns-1)
    def _(): tail.start()
    cc=pltpu.make_async_remote_copy(src_ref=cot,dst_ref=cot_sib,send_sem=csem.at[0],recv_sem=csem.at[1],device_id={"seq":q+1-2*c},device_id_type=MESH)
    cc.start()
    for lt in range(low.shape[1]//128):
        rows=slice(lt*128,(lt+1)*128)
        decay3[:,lt,:]=decay[:,rows]; weight3[:,lt,:]=weight[:,rows]
    rate3[...]=rates(decay3[...],length)
    dec3[...]=jnp.exp(-float(BLK)*rate3[...])
    norm_rows(x,gain[...],low,BLK)
    def put_own(n,lt,v): own3[n,lt:lt+1,:]=v
    block_state(low,rate3,0,BLK-CTX,put_own)
    wcp.wait()
    half=packed.shape[1]//2
    packed[:,:half]=jnp.dot(low[...],w[:,:half],preferred_element_type=F32).astype(BF)
    @pl.when(q>0)
    def _(): tail.wait_recv()
    @pl.when(q==0)
    def _(): tail_x[...]=jnp.zeros_like(tail_x)
    norm_rows(tail_x,gain[...],tail_low,CTX)
    def put_tail(n,lt,v): s3[n,lt:lt+1,:]=v
    block_state(tail_low,rate3,0,CTX,put_tail)
    for n in range(nst):
        s3[n]=jnp.exp(-float(BLK-CTX)*rate3[n])*s3[n]+own3[n]
    ex=Scan(ns,nst,s3,gather,spread,h3,[e0,e1,e2,e3],True)
    ex.collect()
    split_lanes(tail_low,u3,CTX)
    packed[:,half:2*half-half//3]=jnp.dot(low[...],w[:,half:2*half-half//3],preferred_element_type=F32).astype(BF)
    ex.scan(dec3)
    packed[:,2*half-half//3:]=jnp.dot(low[...],w[:,2*half-half//3:],preferred_element_type=F32).astype(BF)
    ex.receive()
    a=[jnp.exp(-rate3[n]) for n in range(nst)]
    k=[weight3[n]*jnp.sqrt(rate3[n]) for n in range(nst)]
    def step(t,h):
        u=u3[t]
        h=tuple(p*v+u for p,v in zip(a,h))
        ys=[p*v for p,v in zip(k,h)]
        while len(ys)>1: ys=[ys[i]+ys[i+1] if i+1<len(ys) else ys[i] for i in range(0,len(ys),2)]
        y3[t]=ys[0]
        return h
    lax.fori_loop(0,CTX,step,tuple(h3[n] for n in range(nst)),unroll=2)
    join_lanes(y3,ctx,CTX)
    d=low.shape[1]
    pairs[...]=jnp.dot(ctx[...],w[:,d:],preferred_element_type=F32).astype(BF)
    ex.drain()
    @pl.when(q<ns-1)
    def _(): tail.wait_send()
    cc.wait()

def front(ns, x, cot, gain, decay, weight, w):
    nst=decay.shape[0]; d=x.shape[1]
    V=pl.BlockSpec(memory_space=pltpu.VMEM); A=pl.BlockSpec(memory_space=pl.ANY)
    S=lambda *s,t=BF: jax.ShapeDtypeStruct(s,t)
    return pl.pallas_call(functools.partial(front_kernel,ns,x.shape[0]*ns),
        out_shape=[S(BLK,d),S(CTX,d),S(BLK,3*d),S(CTX,d),S(CTX,2*d),S(nst,8,128,t=F32),S(nst,8,128,t=F32),S(nst,8,128,t=F32),S(BLK,d)],
        in_specs=[V,A,V,V,V,A],out_specs=[V]*8+[A],
        scratch_shapes=[pltpu.VMEM((d,3*d),BF),pltpu.VMEM((nst,8,128),F32),pltpu.VMEM((CTX,d),BF),pltpu.VMEM((nst,8,128),F32),pltpu.VMEM((nst,8,128),F32),
          pltpu.VMEM((CTX,8,128),F32),pltpu.VMEM((CTX,8,128),F32)]+scan_scratch(ns,nst)+[pltpu.SemaphoreType.DMA,pltpu.SemaphoreType.DMA((2,)),pltpu.SemaphoreType.DMA((2,))],
        compiler_params=pltpu.CompilerParams(collective_id=0,has_side_effects=True,vmem_limit_bytes=63*10**6),
        name="front")(x,cot,gain,decay,weight,w)

NEG=-1e30
NT=(((1,),(1,)),((),()))
TN=(((0,),(0,)),((),()))
NN=(((1,),(0,)),((),()))
def mm(a,b,dims=NN): return lax.dot_general(a,b,dims,preferred_element_type=F32)

def attention_kernel(q,k,v,ck,cv,seg,vis,x,wo,gain,probs,attended,residual,low2,bias):
    h=pl.program_id(0)
    @pl.when(h==0)
    def _():
        row=jnp.broadcast_to(seg[...].astype(F32),(128,BLK))
        col=jnp.transpose(row)
        for i in range(BLK//128):
            ci=col[i*128:(i+1)*128]
            for j in range(BLK//128):
                if j>i:
                    bias[i*128:(i+1)*128,j*128:(j+1)*128]=jnp.full((128,128),NEG,F32); continue
                ok=ci==row[:,j*128:(j+1)*128]
                if i==j: ok=ok&(lax.broadcasted_iota(jnp.int32,(128,128),0)>=lax.broadcasted_iota(jnp.int32,(128,128),1))
                bias[i*128:(i+1)*128,j*128:(j+1)*128]=jnp.where(ok,0.0,NEG)
        seen=jnp.where((vis[...]==1)&(lax.axis_index("seq")>0),0.0,NEG)
        bias[:,BLK:]=jnp.broadcast_to(seen,(BLK,CTX))
    scale=1.0/math.sqrt(HD)
    half=BLK//2
    for r in range(2):
        rows=slice(r*half,(r+1)*half); n=(r+1)*half
        s1=mm(q[rows,:],k[:n,:],NT)*scale+bias[rows,:n]
        s2=mm(q[rows,:],ck[...],NT)*scale+bias[rows,BLK:]
        top=jnp.maximum(jnp.max(s1,axis=-1,keepdims=True),jnp.max(s2,axis=-1,keepdims=True))
        e1=jnp.exp(s1-top); e2=jnp.exp(s2-top)
        inv=1.0/(jnp.sum(e1,axis=-1,keepdims=True)+jnp.sum(e2,axis=-1,keepdims=True))
        p1=(e1*inv).astype(BF); p2=(e2*inv).astype(BF)
        probs[0,rows,:n]=p1; probs[0,rows,BLK:]=p2
        if n<BLK: probs[0,rows,n:BLK]=jnp.zeros((half,BLK-n),BF)
        o=mm(p1,v[:n,:])+mm(p2,cv[...])
        attended[rows,pl.ds(pl.multiple_of(h*HD,HD),HD)]=o.astype(BF)
    @pl.when(h==HEADS-1)
    def _():
        def body(i,_):
            rr=pl.ds(pl.multiple_of(i*128,128),128)
            res=x[rr,:].astype(F32)+mm(attended[rr,:],wo[...])
            residual[rr,:]=res
            m=res-jnp.mean(res,axis=-1,keepdims=True)
            var=jnp.mean(m*m,axis=-1,keepdims=True)
            low2[rr,:]=(m*lax.rsqrt(var+EPS)*gain[...]).astype(BF)
            return 0
        lax.fori_loop(0,BLK//128,body,0)

def attention(packed,pairs,seg,vis,x,wo,gain):
    d=x.shape[1]
    S=lambda *s,t=BF: jax.ShapeDtypeStruct(s,t)
    full=lambda a: pl.BlockSpec(a.shape,lambda h:(0,)*a.ndim)
    return pl.pallas_call(attention_kernel,grid=(HEADS,),
      in_specs=[pl.BlockSpec((BLK,HD),lambda h:(0,h)),pl.BlockSpec((BLK,HD),lambda h:(0,HEADS+h)),pl.BlockSpec((BLK,HD),lambda h:(0,2*HEADS+h)),
        pl.BlockSpec((CTX,HD),lambda h:(0,h)),pl.BlockSpec((CTX,HD),lambda h:(0,HEADS+h)),full(seg),full(vis),full(x),full(wo),full(gain)],
      out_specs=[pl.BlockSpec((1,BLK,BLK+CTX),lambda h:(h,0,0)),pl.BlockSpec((BLK,d),lambda h:(0,0)),pl.BlockSpec((BLK,d),lambda h:(0,0)),pl.BlockSpec((BLK,d),lambda h:(0,0))],
      out_shape=[S(HEADS,BLK,BLK+CTX),S(BLK,d),S(BLK,d,t=F32),S(BLK,d)],
      scratch_shapes=[pltpu.VMEM((BLK,BLK+CTX),F32)],
      compiler_params=pltpu.CompilerParams(vmem_limit_bytes=63*10**6),
      cost_estimate=pl.CostEstimate(flops=4*10**9,bytes_accessed=2*10**7,transcendentals=3*10**6),
      name="attention")(packed,packed,packed,pairs,pairs,seg,vis,x,wo,gain)

G0=math.sqrt(2/math.pi); G1=0.044715
def gelu_pair(h):
    h2=h*h
    th=jnp.tanh(h*(G0+G0*G1*h2))
    p=0.5*(1.0+th)
    return h*p, p+h*(0.5*(1.0-th*th))*(G0+3*G0*G1*h2)


def norm_back(v, gain, dy):
    x=v-jnp.mean(v,axis=-1,keepdims=True)
    s=lax.rsqrt(jnp.mean(x*x,axis=-1,keepdims=True)+EPS)
    nrm=x*s
    dn=dy*gain
    dv=(dn-jnp.mean(dn,axis=-1,keepdims=True)-nrm*jnp.mean(dn*nrm,axis=-1,keepdims=True))*s
    return dv, dy*nrm
def fold(v):
    return jnp.sum(v.reshape(v.shape[0]//8,8,v.shape[1]),axis=0)


def S(*s,t=BF): return jax.ShapeDtypeStruct(s,t)


class Lane:
    def __init__(s, place, order, rows, cw, src, out, scratch):
        s.p,s.order,s.rows,s.cw,s.src,s.out=place,order,rows,cw,src,out
        s.recv=scratch[:3]; s.ss,s.rs=scratch[3],scratch[4]
        s.begun=[]
        s.mine=pl.ds(pl.multiple_of(place.i["x"]*cw,128),cw)
    def held(s, stage, fixed):
        if stage==0: return s.src(fixed)
        left=[a for a in "zyx" if a not in s.order[:stage]]
        cols=slice(None)
        if "x" in fixed and "x" in left: cols=pl.ds(pl.multiple_of(fixed["x"]*s.cw,128),s.cw)
        return s.recv[stage-1].at[(0,)+tuple(fixed.get(a,slice(None)) for a in "zy" if a in left)+(slice(None),cols)]
    def copy(s, stage, k):
        ax="x" if stage==3 else s.order[stage]
        if stage==3: src=s.out.at[:,s.mine]; dst=s.out.at[:,s.mine]
        else: src=s.held(stage,{ax:s.p.at(ax,k)}); dst=s.recv[stage].at[k-1]
        return pltpu.make_async_remote_copy(src_ref=src,dst_ref=dst,send_sem=s.ss.at[stage,k-1],recv_sem=s.rs.at[stage,k-1],device_id=s.p.device(ax,k),device_id_type=MESH)
    def start(s, stage):
        for k in range(1,s.p.n["x" if stage==3 else s.order[stage]]):
            s.copy(stage,k).start(); s.begun.append((stage,k))
    def drain(s):
        for stage,k in s.begun: s.copy(stage,k).wait_send()
    def finish(s, stage):
        for st,k in s.begun:
            if st==stage: s.copy(st,k).wait_recv()
        if stage==3: return
        ax=s.order[stage]; n=s.p.n
        left=[a for a in "zy" if a not in s.order[:stage+1]]
        R=s.recv[stage]; step=min(s.rows,32)
        for lead in itertools.product(*[range(n[a]) for a in left]):
            fixed=dict(zip(left,lead)); fixed[ax]=s.p.i[ax]
            own=s.held(stage,fixed)
            def body(r,_):
                rr=pl.ds(pl.multiple_of(r*step,16),step)
                v=own[rr,:].astype(F32)
                for k in range(n[ax]-1): v=v+R[(k,)+lead+(rr,slice(None))].astype(F32)
                if stage==2: s.out[rr,s.mine]=v.astype(BF)
                else: R[(0,)+lead+(rr,slice(None))]=v.astype(BF)
                return 0
            if s.rows==step: body(0,0)
            else: lax.fori_loop(0,s.rows//step,body,0)

def lane_scratch(n, order, rows, cw):
    most=max(n.values())-1
    return [pltpu.VMEM((n[ax]-1,)+sh,BF) for ax,sh in zip(order,stage_shapes(n,order,rows,cw))]+[pltpu.SemaphoreType.DMA((4,most)),pltpu.SemaphoreType.DMA((4,most))]

def cut(ref, place, row0, rows, col0, cw):
    def src(fixed):
        cols=pl.ds(pl.multiple_of(col0+fixed["x"]*cw,128),cw) if "x" in fixed else pl.ds(col0,cw*place.n["x"])
        return ref.at[tuple(fixed.get(a,slice(None)) for a in "zy")+(pl.ds(row0,rows),cols)]
    return src

def plan_of(n, rf, rb, rc, d, own):
    nx=n["x"]; J=max(1,rf//128); plan=[]
    parts=8 if rf//8>=16 else rf//16
    for i in range(parts): plan.append(("A",0 if J>1 and i<parts//2 else 1,i*(rf//parts),rf//parts,0,d//nx))
    w=max(256,128*nx)
    for c0 in range(0,own,w): plan.append(("B",c0//512,0,rb,c0,w//nx))
    w=max(512,128*nx)
    for k in range(4):
        for c0 in range(0,d,w): plan.append(("C",k,0,rc,c0,w//nx))
    plan.append(("S",0,0,rc,0,128))
    seen={}; full=[]
    for p in plan:
        j=seen.get(p[0],0); seen[p[0]]=j+1
        full.append(p+(ORDERS[p[0]][j%len(ORDERS[p[0]])],))
    return full
ORDERS=dict(A=["zyx","yzx","xyz","xyz","yxz","xyz","yxz","yzx"],B=["xzy","zxy","yxz","xzy","yzx","yxz","xyz","yzx"],
            C=["xyz","xyz","yzx","xyz","xyz","xyz","xyz","xyz"],S=["xyz"])
LINK=91e3; LAT=4.0; MARGIN=1.0; COST=.25

def steps():
    T=[5.0]
    for t in range(4):
        T+=[4.2,("B",t),None,1.4]
        if t%2: T+=[("A",t//2)]
        T+=[None]
    T+=[2.8,None]*4+[.5]+[1.3,None]*4+[1.5,None,1.3,("C",0),None]+[1.9,None]*4
    T+=[1.6,None,1.7,("C",1),None,1.7,("C",2),None,1.5,("C",3),None,1.,None]
    T+=[2.4,None]*4+[1.0,None]*4+[.6,None]*8+[1.8,None]*2+[2.,None,2.5,None,2.,("S",0),None]
    return T

def arrivals(n, plan):
    now=0.; free=dict(x=0.,y=0.,z=0.); wait=[]; count=itertools.count(); res=[]; T=steps()
    def start(i,s):
        _,_,_,r0,_,cw,order=plan[i]; r=plan[i][3]
        if s<3:
            ax=order[s]; vol=math.prod(stage_shapes(n,order,r,cw)[s])*4*(n[ax]**2/4 if n[ax]>2 else 1)
        else: ax="x"; vol=r*cw*4
        free[ax]=max(now,free[ax])+vol/LINK
        heapq.heappush(wait,(free[ax]+LAT,next(count),i,s))
    for at,v in enumerate(T):
        if v is None:
            got=[]
            while wait and (wait[0][0]+MARGIN<=now or at==len(T)-1):
                a,_,i,s=heapq.heappop(wait); now=max(now,a)+COST; got.append((i,s))
                if s<3: start(i,s+1)
            res.append(got)
        elif isinstance(v,tuple):
            for i,p in enumerate(plan):
                if p[:2]==v: start(i,0)
        else: now+=v
    return res

def tree(ys):
    ys=list(ys)
    while len(ys)>1: ys=[ys[i]+ys[i+1] if i+1<len(ys) else ys[i] for i in range(0,len(ys),2)]
    return ys[0]

def main_kernel(n, ns, length, plan, packed_w, *refs):
    (low2,cot,cots,w1,w2,residual,gain2,attended,wo,packed,pairs,probs,low,tail_low,ctx,w_in,x,gain1,decay3,weight3,h3,
     out,igrad,OA,OBk,OBr,OC,OS,
     x2,cot2,A,B,Cf,crec,dx_rec,out_rec,OBf,small,small_rec,tailb,tail_in,
     wsem1,wsem2,lsem,xsem,dsem,osem,csem,bsem,tsem,psem,outsem,s3,gather,spread,hb,e0,e1,e2,e3)=refs[:60]
    scr=refs[60:]
    place=Place(n); c=place.c; sib=place.sibling(); q=lax.axis_index("seq"); g=lax.axis_index("grp")
    d=x2.shape[1]; nz,ny=n["z"],n["y"]; nzy=nz*ny; rf=A.shape[2]; rb=B.shape[2]; own=B.shape[3]; rc=crec.shape[3]
    nst=decay3.shape[0]; J=max(1,rf//128); rj=rf//J
    sem=pltpu.get_barrier_semaphore()
    def sg(i,_):
        @pl.when(i!=q)
        def _(): pl.semaphore_signal(sem,inc=1,device_id={"seq":i},device_id_type=MESH)
        return 0
    lax.fori_loop(0,ns,sg,0)
    for k in range(1,n["x"]): pl.semaphore_signal(sem,inc=1,device_id=place.device("x",k),device_id_type=MESH)
    due=arrivals(n,plan); at=[0]
    outs={"A":OA,"B":OBf,"C":OC,"S":OS}; srcs={"A":lambda k:A,"B":lambda k:B,"C":lambda k:crec.at[k],"S":lambda k:small_rec}
    lanes=[]
    for i,(t,k,r0,r,c0,cw,o) in enumerate(plan):
        oc=(k*d+c0 if t=="C" else c0)
        lanes.append(Lane(place,o,r,cw,cut(srcs[t](k),place,r0,r,c0,cw),outs[t].at[pl.ds(r0,r),pl.ds(oc,cw*n["x"])],scr[5*i:5*i+5]))
    index={}
    for i,p in enumerate(plan): index.setdefault(p[0],[]).append(i)
    bcopies=[]
    def bcopy(c0,w):
        h=rb//2; cs=pl.ds(c0,w)
        return pltpu.make_async_remote_copy(src_ref=OBf.at[pl.ds(pl.multiple_of((1-c)*h,16),h),cs],dst_ref=OBr.at[:,cs],send_sem=bsem.at[0,c0//256],recv_sem=bsem.at[1,c0//256],device_id=sib,device_id_type=MESH)
    def launch(group,k):
        for i in index[group]:
            if plan[i][1]==k: lanes[i].start(0)
    def point():
        for i,s in due[at[0]]:
            lanes[i].finish(s)
            if s<3: lanes[i].start(s+1)
            elif plan[i][0]=="B":
                c0,w=plan[i][4],plan[i][5]*n["x"]; cs=pl.ds(c0,w); h=rb//2
                bcopy(c0,w).start(); bcopies.append((c0,w))
                OBk[:,cs]=OBf[pl.ds(pl.multiple_of(c*h,16),h),cs]
        at[0]+=1

    def forward_part(w1s,w2s,act,dexp):
        tiles=own//512; wd=rj if rj%128==0 else 512; per=512//wd
        def wcopy(b):
            if packed_w: s1=s2=b*wd
            else: s1=s2=lax.rem(b,nzy)*(2*rf)+c*rf+lax.div(b,nzy)*rj
            return (pltpu.make_async_copy(w1.at[:,pl.ds(pl.multiple_of(s1,128),wd)],w1s.at[:,pl.ds(pl.multiple_of(b*wd,128),wd)],wsem1.at[b]),
                    pltpu.make_async_copy(w2.at[pl.ds(pl.multiple_of(s2,16),wd),:],w2s.at[pl.ds(pl.multiple_of(b*wd,16),wd),:],wsem2.at[b]))
        cc=[pltpu.make_async_copy(cot,cot2.at[pl.ds(0,BLK),:],lsem.at[0]),pltpu.make_async_copy(cots,cot2.at[pl.ds(BLK,BLK),:],lsem.at[1]),pltpu.make_async_copy(low2,x2.at[pl.ds(0,BLK),:],lsem.at[2])]
        for v in cc: v.start()
        def go(b,_):
            u,v=wcopy(b); v.start(); u.start(); return 0
        lax.fori_loop(0,own//wd,go,0)
        pl.semaphore_wait(sem,ns-1+n["x"]-1)
        xs=pltpu.make_async_remote_copy(src_ref=low2,dst_ref=x2.at[pl.ds(BLK,BLK),:],send_sem=xsem.at[0],recv_sem=xsem.at[1],device_id=sib,device_id_type=MESH)
        xs.start()
        for v in cc: v.wait()
        for t in range(tiles):
            for b in range(t*per,(t+1)*per): wcopy(b)[1].wait()
            cs=slice(t*512,(t+1)*512)
            u=mm(cot2[...],w2s[cs,:],NT)
            for b in range(t*per,(t+1)*per): wcopy(b)[0].wait()
            if t==0: xs.wait()
            h=mm(x2[...],w1s[:,cs])
            a,gp=gelu_pair(h)
            act[:,cs]=a.astype(BF); dexp[:,cs]=(u*gp).astype(BF)
            v=mm(x2[...],dexp[:,cs],TN).astype(BF)
            for b in range(nzy): B[b//ny,b%ny,:,cs]=v[b*rb:(b+1)*rb]
            launch("B",t)
            point()
            v=mm(act[:,cs],cot2[...],TN).astype(BF)
            for b in range(512//rj):
                e=t*(512//rj)+b; j,zy=e//nzy,e%nzy
                A[zy//ny,zy%ny,j*rj:(j+1)*rj,:]=v[b*rj:(b+1)*rj]
            if t%2: launch("A",t//2)
            point()
        cot2[0:BLK,:]=mm(dexp[BLK:,:],w1s[...],NT).astype(BF)
        dc=pltpu.make_async_remote_copy(src_ref=cot2.at[pl.ds(0,BLK),:],dst_ref=dx_rec,send_sem=dsem.at[0],recv_sem=dsem.at[1],device_id=sib,device_id_type=MESH); dc.start()
        point()
        cot2[BLK:,:]=mm(act[BLK:,:],w2s[...]).astype(BF)
        oc=pltpu.make_async_remote_copy(src_ref=cot2.at[pl.ds(BLK,BLK),:],dst_ref=out_rec,send_sem=osem.at[0],recv_sem=osem.at[1],device_id=sib,device_id_type=MESH); oc.start()
        point()
        x2[0:BLK,:]=mm(dexp[0:BLK,:],w1s[...],NT).astype(BF)
        point()
        x2[BLK:,:]=mm(act[0:BLK,:],w2s[...]).astype(BF)
        point()
        dc.wait(); oc.wait()
    pl.run_scoped(forward_part,pltpu.VMEM((d,own),BF),pltpu.VMEM((own,d),BF),pltpu.VMEM((2*BLK,own),BF),pltpu.VMEM((2*BLK,own),BF))

    def ccopy(k):
        return pltpu.make_async_remote_copy(src_ref=Cf.at[k%2,:,:,1-c],dst_ref=crec.at[k],send_sem=csem.at[0,k],recv_sem=csem.at[1,k],device_id=sib,device_id_type=MESH)
    joined=set()
    def send_half(k, part, slot):
        if k>=2: join_half(k-2); ccopy(k-2).wait_send()
        for r in range(2):
            v=part(slice(r*d//2,(r+1)*d//2)).astype(BF)
            for b in range(nzy):
                e=r*nzy+b
                Cf[slot,e//2//ny,e//2%ny,e%2]=v[b*rc:(b+1)*rc]
        ccopy(k).start()
    def join_half(k):
        if k in joined: return
        joined.add(k); slot=k%2
        ccopy(k).wait_recv()
        def add(z,_):
            for y in range(ny):
                for h in range(rc//16):
                    rr=slice(h*16,h*16+16)
                    crec[k,z,y,rr,:]=(crec[k,z,y,rr,:].astype(F32)+Cf[slot,z,y,c,rr,:].astype(F32)).astype(BF)
            return 0
        lax.fori_loop(0,nz,add,0)
        launch("C",k)

    def rest(res,dq,dk,dv,dck,dcv,lowv,ctxv,ggrad2):
        loads=[pltpu.make_async_copy(residual,res,lsem.at[0]),pltpu.make_async_copy(low,lowv,lsem.at[1]),pltpu.make_async_copy(ctx,ctxv,lsem.at[2])]
        for v in loads: v.start()
        def attention_part(attv,wov,pk,pr,pbuf,branch,agrad):
            more=[pltpu.make_async_copy(attended,attv,lsem.at[3]),pltpu.make_async_copy(wo,wov,lsem.at[4]),pltpu.make_async_copy(packed,pk,lsem.at[5]),pltpu.make_async_copy(pairs,pr,lsem.at[6])]
            for v in more: v.start()
            def pload(h): return pltpu.make_async_copy(probs.at[h],pbuf.at[lax.rem(h,2)],psem.at[lax.rem(h,2)])
            pload(0).start()
            for v in loads: v.wait()
            ggrad2[...]=jnp.zeros_like(ggrad2)
            for part in range(4):
                def body(i,_):
                    rr=pl.ds(pl.multiple_of(part*128+i*64,64),64)
                    dy=x2[rr,:].astype(F32)+dx_rec[rr,:].astype(F32)
                    dvv,gg=norm_back(res[rr,:],gain2[...],dy)
                    stage[rr,:]=(res[rr,:]+x2[pl.ds(pl.multiple_of(BLK+part*128+i*64,64),64),:].astype(F32)+out_rec[rr,:].astype(F32)).astype(BF)
                    r=cot_own[rr,:].astype(F32)+dvv
                    res[rr,:]=r; branch[rr,:]=r.astype(BF)
                    ggrad2[...]+=fold(gg)
                    return 0
                lax.fori_loop(0,2,body,0)
                point()
            oc=pltpu.make_async_copy(stage,out,outsem.at[0]); oc.start()
            for v in more: v.wait()
            send_half(0,lambda r: mm(attv[:,r],branch[...],TN),0)
            point()
            agrad[...]=mm(branch[...],wov[...],NT).astype(BF)
            join_half(0); point()
            scale=1.0/math.sqrt(HD); half=BLK//2
            def head(h,_):
                @pl.when(h<HEADS-1)
                def _(): pload(h+1).start()
                pload(h).wait()
                slot=lax.rem(h,2)
                ql=pl.ds(pl.multiple_of(h*HD,128),HD); kl=pl.ds(pl.multiple_of(d+h*HD,128),HD); vl=pl.ds(pl.multiple_of(2*d+h*HD,128),HD)
                for r in range(2):
                    rows=slice(r*half,(r+1)*half); m=(r+1)*half
                    gr=agrad[rows,ql]
                    dot=jnp.sum(gr.astype(F32)*attv[rows,ql].astype(F32),axis=-1,keepdims=True)
                    p1=pbuf[slot,rows,:m]; p2=pbuf[slot,rows,BLK:]
                    s1=(p1.astype(F32)*(mm(gr,pk[:m,vl],NT)-dot)).astype(BF)
                    s2=(p2.astype(F32)*(mm(gr,pr[:,kl],NT)-dot)).astype(BF)
                    dq[rows,ql]=((mm(s1,pk[:m,kl])+mm(s2,pr[:,ql]))*scale).astype(BF)
                    qr=pk[rows,ql]
                    a1=mm(s1,qr,TN)*scale; a2=mm(s2,qr,TN)*scale; b1=mm(p1,gr,TN); b2=mm(p2,gr,TN)
                    if r==0: first=(a1,a2,b1,b2)
                dk[0:half,ql]=(first[0]+a1[:half]).astype(BF); dk[half:,ql]=a1[half:].astype(BF)
                dv[0:half,ql]=(first[2]+b1[:half]).astype(BF); dv[half:,ql]=b1[half:].astype(BF)
                dck[:,ql]=(first[1]+a2).astype(BF); dcv[:,ql]=(first[3]+b2).astype(BF)
                return 0
            for part in range(4):
                lax.fori_loop(2*part,2*part+2,head,0)
                point()
            oc.wait()
        def bigger(cot_,stage_):
            nonlocal cot_own,stage
            cot_own=cot_; stage=stage_
            cl=pltpu.make_async_copy(cot,cot_,lsem.at[7]); cl.start(); cl.wait()
            pl.run_scoped(attention_part,pltpu.VMEM((BLK,d),BF),pltpu.VMEM((d,d),BF),pltpu.VMEM((BLK,3*d),BF),pltpu.VMEM((CTX,2*d),BF),pltpu.VMEM((2,BLK,BLK+CTX),BF),pltpu.VMEM((BLK,d),BF),pltpu.VMEM((BLK,d),BF))
        cot_own=stage=None
        pl.run_scoped(bigger,pltpu.VMEM((BLK,d),BF),pltpu.VMEM((BLK,d),BF))
        def conv_part(w,dn,sig,u3,g3,y3,G,rate3,dec3,sp3,d0,d1,xv,tl,ggrad1,sm):
            loads=[pltpu.make_async_copy(w_in,w,lsem.at[0]),pltpu.make_async_copy(x,xv,lsem.at[1]),pltpu.make_async_copy(tail_low,tl,lsem.at[2])]
            for v in loads: v.start()
            def g1(): send_half(1,lambda r: mm(lowv[:,r],dq[...],TN),1)
            def g2(): send_half(2,lambda r: mm(lowv[:,r],dk[...],TN)+mm(ctxv[:,r],dck[...],TN),0)
            def g3_(): send_half(3,lambda r: mm(lowv[:,r],dv[...],TN)+mm(ctxv[:,r],dcv[...],TN),1)
            g1(); point(); g2(); join_half(1); point(); g3_(); join_half(2); point()
            for v in loads: v.wait()
            G[...]=(mm(dck[...],w[:,d:2*d],NT)+mm(dcv[...],w[:,2*d:],NT)).astype(BF)
            join_half(3); point()
            rate3[...]=rates(decay3[...],length)
            dec3[...]=jnp.exp(-float(BLK)*rate3[...])
            split_lanes(G,g3,CTX)
            a=lambda k: jnp.exp(-rate3[k]); kk=lambda k: weight3[k]*jnp.sqrt(rate3[k])
            av=[a(k) for k in range(nst)]; kv=[kk(k) for k in range(nst)]
            def back(i,gs):
                t=CTX-1-i; v=g3[t]
                gs=tuple(p*z+v for p,z in zip(av,gs))
                y3[t]=tree(p*z for p,z in zip(kv,gs))
                return gs
            gs=lax.fori_loop(0,CTX,back,tuple(jnp.zeros((8,128),F32) for _ in range(nst)),unroll=2)
            for k in range(nst): s3[k]=gs[k]
            ex=Scan(ns,nst,s3,gather,spread,hb,[e0,e1,e2,e3],False)
            ex.collect()
            point()
            split_lanes(tl,u3,CTX)
            up=lax.broadcasted_iota(jnp.int32,(8,128),0).astype(F32)
            for lt in range(d//128):
                ls=slice(lt*128,(lt+1)*128)
                for part in range(0,nst,8):
                    r=[jnp.broadcast_to(rate3[k,lt:lt+1,:],(8,128)) for k in range(part,part+8)]
                    a8=[jnp.exp(-8.0*v) for v in r]
                    def body(i,cr):
                        acc,der=cr
                        u=lowv[pl.ds(pl.multiple_of(i*16,16),16),ls].astype(F32)
                        for w_ in (u[:8],u[8:]):
                            der=tuple(p*(z+y) for p,z,y in zip(a8,der,acc))
                            acc=tuple(p*y+w_ for p,y in zip(a8,acc))
                        return acc,der
                    zz=tuple(jnp.zeros((8,128),F32) for _ in range(8))
                    acc,der=lax.fori_loop(0,(BLK-CTX)//16,body,(zz,zz))
                    for i,k in enumerate(range(part,part+8)):
                        j=7.0-up
                        sp3[k,lt:lt+1,:]=jnp.sum(jnp.exp(-j*r[i])*(8.0*der[i]+j*acc[i]),axis=0,keepdims=True)
                if lt==2: ex.scan(dec3)
                if lt%2==1: point()
            for part in range(0,nst,4):
                zz=tuple(jnp.zeros((8,128),F32) for _ in range(4))
                aa=[a(k) for k in range(part,part+4)]
                def fwd(t,cr):
                    h,hp,q0,q1=cr
                    u=u3[t]; gg=g3[t]
                    hp=tuple(p*(z+y) for p,z,y in zip(aa,hp,h))
                    h=tuple(p*z+u for p,z in zip(aa,h))
                    return h,hp,tuple(z+gg*y for z,y in zip(q0,h)),tuple(z+gg*y for z,y in zip(q1,hp))
                h,hp,q0,q1=lax.fori_loop(0,CTX,fwd,(tuple(h3[k] for k in range(part,part+4)),zz,zz,zz),unroll=2)
                for i,k in enumerate(range(part,part+4)):
                    d0[k]=q0[i]; d1[k]=q1[i]
                    m=float(BLK-CTX); am=jnp.exp(-m*rate3[k])
                    sp3[k]=aa[i]*(am*hp[i]+m*am*h[i]+sp3[k])
                point()
            ex.receive()
            for lt in range(d//128):
                ls=slice(lt*128,(lt+1)*128)
                r=[jnp.broadcast_to(rate3[k,lt:lt+1,:],(8,128)) for k in range(nst)]
                a8=[jnp.exp(-8.0*z) for z in r]
                v=tuple(jnp.broadcast_to((weight3[k,lt:lt+1,:]*jnp.sqrt(rate3[k,lt:lt+1,:]))*hb[k,lt:lt+1,:],(8,128))*jnp.exp(-(8.0-up)*r[k]) for k in range(nst))
                def two(v):
                    b=tree(v); v=tuple(p*z for p,z in zip(a8,v))
                    t=tree(v); v=tuple(p*z for p,z in zip(a8,v))
                    return jnp.concatenate([t,b],axis=0),v
                def ownrows(i,v):
                    tb,v=two(v)
                    sig[pl.ds(pl.multiple_of(BLK-CTX-16-i*16,16),16),ls]=tb.astype(BF)
                    return v
                v=lax.fori_loop(0,(BLK-CTX)//16,ownrows,v)
                def tailrows(i,v):
                    tb,v=two(v)
                    row=pl.multiple_of(CTX-16-i*16,16)
                    tailb[pl.ds(row,16),ls]=(tb+y3[pl.ds(row,16),lt,:]).astype(BF)
                    return v
                lax.fori_loop(0,CTX//16,tailrows,v)
                point()
            bc=pltpu.make_async_remote_copy(src_ref=tailb,dst_ref=tail_in,send_sem=tsem.at[0],recv_sem=tsem.at[1],device_id={"seq":jnp.maximum(q-1,0)},device_id_type=MESH)
            @pl.when(q>0)
            def _(): bc.start()
            def dnr(r):
                rr=slice(r*256,(r+1)*256)
                dn[rr,:]=mm(dq[rr,:],w[:,:d],NT)+mm(dk[rr,:],w[:,d:2*d],NT)+mm(dv[rr,:],w[:,2*d:],NT)
            dnr(0); point(); dnr(1); point()
            ggrad1[...]=jnp.zeros_like(ggrad1)
            def lastrows(i,_):
                rr=pl.ds(pl.multiple_of(i*64,64),64)
                dvv,gg=norm_back(xv[rr,:].astype(F32),gain1[...],dn[rr,:]+sig[rr,:].astype(F32))
                res[rr,:]=res[rr,:]+dvv
                ggrad1[...]+=fold(gg)
                return 0
            lax.fori_loop(0,(BLK-CTX)//64,lastrows,0)
            point()
            @pl.when(q==ns-1)
            def _(): tail_in[...]=jnp.zeros_like(tail_in)
            @pl.when(q<ns-1)
            def _(): bc.wait_recv()
            sig[BLK-CTX:,:]=tail_in[...]
            lax.fori_loop((BLK-CTX)//64,BLK//64,lastrows,0)
            ic=pltpu.make_async_copy(res,igrad,outsem.at[1]); ic.start()
            sm[...]=jnp.zeros_like(sm)
            for k in range(nst):
                r=rate3[k]; D1=d1[k]+hb[k]*sp3[k]; sq=jnp.sqrt(r)
                kw=sq*d0[k]; kd=weight3[k]*sq*(0.5*d0[k]-r*D1)
                for lt in range(d//128):
                    sm[k:k+1,lt*128:(lt+1)*128]=kw[lt:lt+1,:]; sm[nst+k:nst+k+1,lt*128:(lt+1)*128]=kd[lt:lt+1,:]
            sm[2*nst:2*nst+1,:]=jnp.sum(ggrad1[...],axis=0,keepdims=True)
            sm[2*nst+1:2*nst+2,:]=jnp.sum(ggrad2[...],axis=0,keepdims=True)
            for j in range(d//128):
                v=jnp.transpose(sm[:,j*128:(j+1)*128]).astype(BF)
                for b in range(128//rc):
                    e=j*(128//rc)+b
                    small[e//2//ny,e//2%ny,e%2,:,0:128]=v[b*rc:(b+1)*rc]
                    small[e//2//ny,e//2%ny,e%2,:,128:]=jnp.zeros((rc,small.shape[4]-128),BF)
            def scopy(): return pltpu.make_async_remote_copy(src_ref=small.at[:,:,1-c],dst_ref=small_rec,send_sem=csem.at[0,4],recv_sem=csem.at[1,4],device_id=sib,device_id_type=MESH)
            scopy().start()
            def join_small():
                scopy().wait_recv()
                for z in range(nz):
                    for y in range(ny):
                        small_rec[z,y]=(small_rec[z,y].astype(F32)+small[z,y,c].astype(F32)).astype(BF)
                launch("S",0)
            point()
            join_small()
            ic.wait(); scopy().wait_send(); ex.drain()
            @pl.when(q>0)
            def _(): bc.wait_send()
        M=pltpu.VMEM; st=(nst,8,128)
        pl.run_scoped(conv_part,M((d,3*d),BF),M((BLK,d),F32),M((BLK,d),BF),M((CTX,8,128),F32),M((CTX,8,128),F32),M((CTX,8,128),F32),M((CTX,d),BF),M(st,F32),M(st,F32),M(st,F32),M(st,F32),M(st,F32),M((BLK,d),BF),M((CTX,d),BF),M((8,d),F32),M((128,d),F32))
    M=pltpu.VMEM
    pl.run_scoped(rest,M((BLK,d),F32),M((BLK,d),BF),M((BLK,d),BF),M((BLK,d),BF),M((CTX,d),BF),M((CTX,d),BF),M((BLK,d),BF),M((CTX,d),BF),M((8,d),F32))
    point()
    assert at[0]==len(due)
    for v in bcopies: bcopy(*v).wait()
    for v in lanes: v.drain()
    for k in (2,3): ccopy(k).wait_send()

def main(n, ns, low2,cot,cots,w1,w2,residual,gain2,attended,wo,packed,pairs,probs,low,tail_low,ctx,w_in,x,gain1,decay3,weight3,h3):
    d=x.shape[1]; ff=w1.shape[1]; nz,ny,nx=n["z"],n["y"],n["x"]; nzy=nz*ny; own=ff//2; rf=own//nzy; rb=d//nzy; rc=d//ns; nst=decay3.shape[0]
    J=max(1,rf//128); rj=rf//J
    packed_w=rj%128!=0
    if packed_w:
        c=lax.rem(lax.axis_index("seq"),2)
        w1=lax.dynamic_index_in_dim(w1.reshape(d,nzy,2,rf),c,2,keepdims=False).reshape(d,own)
        w2=lax.dynamic_index_in_dim(w2.reshape(nzy,2,rf,d),c,1,keepdims=False).reshape(own,d)
    plan=plan_of(n,rf,rb,rc,d,own)
    V=pl.BlockSpec(memory_space=pltpu.VMEM); Y=pl.BlockSpec(memory_space=pl.ANY); M=pltpu.VMEM; D=pltpu.SemaphoreType.DMA
    wd=rj if not packed_w else 512
    scr=[M((2*BLK,d),BF),M((2*BLK,d),BF),M((nz,ny,rf,d),BF),M((nz,ny,rb,own),BF),M((2,nz,ny,2,rc,d),BF),M((4,nz,ny,rc,d),BF),M((BLK,d),BF),M((BLK,d),BF),
         M((rb,own),BF),M((nz,ny,2,rc,128*nx),BF),M((nz,ny,rc,128*nx),BF),M((CTX,d),BF),M((CTX,d),BF),
         D((own//wd,)),D((own//wd,)),D((8,)),D((2,)),D((2,)),D((2,)),D((2,5)),D((2,8)),D((2,)),D((2,)),D((2,))]
    sc=scan_scratch(ns,nst)
    scr+=[sc[0],sc[1],sc[2],M((nst,8,128),F32)]+sc[3:]
    for (t,k,r0,r,c0,cw,o) in plan: scr+=lane_scratch(n,o,r,cw)
    ins=[low2,cot,cots,w1,w2,residual,gain2,attended,wo,packed,pairs,probs,low,tail_low,ctx,w_in,x,gain1,decay3,weight3,h3]
    small_in={6,17,18,19,20}
    return pl.pallas_call(functools.partial(main_kernel,n,ns,BLK*ns,plan,packed_w),
        out_shape=[S(BLK,d),S(BLK,d,t=F32),S(rf,d),S(rc,own),S(rc,own),S(rc,4*d),S(rc,128*nx)],
        in_specs=[V if i in small_in else Y for i in range(len(ins))],out_specs=[Y,Y]+[V]*5,scratch_shapes=scr,
        compiler_params=pltpu.CompilerParams(collective_id=1,has_side_effects=True,vmem_limit_bytes=63*10**6),
        cost_estimate=pl.CostEstimate(flops=45*10**9,bytes_accessed=6*10**7,transcendentals=2*10**6),name="main")(*ins)


def closing_kernel(n, out0, igrad0, OA, OBk, OBr, OC, OS, out, igrad, g1, qkv, kw, kd, ao, g2, eg, ra):
    c=lax.rem(lax.axis_index("seq"),2)
    igrad[...]=igrad0[...]; out[...]=out0[...]
    d=OA.shape[1]; nst=kw.shape[0]
    ra[...]=OA[...].astype(F32)
    ao[...]=OC[:,:d].astype(F32)
    qkv[...]=OC[:,d:].astype(F32)
    s=OS[:,:128].astype(F32)
    t=jnp.transpose(s)
    kw[...]=t[:nst,:]; kd[...]=t[nst:2*nst,:]
    g1[...]=t[2*nst:2*nst+1,:]; g2[...]=t[2*nst+1:2*nst+2,:]
    nzy=n["z"]*n["y"]; rf=OBk.shape[1]//nzy; J=max(1,rf//128); rj=rf//J
    if rj%128==0:
        for j in range(J):
            for b in range(nzy):
                o=slice((j*nzy+b)*rj,(j*nzy+b+1)*rj)
                eg[:,pl.ds(pl.multiple_of((2*b+c)*rf+j*rj,128),rj)]=OBk[:,o].astype(F32)
                eg[:,pl.ds(pl.multiple_of((2*b+1-c)*rf+j*rj,128),rj)]=OBr[:,o].astype(F32)

def closing(n, out, igrad, OA, OBk, OBr, OC, OS, nst):
    V=pl.BlockSpec(memory_space=pltpu.VMEM); d=OA.shape[1]; rc=OC.shape[0]
    nzy=n["z"]*n["y"]; rf=OBk.shape[1]//nzy; J=max(1,rf//128); rj=rf//J
    res=list(pl.pallas_call(functools.partial(closing_kernel,n),
      out_shape=[S(*out.shape),S(*igrad.shape,t=F32),S(1,rc,t=F32),S(rc,3*d,t=F32),S(nst,rc,t=F32),S(nst,rc,t=F32),S(rc,d,t=F32),S(1,rc,t=F32),S(rc,2*OBk.shape[1],t=F32),S(*OA.shape,t=F32)],
      in_specs=[V]*7,out_specs=[V]*10,
      compiler_params=pltpu.CompilerParams(vmem_limit_bytes=63*10**6),name="closing")(out,igrad,OA,OBk,OBr,OC,OS))
    if rj%128:
        c=lax.rem(lax.axis_index("seq"),2)
        keep=OBk.reshape(rc,J,nzy,rj); other=OBr.reshape(rc,J,nzy,rj)
        e=jnp.stack([jnp.where(c==0,keep,other),jnp.where(c==0,other,keep)],3)
        res[8]=e.transpose(0,2,3,1,4).reshape(rc,2*OBk.shape[1]).astype(F32)
    res[0]=res[0][None]; res[1]=res[1][None]; res[4]=res[4].T; res[5]=res[5].T; res[2]=res[2].reshape(rc); res[7]=res[7].reshape(rc)
    return tuple(res)

def local(layer_input,segment_ids,context_mask,first_gain,attention_in,kernel_weight,kernel_decay,attention_out,second_gain,expand_weight,reduce_weight,cotangent):
    ns=lax.axis_size("seq"); nx=lax.axis_size("grp"); nst=kernel_decay.shape[1]; n=sizes(nx,ns)
    x=layer_input[0]; cot=cotangent[0]
    low,tail_low,packed,ctx,pairs,h3,decay3,weight3,cot_sib=front(ns,x,cot,first_gain[None],kernel_decay.T,kernel_weight.T,attention_in)
    probs,attended,residual,low2=attention(packed,pairs,segment_ids,context_mask[0],x,attention_out,second_gain[None])
    got=main(n,ns,low2,cot,cot_sib,expand_weight,reduce_weight,residual,second_gain[None],attended,attention_out,packed,pairs,probs,low,tail_low,ctx,attention_in,x,first_gain[None],decay3,weight3,h3)
    return closing(n,*got,nst)

def solution(mesh):
    ins=(P("grp","seq",None),P("grp","seq"),P("grp","seq",None))+(P(),)*8+(P("grp","seq",None),)
    outs=(P("grp","seq",None),)*2+(P("seq"),)+(P("seq",None),)*4+(P("seq"),)+(P("seq",None),)*2
    return jax.shard_map(local,mesh=mesh,in_specs=ins,out_specs=outs,check_vma=False)
```

```python
import functools
import heapq
import itertools
import math

import jax
import jax.numpy as jnp
from jax import lax
from jax.experimental import pallas as pl
from jax.experimental.pallas import tpu as pltpu
from jax.sharding import PartitionSpec as P

MESH=pl.DeviceIdType.MESH
BF=jnp.bfloat16

def sizes(nx, ns):
    ny = nx if ns % (2*nx)==0 else 1
    return {"x":nx,"y":ny,"z":ns//(2*ny)}

class Place:
    def __init__(s, n):
        s.n=n; q=lax.axis_index("seq")
        s.i=dict(x=lax.axis_index("grp"), y=lax.rem(lax.div(q,2),n["y"]), z=lax.div(q,2*n["y"])); s.c=lax.rem(q,2)
        s.to={}; s.ids={}
        for ax in "xyz":
            for k in range(1,n[ax]):
                v=s.i[ax]+k; s.to[ax,k]=jnp.where(v>=n[ax],v-n[ax],v)
                j=dict(s.i); j[ax]=s.to[ax,k]
                s.ids[ax,k]={"grp":j["x"],"seq":(j["z"]*n["y"]+j["y"])*2+s.c}
        s.other={"grp":s.i["x"],"seq":q+1-2*s.c}
    def at(s, ax, k): return s.to[ax,k]
    def device(s, ax, k): return s.ids[ax,k]
    def sibling(s): return s.other

def stage_shapes(n, order, rows, cw):
    left=dict(n); out=[]
    for ax in order:
        del left[ax]
        out.append(tuple(left[a] for a in "zy" if a in left)+(rows, cw*(left["x"] if "x" in left else 1)))
    return out


EPS=1e-5
BLK=512; CTX=128; HEADS=8; HD=128
F32=jnp.float32

def norm_rows(src, gain, dst, rows, step=64):
    def body(i,_):
        rr=pl.ds(pl.multiple_of(i*step,16),step)
        x=src[rr,:].astype(F32)
        x=x-jnp.mean(x,axis=-1,keepdims=True)
        v=jnp.mean(x*x,axis=-1,keepdims=True)
        dst[rr,:]=(x*lax.rsqrt(v+EPS)*gain).astype(BF)
        return 0
    lax.fori_loop(0,rows//step,body,0)

def rates(decay, length):
    return jnp.exp(decay)*(1.0/length)

def block_state(low, rate3, row0, rows, put):
    nst=rate3.shape[0]
    back=7.0-lax.broadcasted_iota(jnp.int32,(8,128),0).astype(F32)
    for lt in range(low.shape[1]//128):
        lanes=pl.ds(lt*128,128)
        r=[jnp.broadcast_to(rate3[n,lt:lt+1,:],(8,128)) for n in range(nst)]
        a8=[jnp.exp(-8.0*v) for v in r]
        def body(g,acc):
            u=low[pl.ds(pl.multiple_of(row0+g*16,16),16),lanes].astype(F32)
            lo,hi=u[:8],u[8:]
            acc=tuple(a*c+lo for a,c in zip(a8,acc))
            return tuple(a*c+hi for a,c in zip(a8,acc))
        acc=lax.fori_loop(0,rows//16,body,tuple(jnp.zeros((8,128),F32) for _ in range(nst)),unroll=2)
        for n in range(nst):
            put(n,lt,jnp.sum(acc[n]*jnp.exp(-back*r[n]),axis=0,keepdims=True))

def split_lanes(src, dst, rows):
    def body(g,_):
        for lt in range(src.shape[1]//128):
            v=src[pl.ds(pl.multiple_of(g*16,16),16),lt*128:(lt+1)*128].astype(F32)
            dst[pl.ds(g*16,16),lt,:]=v
        return 0
    lax.fori_loop(0,rows//16,body,0)

def join_lanes(src, dst, rows):
    def body(g,_):
        for lt in range(dst.shape[1]//128):
            dst[pl.ds(pl.multiple_of(g*16,16),16),lt*128:(lt+1)*128]=src[pl.ds(g*16,16),lt,:].astype(dst.dtype)
        return 0
    lax.fori_loop(0,rows//16,body,0)

class Scan:
    def __init__(s, ns, nst, s3, gather, spread, h3, sem, forward):
        s.ns,s.nst,s.s3,s.gather,s.spread,s.h3=ns,nst,s3,gather,spread,h3
        s.sem=sem; s.forward=forward; s.q=lax.axis_index("seq"); s.stride=ns//nst
        s.n=lax.div(s.q,s.stride); s.scans=lax.rem(s.q,s.stride)==0
    def to_scanner(s, n):
        return pltpu.make_async_remote_copy(src_ref=s.s3.at[n],dst_ref=s.gather.at[s.q],send_sem=s.sem[0].at[n],recv_sem=s.sem[1].at[s.q],device_id={"seq":n*s.stride},device_id_type=MESH)
    def from_block(s, b):
        return pltpu.make_async_remote_copy(src_ref=s.s3.at[0],dst_ref=s.gather.at[b],send_sem=s.sem[0].at[0],recv_sem=s.sem[1].at[b],device_id={"seq":b},device_id_type=MESH)
    def to_block(s, b):
        return pltpu.make_async_remote_copy(src_ref=s.spread.at[b],dst_ref=s.h3.at[s.n],send_sem=s.sem[2].at[b],recv_sem=s.sem[3].at[s.n],device_id={"seq":b},device_id_type=MESH)
    def from_scanner(s, n):
        return pltpu.make_async_remote_copy(src_ref=s.spread.at[0],dst_ref=s.h3.at[n],send_sem=s.sem[2].at[0],recv_sem=s.sem[3].at[n],device_id={"seq":n*s.stride},device_id_type=MESH)
    def each(s, count, fn, skip):
        def body(i,_):
            @pl.when(i!=skip)
            def _(): fn(i)
            return 0
        lax.fori_loop(0,count,body,0)
    def collect(s):
        mine=jnp.where(s.scans,s.n,s.nst)
        s.each(s.nst,lambda n:s.to_scanner(n).start(),mine)
    def scan(s, decay_block):
        mine=jnp.where(s.scans,s.n,s.nst)
        @pl.when(s.scans)
        def _():
            s.gather[s.q]=s.s3[s.n]
            s.each(s.ns,lambda b:s.from_block(b).wait_recv(),s.q)
            a=decay_block[s.n]
            def body(i,h):
                b=i if s.forward else s.ns-1-i
                s.spread[b]=h
                return a*h+s.gather[b]
            lax.fori_loop(0,s.ns,body,jnp.zeros((8,128),F32))
            s.each(s.ns,lambda b:s.to_block(b).start(),s.q)
            s.h3[s.n]=s.spread[s.q]
    def receive(s):
        mine=jnp.where(s.scans,s.n,s.nst)
        s.each(s.nst,lambda n:s.from_scanner(n).wait_recv(),mine)
    def drain(s):
        mine=jnp.where(s.scans,s.n,s.nst)
        s.each(s.nst,lambda n:s.to_scanner(n).wait_send(),mine)
        @pl.when(s.scans)
        def _(): s.each(s.ns,lambda b:s.to_block(b).wait_send(),s.q)

def scan_scratch(ns,nst):
    return [pltpu.VMEM((nst,8,128),F32),pltpu.VMEM((ns,8,128),F32),pltpu.VMEM((ns,8,128),F32),
      pltpu.SemaphoreType.DMA((nst,)),pltpu.SemaphoreType.DMA((ns,)),pltpu.SemaphoreType.DMA((ns,)),pltpu.SemaphoreType.DMA((nst,))]

def front_kernel(ns, length, x, cot, gain, decay, weight, w_hbm, low_out, tail_low, packed_out, ctx, pairs, h3, decay3, weight3, cot_sib,
                 low, packed, osem, w, own3, tail_x, rate3, dec3, u3, y3, s3, gather, spread, e0, e1, e2, e3, wsem, tsem, csem):
    q=lax.axis_index("seq"); c=lax.rem(q,2); g=lax.axis_index("grp")
    nst=decay.shape[0]
    sem=pltpu.get_barrier_semaphore()
    def sig(i,_):
        @pl.when(i!=q)
        def _(): pl.semaphore_signal(sem,inc=1,device_id={"seq":i},device_id_type=MESH)
        return 0
    lax.fori_loop(0,ns,sig,0)
    wcp=pltpu.make_async_copy(w_hbm,w,wsem); wcp.start()
    pl.semaphore_wait(sem,ns-1)
    tail=pltpu.make_async_remote_copy(src_ref=x.at[pl.ds(BLK-CTX,CTX),:],dst_ref=tail_x,send_sem=tsem.at[0],recv_sem=tsem.at[1],device_id={"seq":jnp.minimum(q+1,ns-1)},device_id_type=MESH)
    @pl.when(q<ns-1)
    def _(): tail.start()
    cc=pltpu.make_async_remote_copy(src_ref=cot,dst_ref=cot_sib,send_sem=csem.at[0],recv_sem=csem.at[1],device_id={"seq":q+1-2*c},device_id_type=MESH)
    cc.start()
    for lt in range(low.shape[1]//128):
        rows=slice(lt*128,(lt+1)*128)
        decay3[:,lt,:]=decay[:,rows]; weight3[:,lt,:]=weight[:,rows]
    rate3[...]=rates(decay3[...],length)
    dec3[...]=jnp.exp(-float(BLK)*rate3[...])
    norm_rows(x,gain[...],low,BLK)
    lc=pltpu.make_async_copy(low,low_out,osem.at[0]); lc.start()
    def put_own(n,lt,v): own3[n,lt:lt+1,:]=v
    block_state(low,rate3,0,BLK-CTX,put_own)
    wcp.wait()
    half=packed.shape[1]//2
    packed[:,:half]=jnp.dot(low[...],w[:,:half],preferred_element_type=F32).astype(BF)
    pc=pltpu.make_async_copy(packed.at[:,pl.ds(0,half)],packed_out.at[:,pl.ds(0,half)],osem.at[1]); pc.start()
    @pl.when(q>0)
    def _(): tail.wait_recv()
    @pl.when(q==0)
    def _(): tail_x[...]=jnp.zeros_like(tail_x)
    norm_rows(tail_x,gain[...],tail_low,CTX)
    def put_tail(n,lt,v): s3[n,lt:lt+1,:]=v
    block_state(tail_low,rate3,0,CTX,put_tail)
    for n in range(nst):
        s3[n]=jnp.exp(-float(BLK-CTX)*rate3[n])*s3[n]+own3[n]
    ex=Scan(ns,nst,s3,gather,spread,h3,[e0,e1,e2,e3],True)
    ex.collect()
    split_lanes(tail_low,u3,CTX)
    packed[:,half:2*half-half//3]=jnp.dot(low[...],w[:,half:2*half-half//3],preferred_element_type=F32).astype(BF)
    ex.scan(dec3)
    packed[:,2*half-half//3:]=jnp.dot(low[...],w[:,2*half-half//3:],preferred_element_type=F32).astype(BF)
    pd=pltpu.make_async_copy(packed.at[:,pl.ds(half,half)],packed_out.at[:,pl.ds(half,half)],osem.at[2]); pd.start()
    ex.receive()
    a=[jnp.exp(-rate3[n]) for n in range(nst)]
    k=[weight3[n]*jnp.sqrt(rate3[n]) for n in range(nst)]
    def step(t,h):
        u=u3[t]
        h=tuple(p*v+u for p,v in zip(a,h))
        ys=[p*v for p,v in zip(k,h)]
        while len(ys)>1: ys=[ys[i]+ys[i+1] if i+1<len(ys) else ys[i] for i in range(0,len(ys),2)]
        y3[t]=ys[0]
        return h
    lax.fori_loop(0,CTX,step,tuple(h3[n] for n in range(nst)),unroll=2)
    join_lanes(y3,ctx,CTX)
    d=low.shape[1]
    pairs[...]=jnp.dot(ctx[...],w[:,d:],preferred_element_type=F32).astype(BF)
    ex.drain()
    @pl.when(q<ns-1)
    def _(): tail.wait_send()
    cc.wait(); lc.wait(); pc.wait(); pd.wait()

def front(ns, x, cot, gain, decay, weight, w):
    nst=decay.shape[0]; d=x.shape[1]
    V=pl.BlockSpec(memory_space=pltpu.VMEM); A=pl.BlockSpec(memory_space=pl.ANY)
    S=lambda *s,t=BF: jax.ShapeDtypeStruct(s,t)
    return pl.pallas_call(functools.partial(front_kernel,ns,x.shape[0]*ns),
        out_shape=[S(BLK,d),S(CTX,d),S(BLK,3*d),S(CTX,d),S(CTX,2*d),S(nst,8,128,t=F32),S(nst,8,128,t=F32),S(nst,8,128,t=F32),S(BLK,d)],
        in_specs=[V,A,V,V,V,A],out_specs=[A,V,A]+[V]*5+[A],
        scratch_shapes=[pltpu.VMEM((BLK,d),BF),pltpu.VMEM((BLK,3*d),BF),pltpu.SemaphoreType.DMA((3,)),pltpu.VMEM((d,3*d),BF),pltpu.VMEM((nst,8,128),F32),pltpu.VMEM((CTX,d),BF),pltpu.VMEM((nst,8,128),F32),pltpu.VMEM((nst,8,128),F32),
          pltpu.VMEM((CTX,8,128),F32),pltpu.VMEM((CTX,8,128),F32)]+scan_scratch(ns,nst)+[pltpu.SemaphoreType.DMA,pltpu.SemaphoreType.DMA((2,)),pltpu.SemaphoreType.DMA((2,))],
        compiler_params=pltpu.CompilerParams(collective_id=0,has_side_effects=True,vmem_limit_bytes=63*10**6),
        name="front")(x,cot,gain,decay,weight,w)

NEG=-1e30
NT=(((1,),(1,)),((),()))
TN=(((0,),(0,)),((),()))
NN=(((1,),(0,)),((),()))
def mm(a,b,dims=NN): return lax.dot_general(a,b,dims,preferred_element_type=F32)

def attention_kernel(q,k,v,ck,cv,seg,vis,x,wo,gain,probs,attended,residual,low2,bias):
    h=pl.program_id(0)
    @pl.when(h==0)
    def _():
        row=jnp.broadcast_to(seg[...].astype(F32),(128,BLK))
        col=jnp.transpose(row)
        for i in range(BLK//128):
            ci=col[i*128:(i+1)*128]
            for j in range(BLK//128):
                if j>i:
                    bias[i*128:(i+1)*128,j*128:(j+1)*128]=jnp.full((128,128),NEG,F32); continue
                ok=ci==row[:,j*128:(j+1)*128]
                if i==j: ok=ok&(lax.broadcasted_iota(jnp.int32,(128,128),0)>=lax.broadcasted_iota(jnp.int32,(128,128),1))
                bias[i*128:(i+1)*128,j*128:(j+1)*128]=jnp.where(ok,0.0,NEG)
        seen=jnp.where((vis[...]==1)&(lax.axis_index("seq")>0),0.0,NEG)
        bias[:,BLK:]=jnp.broadcast_to(seen,(BLK,CTX))
    scale=1.0/math.sqrt(HD)
    half=BLK//2
    for r in range(2):
        rows=slice(r*half,(r+1)*half); n=(r+1)*half
        s1=mm(q[rows,:],k[:n,:],NT)*scale+bias[rows,:n]
        s2=mm(q[rows,:],ck[...],NT)*scale+bias[rows,BLK:]
        top=jnp.maximum(jnp.max(s1,axis=-1,keepdims=True),jnp.max(s2,axis=-1,keepdims=True))
        e1=jnp.exp(s1-top); e2=jnp.exp(s2-top)
        inv=1.0/(jnp.sum(e1,axis=-1,keepdims=True)+jnp.sum(e2,axis=-1,keepdims=True))
        p1=(e1*inv).astype(BF); p2=(e2*inv).astype(BF)
        probs[0,rows,:n]=p1; probs[0,rows,BLK:]=p2
        if n<BLK: probs[0,rows,n:BLK]=jnp.zeros((half,BLK-n),BF)
        o=mm(p1,v[:n,:])+mm(p2,cv[...])
        attended[rows,pl.ds(pl.multiple_of(h*HD,HD),HD)]=o.astype(BF)
    @pl.when(h==HEADS-1)
    def _():
        def body(i,_):
            rr=pl.ds(pl.multiple_of(i*128,128),128)
            res=x[rr,:].astype(F32)+mm(attended[rr,:],wo[...])
            residual[rr,:]=res
            m=res-jnp.mean(res,axis=-1,keepdims=True)
            var=jnp.mean(m*m,axis=-1,keepdims=True)
            low2[rr,:]=(m*lax.rsqrt(var+EPS)*gain[...]).astype(BF)
            return 0
        lax.fori_loop(0,BLK//128,body,0)

def attention(packed,pairs,seg,vis,x,wo,gain):
    d=x.shape[1]
    S=lambda *s,t=BF: jax.ShapeDtypeStruct(s,t)
    full=lambda a: pl.BlockSpec(a.shape,lambda h:(0,)*a.ndim)
    return pl.pallas_call(attention_kernel,grid=(HEADS,),
      in_specs=[pl.BlockSpec((BLK,HD),lambda h:(0,h)),pl.BlockSpec((BLK,HD),lambda h:(0,HEADS+h)),pl.BlockSpec((BLK,HD),lambda h:(0,2*HEADS+h)),
        pl.BlockSpec((CTX,HD),lambda h:(0,h)),pl.BlockSpec((CTX,HD),lambda h:(0,HEADS+h)),full(seg),full(vis),full(x),full(wo),full(gain)],
      out_specs=[pl.BlockSpec((1,BLK,BLK+CTX),lambda h:(h,0,0)),pl.BlockSpec((BLK,d),lambda h:(0,0)),pl.BlockSpec((BLK,d),lambda h:(0,0)),pl.BlockSpec((BLK,d),lambda h:(0,0))],
      out_shape=[S(HEADS,BLK,BLK+CTX),S(BLK,d),S(BLK,d,t=F32),S(BLK,d)],
      scratch_shapes=[pltpu.VMEM((BLK,BLK+CTX),F32)],
      compiler_params=pltpu.CompilerParams(vmem_limit_bytes=63*10**6),
      cost_estimate=pl.CostEstimate(flops=4*10**9,bytes_accessed=2*10**7,transcendentals=3*10**6),
      name="attention")(packed,packed,packed,pairs,pairs,seg,vis,x,wo,gain)

G0=math.sqrt(2/math.pi); G1=0.044715
def gelu_pair(h):
    h2=h*h
    th=jnp.tanh(h*(G0+G0*G1*h2))
    p=0.5*(1.0+th)
    return h*p, p+h*(0.5*(1.0-th*th))*(G0+3*G0*G1*h2)


def norm_back(v, gain, dy):
    x=v-jnp.mean(v,axis=-1,keepdims=True)
    s=lax.rsqrt(jnp.mean(x*x,axis=-1,keepdims=True)+EPS)
    nrm=x*s
    dn=dy*gain
    dv=(dn-jnp.mean(dn,axis=-1,keepdims=True)-nrm*jnp.mean(dn*nrm,axis=-1,keepdims=True))*s
    return dv, dy*nrm
def fold(v):
    return jnp.sum(v.reshape(v.shape[0]//8,8,v.shape[1]),axis=0)


def S(*s,t=BF): return jax.ShapeDtypeStruct(s,t)


class Lane:
    def __init__(s, place, order, rows, cw, src, out, scratch):
        s.p,s.order,s.rows,s.cw,s.src,s.out=place,order,rows,cw,src,out
        s.recv=scratch[:3]; s.ss,s.rs=scratch[3],scratch[4]
        s.begun=[]
        s.mine=pl.ds(pl.multiple_of(place.i["x"]*cw,128),cw)
    def held(s, stage, fixed):
        if stage==0: return s.src(fixed)
        left=[a for a in "zyx" if a not in s.order[:stage]]
        cols=slice(None)
        if "x" in fixed and "x" in left: cols=pl.ds(pl.multiple_of(fixed["x"]*s.cw,128),s.cw)
        return s.recv[stage-1].at[(0,)+tuple(fixed.get(a,slice(None)) for a in "zy" if a in left)+(slice(None),cols)]
    def copy(s, stage, k):
        ax="x" if stage==3 else s.order[stage]
        if stage==3: src=s.out.at[:,s.mine]; dst=s.out.at[:,s.mine]
        else: src=s.held(stage,{ax:s.p.at(ax,k)}); dst=s.recv[stage].at[k-1]
        return pltpu.make_async_remote_copy(src_ref=src,dst_ref=dst,send_sem=s.ss.at[stage,k-1],recv_sem=s.rs.at[stage,k-1],device_id=s.p.device(ax,k),device_id_type=MESH)
    def start(s, stage):
        for k in range(1,s.p.n["x" if stage==3 else s.order[stage]]):
            s.copy(stage,k).start(); s.begun.append((stage,k))
    def drain(s):
        for stage,k in s.begun: s.copy(stage,k).wait_send()
    def finish(s, stage):
        for st,k in s.begun:
            if st==stage: s.copy(st,k).wait_recv()
        if stage==3: return
        ax=s.order[stage]; n=s.p.n
        left=[a for a in "zy" if a not in s.order[:stage+1]]
        R=s.recv[stage]; step=min(s.rows,32)
        for lead in itertools.product(*[range(n[a]) for a in left]):
            fixed=dict(zip(left,lead)); fixed[ax]=s.p.i[ax]
            own=s.held(stage,fixed)
            def body(r,_):
                rr=pl.ds(pl.multiple_of(r*step,16),step)
                v=own[rr,:].astype(F32)
                for k in range(n[ax]-1): v=v+R[(k,)+lead+(rr,slice(None))].astype(F32)
                if stage==2: s.out[rr,s.mine]=v.astype(BF)
                else: R[(0,)+lead+(rr,slice(None))]=v.astype(BF)
                return 0
            if s.rows==step: body(0,0)
            else: lax.fori_loop(0,s.rows//step,body,0)

def lane_scratch(n, order, rows, cw):
    most=max(n.values())-1
    return [pltpu.VMEM((n[ax]-1,)+sh,BF) for ax,sh in zip(order,stage_shapes(n,order,rows,cw))]+[pltpu.SemaphoreType.DMA((4,most)),pltpu.SemaphoreType.DMA((4,most))]

def cut(ref, place, row0, rows, col0, cw):
    def src(fixed):
        cols=pl.ds(pl.multiple_of(col0+fixed["x"]*cw,128),cw) if "x" in fixed else pl.ds(col0,cw*place.n["x"])
        return ref.at[tuple(fixed.get(a,slice(None)) for a in "zy")+(pl.ds(row0,rows),cols)]
    return src

def plan_of(n, rf, rb, rc, d, own):
    nx=n["x"]; J=max(1,rf//128); plan=[]
    parts=AP if rf//AP>=16 else rf//16
    for i in range(parts): plan.append(("A",0 if J>1 and i<parts//2 else 1,i*(rf//parts),rf//parts,0,d//nx))
    w=max(BW,128*nx)
    for c0 in range(0,own,w): plan.append(("B",c0//512,0,rb,c0,w//nx))
    w=max(CW,128*nx)
    for k in range(4):
        for c0 in range(0,d,w): plan.append(("C",k,0,rc,c0,w//nx))
    plan.append(("S",0,0,rc,0,128))
    seen={}; full=[]
    for p in plan:
        j=seen.get(p[0],0); seen[p[0]]=j+1
        full.append(p+(ORDERS[p[0]][j%len(ORDERS[p[0]])],))
    return full
ORDERS=dict(A=["xyz","zxy","xyz","yzx"],B=["yxz","yzx","xyz","xyz"],C=["yzx","xyz","xyz","yxz"],S=["xyz"])
AP=4; BW=512; CW=1024; HOLD=0
LINK=91e3; LAT=4.0; MARGIN=1.0; COST=.25

def steps():
    T=[5.0]
    for t in range(4):
        T+=[4.2,("B",t),None,1.4]
        if t%2: T+=[("A",t//2)]
        T+=[None]
    T+=[2.8,None]*4+[.5]+[1.3,None]*4+[1.5,None,1.3,("C",0),None]+[1.9,None]*4
    T+=[1.6,None,1.7,("C",1),None,1.7,("C",2),None,1.5,("C",3),None,1.,None]
    T+=[2.4,None]*4+[1.0,None]*4+[.6,None]*8+[1.8,None]*2+[2.,None,2.5,None,2.,("S",0),None]
    return T

def arrivals(n, plan):
    now=0.; free=dict(x=0.,y=0.,z=0.); wait=[]; count=itertools.count(); res=[]; T=steps()
    def start(i,s):
        _,_,_,r0,_,cw,order=plan[i]; r=plan[i][3]
        if s<3:
            ax=order[s]; vol=math.prod(stage_shapes(n,order,r,cw)[s])*4*(n[ax]**2/4 if n[ax]>2 else 1)
        else: ax="x"; vol=r*cw*4
        free[ax]=max(now,free[ax])+vol/LINK
        heapq.heappush(wait,(free[ax]+LAT,next(count),i,s))
    for at,v in enumerate(T):
        if v is None:
            got=[]
            while wait and len(res)>=HOLD and (wait[0][0]+MARGIN<=now or at==len(T)-1):
                a,_,i,s=heapq.heappop(wait); now=max(now,a)+COST; got.append((i,s))
                if s<3: start(i,s+1)
            res.append(got)
        elif isinstance(v,tuple):
            for i,p in enumerate(plan):
                if p[:2]==v: start(i,0)
        else: now+=v
    return res

def tree(ys):
    ys=list(ys)
    while len(ys)>1: ys=[ys[i]+ys[i+1] if i+1<len(ys) else ys[i] for i in range(0,len(ys),2)]
    return ys[0]

def main_kernel(n, ns, length, plan, packed_w, *refs):
    (low2,cot,cots,w1,w2,residual,gain2,attended,wo,packed,pairs,probs,low,tail_low,ctx,w_in,x,gain1,decay3,weight3,h3,
     out,igrad,OA,OBk,OBr,OC,OS,
     x2,cot2,A,B,Cf,crec,dx_rec,out_rec,OBf,small,small_rec,tailb,tail_in,
     wsem1,wsem2,lsem,xsem,dsem,osem,csem,bsem,tsem,psem,outsem,s3,gather,spread,hb,e0,e1,e2,e3)=refs[:60]
    scr=refs[60:]
    place=Place(n); c=place.c; sib=place.sibling(); q=lax.axis_index("seq"); g=lax.axis_index("grp")
    d=x2.shape[1]; nz,ny=n["z"],n["y"]; nzy=nz*ny; rf=A.shape[2]; rb=B.shape[2]; own=B.shape[3]; rc=crec.shape[3]
    nst=decay3.shape[0]; J=max(1,rf//128); rj=rf//J
    sem=pltpu.get_barrier_semaphore()
    def sg(i,_):
        @pl.when(i!=q)
        def _(): pl.semaphore_signal(sem,inc=1,device_id={"seq":i},device_id_type=MESH)
        return 0
    lax.fori_loop(0,ns,sg,0)
    for k in range(1,n["x"]): pl.semaphore_signal(sem,inc=1,device_id=place.device("x",k),device_id_type=MESH)
    due=arrivals(n,plan); at=[0]
    outs={"A":OA,"B":OBf,"C":OC,"S":OS}; srcs={"A":lambda k:A,"B":lambda k:B,"C":lambda k:crec.at[k],"S":lambda k:small_rec}
    lanes=[]
    for i,(t,k,r0,r,c0,cw,o) in enumerate(plan):
        oc=(k*d+c0 if t=="C" else c0)
        lanes.append(Lane(place,o,r,cw,cut(srcs[t](k),place,r0,r,c0,cw),outs[t].at[pl.ds(r0,r),pl.ds(oc,cw*n["x"])],scr[5*i:5*i+5]))
    index={}
    for i,p in enumerate(plan): index.setdefault(p[0],[]).append(i)
    bcopies=[]
    def bcopy(c0,w):
        h=rb//2; cs=pl.ds(c0,w)
        return pltpu.make_async_remote_copy(src_ref=OBf.at[pl.ds(pl.multiple_of((1-c)*h,16),h),cs],dst_ref=OBr.at[:,cs],send_sem=bsem.at[0,c0//256],recv_sem=bsem.at[1,c0//256],device_id=sib,device_id_type=MESH)
    def launch(group,k):
        for i in index[group]:
            if plan[i][1]==k: lanes[i].start(0)
    def point():
        for i,s in due[at[0]]:
            lanes[i].finish(s)
            if s<3: lanes[i].start(s+1)
            elif plan[i][0]=="B":
                c0,w=plan[i][4],plan[i][5]*n["x"]; cs=pl.ds(c0,w); h=rb//2
                bcopy(c0,w).start(); bcopies.append((c0,w))
                OBk[:,cs]=OBf[pl.ds(pl.multiple_of(c*h,16),h),cs]
        at[0]+=1

    def forward_part(w1s,w2s,act,dexp):
        tiles=own//512; wd=rj if rj%128==0 else 512; per=512//wd
        def wcopy(b):
            if packed_w: s1=s2=b*wd
            else: s1=s2=lax.rem(b,nzy)*(2*rf)+c*rf+lax.div(b,nzy)*rj
            return (pltpu.make_async_copy(w1.at[:,pl.ds(pl.multiple_of(s1,128),wd)],w1s.at[:,pl.ds(pl.multiple_of(b*wd,128),wd)],wsem1.at[b]),
                    pltpu.make_async_copy(w2.at[pl.ds(pl.multiple_of(s2,16),wd),:],w2s.at[pl.ds(pl.multiple_of(b*wd,16),wd),:],wsem2.at[b]))
        cc=[pltpu.make_async_copy(cot,cot2.at[pl.ds(0,BLK),:],lsem.at[0]),pltpu.make_async_copy(cots,cot2.at[pl.ds(BLK,BLK),:],lsem.at[1]),pltpu.make_async_copy(low2,x2.at[pl.ds(0,BLK),:],lsem.at[2])]
        for v in cc: v.start()
        def go(b,_):
            u,v=wcopy(b); v.start(); u.start(); return 0
        lax.fori_loop(0,own//wd,go,0)
        pl.semaphore_wait(sem,ns-1+n["x"]-1)
        xs=pltpu.make_async_remote_copy(src_ref=low2,dst_ref=x2.at[pl.ds(BLK,BLK),:],send_sem=xsem.at[0],recv_sem=xsem.at[1],device_id=sib,device_id_type=MESH)
        xs.start()
        for v in cc: v.wait()
        for t in range(tiles):
            for b in range(t*per,(t+1)*per): wcopy(b)[1].wait()
            cs=slice(t*512,(t+1)*512)
            u=mm(cot2[...],w2s[cs,:],NT)
            for b in range(t*per,(t+1)*per): wcopy(b)[0].wait()
            if t==0: xs.wait()
            h=mm(x2[...],w1s[:,cs])
            a,gp=gelu_pair(h)
            act[:,cs]=a.astype(BF); dexp[:,cs]=(u*gp).astype(BF)
            v=mm(x2[...],dexp[:,cs],TN).astype(BF)
            for b in range(nzy): B[b//ny,b%ny,:,cs]=v[b*rb:(b+1)*rb]
            launch("B",t)
            point()
            v=mm(act[:,cs],cot2[...],TN).astype(BF)
            for b in range(512//rj):
                e=t*(512//rj)+b; j,zy=e//nzy,e%nzy
                A[zy//ny,zy%ny,j*rj:(j+1)*rj,:]=v[b*rj:(b+1)*rj]
            if t%2: launch("A",t//2)
            point()
        cot2[0:BLK,:]=mm(dexp[BLK:,:],w1s[...],NT).astype(BF)
        dc=pltpu.make_async_remote_copy(src_ref=cot2.at[pl.ds(0,BLK),:],dst_ref=dx_rec,send_sem=dsem.at[0],recv_sem=dsem.at[1],device_id=sib,device_id_type=MESH); dc.start()
        point()
        cot2[BLK:,:]=mm(act[BLK:,:],w2s[...]).astype(BF)
        oc=pltpu.make_async_remote_copy(src_ref=cot2.at[pl.ds(BLK,BLK),:],dst_ref=out_rec,send_sem=osem.at[0],recv_sem=osem.at[1],device_id=sib,device_id_type=MESH); oc.start()
        point()
        x2[0:BLK,:]=mm(dexp[0:BLK,:],w1s[...],NT).astype(BF)
        point()
        x2[BLK:,:]=mm(act[0:BLK,:],w2s[...]).astype(BF)
        point()
        dc.wait(); oc.wait()
    pl.run_scoped(forward_part,pltpu.VMEM((d,own),BF),pltpu.VMEM((own,d),BF),pltpu.VMEM((2*BLK,own),BF),pltpu.VMEM((2*BLK,own),BF))

    def ccopy(k):
        return pltpu.make_async_remote_copy(src_ref=Cf.at[k%2,:,:,1-c],dst_ref=crec.at[k],send_sem=csem.at[0,k],recv_sem=csem.at[1,k],device_id=sib,device_id_type=MESH)
    joined=set()
    def send_half(k, part, slot):
        if k>=2: join_half(k-2); ccopy(k-2).wait_send()
        for r in range(2):
            v=part(slice(r*d//2,(r+1)*d//2)).astype(BF)
            for b in range(nzy):
                e=r*nzy+b
                Cf[slot,e//2//ny,e//2%ny,e%2]=v[b*rc:(b+1)*rc]
        ccopy(k).start()
    def join_half(k):
        if k in joined: return
        joined.add(k); slot=k%2
        ccopy(k).wait_recv()
        def add(z,_):
            for y in range(ny):
                for h in range(rc//16):
                    rr=slice(h*16,h*16+16)
                    crec[k,z,y,rr,:]=(crec[k,z,y,rr,:].astype(F32)+Cf[slot,z,y,c,rr,:].astype(F32)).astype(BF)
            return 0
        lax.fori_loop(0,nz,add,0)
        launch("C",k)

    def rest(res,dq,dk,dv,dck,dcv,lowv,ctxv,ggrad2):
        loads=[pltpu.make_async_copy(residual,res,lsem.at[0]),pltpu.make_async_copy(low,lowv,lsem.at[1]),pltpu.make_async_copy(ctx,ctxv,lsem.at[2])]
        for v in loads: v.start()
        def attention_part(attv,wov,pk,pr,pbuf,branch,agrad):
            more=[pltpu.make_async_copy(attended,attv,lsem.at[3]),pltpu.make_async_copy(wo,wov,lsem.at[4]),pltpu.make_async_copy(packed,pk,lsem.at[5]),pltpu.make_async_copy(pairs,pr,lsem.at[6])]
            for v in more: v.start()
            def pload(h): return pltpu.make_async_copy(probs.at[h],pbuf.at[lax.rem(h,2)],psem.at[lax.rem(h,2)])
            pload(0).start()
            for v in loads: v.wait()
            ggrad2[...]=jnp.zeros_like(ggrad2)
            for part in range(4):
                def body(i,_):
                    rr=pl.ds(pl.multiple_of(part*128+i*64,64),64)
                    dy=x2[rr,:].astype(F32)+dx_rec[rr,:].astype(F32)
                    dvv,gg=norm_back(res[rr,:],gain2[...],dy)
                    stage[rr,:]=(res[rr,:]+x2[pl.ds(pl.multiple_of(BLK+part*128+i*64,64),64),:].astype(F32)+out_rec[rr,:].astype(F32)).astype(BF)
                    r=cot_own[rr,:].astype(F32)+dvv
                    res[rr,:]=r; branch[rr,:]=r.astype(BF)
                    ggrad2[...]+=fold(gg)
                    return 0
                lax.fori_loop(0,2,body,0)
                point()
            oc=pltpu.make_async_copy(stage,out,outsem.at[0]); oc.start()
            for v in more: v.wait()
            send_half(0,lambda r: mm(attv[:,r],branch[...],TN),0)
            point()
            agrad[...]=mm(branch[...],wov[...],NT).astype(BF)
            join_half(0); point()
            scale=1.0/math.sqrt(HD); half=BLK//2
            def head(h,_):
                @pl.when(h<HEADS-1)
                def _(): pload(h+1).start()
                pload(h).wait()
                slot=lax.rem(h,2)
                ql=pl.ds(pl.multiple_of(h*HD,128),HD); kl=pl.ds(pl.multiple_of(d+h*HD,128),HD); vl=pl.ds(pl.multiple_of(2*d+h*HD,128),HD)
                for r in range(2):
                    rows=slice(r*half,(r+1)*half); m=(r+1)*half
                    gr=agrad[rows,ql]
                    dot=jnp.sum(gr.astype(F32)*attv[rows,ql].astype(F32),axis=-1,keepdims=True)
                    p1=pbuf[slot,rows,:m]; p2=pbuf[slot,rows,BLK:]
                    s1=(p1.astype(F32)*(mm(gr,pk[:m,vl],NT)-dot)).astype(BF)
                    s2=(p2.astype(F32)*(mm(gr,pr[:,kl],NT)-dot)).astype(BF)
                    dq[rows,ql]=((mm(s1,pk[:m,kl])+mm(s2,pr[:,ql]))*scale).astype(BF)
                    qr=pk[rows,ql]
                    a1=mm(s1,qr,TN)*scale; a2=mm(s2,qr,TN)*scale; b1=mm(p1,gr,TN); b2=mm(p2,gr,TN)
                    if r==0: first=(a1,a2,b1,b2)
                dk[0:half,ql]=(first[0]+a1[:half]).astype(BF); dk[half:,ql]=a1[half:].astype(BF)
                dv[0:half,ql]=(first[2]+b1[:half]).astype(BF); dv[half:,ql]=b1[half:].astype(BF)
                dck[:,ql]=(first[1]+a2).astype(BF); dcv[:,ql]=(first[3]+b2).astype(BF)
                return 0
            for part in range(4):
                lax.fori_loop(2*part,2*part+2,head,0)
                point()
            oc.wait()
        def bigger(cot_,stage_):
            nonlocal cot_own,stage
            cot_own=cot_; stage=stage_
            cl=pltpu.make_async_copy(cot,cot_,lsem.at[7]); cl.start(); cl.wait()
            pl.run_scoped(attention_part,pltpu.VMEM((BLK,d),BF),pltpu.VMEM((d,d),BF),pltpu.VMEM((BLK,3*d),BF),pltpu.VMEM((CTX,2*d),BF),pltpu.VMEM((2,BLK,BLK+CTX),BF),pltpu.VMEM((BLK,d),BF),pltpu.VMEM((BLK,d),BF))
        cot_own=stage=None
        pl.run_scoped(bigger,pltpu.VMEM((BLK,d),BF),pltpu.VMEM((BLK,d),BF))
        def conv_part(w,dn,sig,u3,g3,y3,G,rate3,dec3,sp3,d0,d1,xv,tl,ggrad1,sm):
            loads=[pltpu.make_async_copy(w_in,w,lsem.at[0]),pltpu.make_async_copy(x,xv,lsem.at[1]),pltpu.make_async_copy(tail_low,tl,lsem.at[2])]
            for v in loads: v.start()
            def g1(): send_half(1,lambda r: mm(lowv[:,r],dq[...],TN),1)
            def g2(): send_half(2,lambda r: mm(lowv[:,r],dk[...],TN)+mm(ctxv[:,r],dck[...],TN),0)
            def g3_(): send_half(3,lambda r: mm(lowv[:,r],dv[...],TN)+mm(ctxv[:,r],dcv[...],TN),1)
            g1(); point(); g2(); join_half(1); point(); g3_(); join_half(2); point()
            for v in loads: v.wait()
            G[...]=(mm(dck[...],w[:,d:2*d],NT)+mm(dcv[...],w[:,2*d:],NT)).astype(BF)
            join_half(3); point()
            rate3[...]=rates(decay3[...],length)
            dec3[...]=jnp.exp(-float(BLK)*rate3[...])
            split_lanes(G,g3,CTX)
            a=lambda k: jnp.exp(-rate3[k]); kk=lambda k: weight3[k]*jnp.sqrt(rate3[k])
            av=[a(k) for k in range(nst)]; kv=[kk(k) for k in range(nst)]
            def back(i,gs):
                t=CTX-1-i; v=g3[t]
                gs=tuple(p*z+v for p,z in zip(av,gs))
                y3[t]=tree(p*z for p,z in zip(kv,gs))
                return gs
            gs=lax.fori_loop(0,CTX,back,tuple(jnp.zeros((8,128),F32) for _ in range(nst)),unroll=2)
            for k in range(nst): s3[k]=gs[k]
            ex=Scan(ns,nst,s3,gather,spread,hb,[e0,e1,e2,e3],False)
            ex.collect()
            point()
            split_lanes(tl,u3,CTX)
            up=lax.broadcasted_iota(jnp.int32,(8,128),0).astype(F32)
            for lt in range(d//128):
                ls=slice(lt*128,(lt+1)*128)
                for part in range(0,nst,8):
                    r=[jnp.broadcast_to(rate3[k,lt:lt+1,:],(8,128)) for k in range(part,part+8)]
                    a8=[jnp.exp(-8.0*v) for v in r]
                    def body(i,cr):
                        acc,der=cr
                        u=lowv[pl.ds(pl.multiple_of(i*16,16),16),ls].astype(F32)
                        for w_ in (u[:8],u[8:]):
                            der=tuple(p*(z+y) for p,z,y in zip(a8,der,acc))
                            acc=tuple(p*y+w_ for p,y in zip(a8,acc))
                        return acc,der
                    zz=tuple(jnp.zeros((8,128),F32) for _ in range(8))
                    acc,der=lax.fori_loop(0,(BLK-CTX)//16,body,(zz,zz))
                    for i,k in enumerate(range(part,part+8)):
                        j=7.0-up
                        sp3[k,lt:lt+1,:]=jnp.sum(jnp.exp(-j*r[i])*(8.0*der[i]+j*acc[i]),axis=0,keepdims=True)
                if lt==2: ex.scan(dec3)
                if lt%2==1: point()
            for part in range(0,nst,4):
                zz=tuple(jnp.zeros((8,128),F32) for _ in range(4))
                aa=[a(k) for k in range(part,part+4)]
                def fwd(t,cr):
                    h,hp,q0,q1=cr
                    u=u3[t]; gg=g3[t]
                    hp=tuple(p*(z+y) for p,z,y in zip(aa,hp,h))
                    h=tuple(p*z+u for p,z in zip(aa,h))
                    return h,hp,tuple(z+gg*y for z,y in zip(q0,h)),tuple(z+gg*y for z,y in zip(q1,hp))
                h,hp,q0,q1=lax.fori_loop(0,CTX,fwd,(tuple(h3[k] for k in range(part,part+4)),zz,zz,zz),unroll=2)
                for i,k in enumerate(range(part,part+4)):
                    d0[k]=q0[i]; d1[k]=q1[i]
                    m=float(BLK-CTX); am=jnp.exp(-m*rate3[k])
                    sp3[k]=aa[i]*(am*hp[i]+m*am*h[i]+sp3[k])
                point()
            ex.receive()
            for lt in range(d//128):
                ls=slice(lt*128,(lt+1)*128)
                r=[jnp.broadcast_to(rate3[k,lt:lt+1,:],(8,128)) for k in range(nst)]
                a8=[jnp.exp(-8.0*z) for z in r]
                v=tuple(jnp.broadcast_to((weight3[k,lt:lt+1,:]*jnp.sqrt(rate3[k,lt:lt+1,:]))*hb[k,lt:lt+1,:],(8,128))*jnp.exp(-(8.0-up)*r[k]) for k in range(nst))
                def two(v):
                    b=tree(v); v=tuple(p*z for p,z in zip(a8,v))
                    t=tree(v); v=tuple(p*z for p,z in zip(a8,v))
                    return jnp.concatenate([t,b],axis=0),v
                def ownrows(i,v):
                    tb,v=two(v)
                    sig[pl.ds(pl.multiple_of(BLK-CTX-16-i*16,16),16),ls]=tb.astype(BF)
                    return v
                v=lax.fori_loop(0,(BLK-CTX)//16,ownrows,v)
                def tailrows(i,v):
                    tb,v=two(v)
                    row=pl.multiple_of(CTX-16-i*16,16)
                    tailb[pl.ds(row,16),ls]=(tb+y3[pl.ds(row,16),lt,:]).astype(BF)
                    return v
                lax.fori_loop(0,CTX//16,tailrows,v)
                point()
            bc=pltpu.make_async_remote_copy(src_ref=tailb,dst_ref=tail_in,send_sem=tsem.at[0],recv_sem=tsem.at[1],device_id={"seq":jnp.maximum(q-1,0)},device_id_type=MESH)
            @pl.when(q>0)
            def _(): bc.start()
            def dnr(r):
                rr=slice(r*256,(r+1)*256)
                dn[rr,:]=mm(dq[rr,:],w[:,:d],NT)+mm(dk[rr,:],w[:,d:2*d],NT)+mm(dv[rr,:],w[:,2*d:],NT)
            dnr(0); point(); dnr(1); point()
            ggrad1[...]=jnp.zeros_like(ggrad1)
            def lastrows(i,_):
                rr=pl.ds(pl.multiple_of(i*64,64),64)
                dvv,gg=norm_back(xv[rr,:].astype(F32),gain1[...],dn[rr,:]+sig[rr,:].astype(F32))
                res[rr,:]=res[rr,:]+dvv
                ggrad1[...]+=fold(gg)
                return 0
            lax.fori_loop(0,(BLK-CTX)//64,lastrows,0)
            point()
            @pl.when(q==ns-1)
            def _(): tail_in[...]=jnp.zeros_like(tail_in)
            @pl.when(q<ns-1)
            def _(): bc.wait_recv()
            sig[BLK-CTX:,:]=tail_in[...]
            lax.fori_loop((BLK-CTX)//64,BLK//64,lastrows,0)
            ic=pltpu.make_async_copy(res,igrad,outsem.at[1]); ic.start()
            sm[...]=jnp.zeros_like(sm)
            for k in range(nst):
                r=rate3[k]; D1=d1[k]+hb[k]*sp3[k]; sq=jnp.sqrt(r)
                kw=sq*d0[k]; kd=weight3[k]*sq*(0.5*d0[k]-r*D1)
                for lt in range(d//128):
                    sm[k:k+1,lt*128:(lt+1)*128]=kw[lt:lt+1,:]; sm[nst+k:nst+k+1,lt*128:(lt+1)*128]=kd[lt:lt+1,:]
            sm[2*nst:2*nst+1,:]=jnp.sum(ggrad1[...],axis=0,keepdims=True)
            sm[2*nst+1:2*nst+2,:]=jnp.sum(ggrad2[...],axis=0,keepdims=True)
            for j in range(d//128):
                v=jnp.transpose(sm[:,j*128:(j+1)*128]).astype(BF)
                for b in range(128//rc):
                    e=j*(128//rc)+b
                    small[e//2//ny,e//2%ny,e%2,:,0:128]=v[b*rc:(b+1)*rc]
                    small[e//2//ny,e//2%ny,e%2,:,128:]=jnp.zeros((rc,small.shape[4]-128),BF)
            def scopy(): return pltpu.make_async_remote_copy(src_ref=small.at[:,:,1-c],dst_ref=small_rec,send_sem=csem.at[0,4],recv_sem=csem.at[1,4],device_id=sib,device_id_type=MESH)
            scopy().start()
            def join_small():
                scopy().wait_recv()
                for z in range(nz):
                    for y in range(ny):
                        small_rec[z,y]=(small_rec[z,y].astype(F32)+small[z,y,c].astype(F32)).astype(BF)
                launch("S",0)
            point()
            join_small()
            ic.wait(); scopy().wait_send(); ex.drain()
            @pl.when(q>0)
            def _(): bc.wait_send()
        M=pltpu.VMEM; st=(nst,8,128)
        pl.run_scoped(conv_part,M((d,3*d),BF),M((BLK,d),F32),M((BLK,d),BF),M((CTX,8,128),F32),M((CTX,8,128),F32),M((CTX,8,128),F32),M((CTX,d),BF),M(st,F32),M(st,F32),M(st,F32),M(st,F32),M(st,F32),M((BLK,d),BF),M((CTX,d),BF),M((8,d),F32),M((128,d),F32))
    M=pltpu.VMEM
    pl.run_scoped(rest,M((BLK,d),F32),M((BLK,d),BF),M((BLK,d),BF),M((BLK,d),BF),M((CTX,d),BF),M((CTX,d),BF),M((BLK,d),BF),M((CTX,d),BF),M((8,d),F32))
    point()
    assert at[0]==len(due)
    for v in bcopies: bcopy(*v).wait()
    for v in lanes: v.drain()
    for k in (2,3): ccopy(k).wait_send()

def main(n, ns, low2,cot,cots,w1,w2,residual,gain2,attended,wo,packed,pairs,probs,low,tail_low,ctx,w_in,x,gain1,decay3,weight3,h3):
    d=x.shape[1]; ff=w1.shape[1]; nz,ny,nx=n["z"],n["y"],n["x"]; nzy=nz*ny; own=ff//2; rf=own//nzy; rb=d//nzy; rc=d//ns; nst=decay3.shape[0]
    J=max(1,rf//128); rj=rf//J
    packed_w=rj%128!=0
    if packed_w:
        c=lax.rem(lax.axis_index("seq"),2)
        w1=lax.dynamic_index_in_dim(w1.reshape(d,nzy,2,rf),c,2,keepdims=False).reshape(d,own)
        w2=lax.dynamic_index_in_dim(w2.reshape(nzy,2,rf,d),c,1,keepdims=False).reshape(own,d)
    plan=plan_of(n,rf,rb,rc,d,own)
    V=pl.BlockSpec(memory_space=pltpu.VMEM); Y=pl.BlockSpec(memory_space=pl.ANY); M=pltpu.VMEM; D=pltpu.SemaphoreType.DMA
    wd=rj if not packed_w else 512
    scr=[M((2*BLK,d),BF),M((2*BLK,d),BF),M((nz,ny,rf,d),BF),M((nz,ny,rb,own),BF),M((2,nz,ny,2,rc,d),BF),M((4,nz,ny,rc,d),BF),M((BLK,d),BF),M((BLK,d),BF),
         M((rb,own),BF),M((nz,ny,2,rc,128*nx),BF),M((nz,ny,rc,128*nx),BF),M((CTX,d),BF),M((CTX,d),BF),
         D((own//wd,)),D((own//wd,)),D((8,)),D((2,)),D((2,)),D((2,)),D((2,5)),D((2,8)),D((2,)),D((2,)),D((2,))]
    sc=scan_scratch(ns,nst)
    scr+=[sc[0],sc[1],sc[2],M((nst,8,128),F32)]+sc[3:]
    for (t,k,r0,r,c0,cw,o) in plan: scr+=lane_scratch(n,o,r,cw)
    ins=[low2,cot,cots,w1,w2,residual,gain2,attended,wo,packed,pairs,probs,low,tail_low,ctx,w_in,x,gain1,decay3,weight3,h3]
    small_in={6,17,18,19,20}
    return pl.pallas_call(functools.partial(main_kernel,n,ns,BLK*ns,plan,packed_w),
        out_shape=[S(BLK,d),S(BLK,d,t=F32),S(rf,d),S(rc,own),S(rc,own),S(rc,4*d),S(rc,128*nx)],
        in_specs=[V if i in small_in else Y for i in range(len(ins))],out_specs=[Y,Y]+[V]*5,scratch_shapes=scr,
        compiler_params=pltpu.CompilerParams(collective_id=1,has_side_effects=True,vmem_limit_bytes=63*10**6),
        cost_estimate=pl.CostEstimate(flops=45*10**9,bytes_accessed=6*10**7,transcendentals=2*10**6),name="main")(*ins)


def closing_kernel(n, out0, igrad0, OA, OBk, OBr, OC, OS, out, igrad, g1, qkv, kw, kd, ao, g2, eg, ra):
    c=lax.rem(lax.axis_index("seq"),2)
    igrad[...]=igrad0[...]; out[...]=out0[...]
    d=OA.shape[1]; nst=kw.shape[0]
    ra[...]=OA[...].astype(F32)
    ao[...]=OC[:,:d].astype(F32)
    qkv[...]=OC[:,d:].astype(F32)
    s=OS[:,:128].astype(F32)
    t=jnp.transpose(s)
    kw[...]=t[:nst,:]; kd[...]=t[nst:2*nst,:]
    g1[...]=t[2*nst:2*nst+1,:]; g2[...]=t[2*nst+1:2*nst+2,:]
    nzy=n["z"]*n["y"]; rf=OBk.shape[1]//nzy; J=max(1,rf//128); rj=rf//J
    if rj%128==0:
        for j in range(J):
            for b in range(nzy):
                o=slice((j*nzy+b)*rj,(j*nzy+b+1)*rj)
                eg[:,pl.ds(pl.multiple_of((2*b+c)*rf+j*rj,128),rj)]=OBk[:,o].astype(F32)
                eg[:,pl.ds(pl.multiple_of((2*b+1-c)*rf+j*rj,128),rj)]=OBr[:,o].astype(F32)

def closing(n, out, igrad, OA, OBk, OBr, OC, OS, nst):
    V=pl.BlockSpec(memory_space=pltpu.VMEM); d=OA.shape[1]; rc=OC.shape[0]
    nzy=n["z"]*n["y"]; rf=OBk.shape[1]//nzy; J=max(1,rf//128); rj=rf//J
    res=list(pl.pallas_call(functools.partial(closing_kernel,n),
      out_shape=[S(*out.shape),S(*igrad.shape,t=F32),S(1,rc,t=F32),S(rc,3*d,t=F32),S(nst,rc,t=F32),S(nst,rc,t=F32),S(rc,d,t=F32),S(1,rc,t=F32),S(rc,2*OBk.shape[1],t=F32),S(*OA.shape,t=F32)],
      in_specs=[V]*7,out_specs=[V]*10,
      compiler_params=pltpu.CompilerParams(vmem_limit_bytes=63*10**6),name="closing")(out,igrad,OA,OBk,OBr,OC,OS))
    if rj%128:
        c=lax.rem(lax.axis_index("seq"),2)
        keep=OBk.reshape(rc,J,nzy,rj); other=OBr.reshape(rc,J,nzy,rj)
        e=jnp.stack([jnp.where(c==0,keep,other),jnp.where(c==0,other,keep)],3)
        res[8]=e.transpose(0,2,3,1,4).reshape(rc,2*OBk.shape[1]).astype(F32)
    res[0]=res[0][None]; res[1]=res[1][None]; res[4]=res[4].T; res[5]=res[5].T; res[2]=res[2].reshape(rc); res[7]=res[7].reshape(rc)
    return tuple(res)

def local(layer_input,segment_ids,context_mask,first_gain,attention_in,kernel_weight,kernel_decay,attention_out,second_gain,expand_weight,reduce_weight,cotangent):
    ns=lax.axis_size("seq"); nx=lax.axis_size("grp"); nst=kernel_decay.shape[1]; n=sizes(nx,ns)
    x=layer_input[0]; cot=cotangent[0]
    low,tail_low,packed,ctx,pairs,h3,decay3,weight3,cot_sib=front(ns,x,cot,first_gain[None],kernel_decay.T,kernel_weight.T,attention_in)
    probs,attended,residual,low2=attention(packed,pairs,segment_ids,context_mask[0],x,attention_out,second_gain[None])
    got=main(n,ns,low2,cot,cot_sib,expand_weight,reduce_weight,residual,second_gain[None],attended,attention_out,packed,pairs,probs,low,tail_low,ctx,attention_in,x,first_gain[None],decay3,weight3,h3)
    return closing(n,*got,nst)

def solution(mesh):
    ins=(P("grp","seq",None),P("grp","seq"),P("grp","seq",None))+(P(),)*8+(P("grp","seq",None),)
    outs=(P("grp","seq",None),)*2+(P("seq"),)+(P("seq",None),)*4+(P("seq"),)+(P("seq",None),)*2
    return jax.shard_map(local,mesh=mesh,in_specs=ins,out_specs=outs,check_vma=False)
```

```python
import functools
import heapq
import itertools
import math

import jax
import jax.numpy as jnp
from jax import lax
from jax.experimental import pallas as pl
from jax.experimental.pallas import tpu as pltpu
from jax.sharding import PartitionSpec as P

MESH=pl.DeviceIdType.MESH
BF=jnp.bfloat16

def sizes(nx, ns):
    ny = nx if ns % (2*nx)==0 else 1
    return {"x":nx,"y":ny,"z":ns//(2*ny)}

class Place:
    def __init__(s, n):
        s.n=n; q=lax.axis_index("seq")
        s.i=dict(x=lax.axis_index("grp"), y=lax.rem(lax.div(q,2),n["y"]), z=lax.div(q,2*n["y"])); s.c=lax.rem(q,2)
        s.to={}; s.ids={}
        for ax in "xyz":
            for k in range(1,n[ax]):
                v=s.i[ax]+k; s.to[ax,k]=jnp.where(v>=n[ax],v-n[ax],v)
                j=dict(s.i); j[ax]=s.to[ax,k]
                s.ids[ax,k]={"grp":j["x"],"seq":(j["z"]*n["y"]+j["y"])*2+s.c}
        s.other={"grp":s.i["x"],"seq":q+1-2*s.c}
    def at(s, ax, k): return s.to[ax,k]
    def device(s, ax, k): return s.ids[ax,k]
    def sibling(s): return s.other

def stage_shapes(n, order, rows, cw):
    left=dict(n); out=[]
    for ax in order:
        del left[ax]
        out.append(tuple(left[a] for a in "zy" if a in left)+(rows, cw*(left["x"] if "x" in left else 1)))
    return out


EPS=1e-5
BLK=512; CTX=128; HEADS=8; HD=128
F32=jnp.float32

def norm_rows(src, gain, dst, rows, step=64):
    def body(i,_):
        rr=pl.ds(pl.multiple_of(i*step,16),step)
        x=src[rr,:].astype(F32)
        x=x-jnp.mean(x,axis=-1,keepdims=True)
        v=jnp.mean(x*x,axis=-1,keepdims=True)
        dst[rr,:]=(x*lax.rsqrt(v+EPS)*gain).astype(BF)
        return 0
    lax.fori_loop(0,rows//step,body,0)

def rates(decay, length):
    return jnp.exp(decay)*(1.0/length)

def block_state(low, rate3, row0, rows, put):
    nst=rate3.shape[0]
    back=7.0-lax.broadcasted_iota(jnp.int32,(8,128),0).astype(F32)
    for lt in range(low.shape[1]//128):
        lanes=pl.ds(lt*128,128)
        r=[jnp.broadcast_to(rate3[n,lt:lt+1,:],(8,128)) for n in range(nst)]
        a8=[jnp.exp(-8.0*v) for v in r]
        def body(g,acc):
            u=low[pl.ds(pl.multiple_of(row0+g*16,16),16),lanes].astype(F32)
            lo,hi=u[:8],u[8:]
            acc=tuple(a*c+lo for a,c in zip(a8,acc))
            return tuple(a*c+hi for a,c in zip(a8,acc))
        acc=lax.fori_loop(0,rows//16,body,tuple(jnp.zeros((8,128),F32) for _ in range(nst)),unroll=4)
        for n in range(nst):
            put(n,lt,jnp.sum(acc[n]*jnp.exp(-back*r[n]),axis=0,keepdims=True))

def split_lanes(src, dst, rows):
    def body(g,_):
        for lt in range(src.shape[1]//128):
            v=src[pl.ds(pl.multiple_of(g*16,16),16),lt*128:(lt+1)*128].astype(F32)
            dst[pl.ds(g*16,16),lt,:]=v
        return 0
    lax.fori_loop(0,rows//16,body,0)

def join_lanes(src, dst, rows):
    def body(g,_):
        for lt in range(dst.shape[1]//128):
            dst[pl.ds(pl.multiple_of(g*16,16),16),lt*128:(lt+1)*128]=src[pl.ds(g*16,16),lt,:].astype(dst.dtype)
        return 0
    lax.fori_loop(0,rows//16,body,0)

class Scan:
    def __init__(s, ns, nst, s3, gather, spread, h3, sem, forward):
        s.ns,s.nst,s.s3,s.gather,s.spread,s.h3=ns,nst,s3,gather,spread,h3
        s.sem=sem; s.forward=forward; s.q=lax.axis_index("seq"); s.stride=ns//nst
        s.n=lax.div(s.q,s.stride); s.scans=lax.rem(s.q,s.stride)==0
    def to_scanner(s, n):
        return pltpu.make_async_remote_copy(src_ref=s.s3.at[n],dst_ref=s.gather.at[s.q],send_sem=s.sem[0].at[n],recv_sem=s.sem[1].at[s.q],device_id={"seq":n*s.stride},device_id_type=MESH)
    def from_block(s, b):
        return pltpu.make_async_remote_copy(src_ref=s.s3.at[0],dst_ref=s.gather.at[b],send_sem=s.sem[0].at[0],recv_sem=s.sem[1].at[b],device_id={"seq":b},device_id_type=MESH)
    def to_block(s, b):
        return pltpu.make_async_remote_copy(src_ref=s.spread.at[b],dst_ref=s.h3.at[s.n],send_sem=s.sem[2].at[b],recv_sem=s.sem[3].at[s.n],device_id={"seq":b},device_id_type=MESH)
    def from_scanner(s, n):
        return pltpu.make_async_remote_copy(src_ref=s.spread.at[0],dst_ref=s.h3.at[n],send_sem=s.sem[2].at[0],recv_sem=s.sem[3].at[n],device_id={"seq":n*s.stride},device_id_type=MESH)
    def each(s, count, fn, skip):
        def body(i,_):
            @pl.when(i!=skip)
            def _(): fn(i)
            return 0
        lax.fori_loop(0,count,body,0)
    def collect(s):
        mine=jnp.where(s.scans,s.n,s.nst)
        s.each(s.nst,lambda n:s.to_scanner(n).start(),mine)
    def scan(s, decay_block):
        mine=jnp.where(s.scans,s.n,s.nst)
        @pl.when(s.scans)
        def _():
            s.gather[s.q]=s.s3[s.n]
            s.each(s.ns,lambda b:s.from_block(b).wait_recv(),s.q)
            a=decay_block[s.n]
            def body(i,h):
                b=i if s.forward else s.ns-1-i
                s.spread[b]=h
                return a*h+s.gather[b]
            lax.fori_loop(0,s.ns,body,jnp.zeros((8,128),F32))
            s.each(s.ns,lambda b:s.to_block(b).start(),s.q)
            s.h3[s.n]=s.spread[s.q]
    def receive(s):
        mine=jnp.where(s.scans,s.n,s.nst)
        s.each(s.nst,lambda n:s.from_scanner(n).wait_recv(),mine)
    def drain(s):
        mine=jnp.where(s.scans,s.n,s.nst)
        s.each(s.nst,lambda n:s.to_scanner(n).wait_send(),mine)
        @pl.when(s.scans)
        def _(): s.each(s.ns,lambda b:s.to_block(b).wait_send(),s.q)

def scan_scratch(ns,nst):
    return [pltpu.VMEM((nst,8,128),F32),pltpu.VMEM((ns,8,128),F32),pltpu.VMEM((ns,8,128),F32),
      pltpu.SemaphoreType.DMA((nst,)),pltpu.SemaphoreType.DMA((ns,)),pltpu.SemaphoreType.DMA((ns,)),pltpu.SemaphoreType.DMA((nst,))]

def front_kernel(ns, length, x, cot, gain, decay, weight, w_hbm, low_out, tail_low, packed_out, ctx, pairs, h3, decay3, weight3, cot_sib,
                 low, packed, osem, w, own3, tail_x, rate3, dec3, u3, y3, s3, gather, spread, e0, e1, e2, e3, wsem, tsem, csem):
    q=lax.axis_index("seq"); c=lax.rem(q,2); g=lax.axis_index("grp")
    nst=decay.shape[0]
    sem=pltpu.get_barrier_semaphore()
    def sig(i,_):
        @pl.when(i!=q)
        def _(): pl.semaphore_signal(sem,inc=1,device_id={"seq":i},device_id_type=MESH)
        return 0
    lax.fori_loop(0,ns,sig,0)
    wcp=pltpu.make_async_copy(w_hbm,w,wsem); wcp.start()
    pl.semaphore_wait(sem,ns-1)
    tail=pltpu.make_async_remote_copy(src_ref=x.at[pl.ds(BLK-CTX,CTX),:],dst_ref=tail_x,send_sem=tsem.at[0],recv_sem=tsem.at[1],device_id={"seq":jnp.minimum(q+1,ns-1)},device_id_type=MESH)
    @pl.when(q<ns-1)
    def _(): tail.start()
    cc=pltpu.make_async_remote_copy(src_ref=cot,dst_ref=cot_sib,send_sem=csem.at[0],recv_sem=csem.at[1],device_id={"seq":q+1-2*c},device_id_type=MESH)
    cc.start()
    for lt in range(low.shape[1]//128):
        rows=slice(lt*128,(lt+1)*128)
        decay3[:,lt,:]=decay[:,rows]; weight3[:,lt,:]=weight[:,rows]
    rate3[...]=rates(decay3[...],length)
    dec3[...]=jnp.exp(-float(BLK)*rate3[...])
    norm_rows(x,gain[...],low,BLK)
    lc=pltpu.make_async_copy(low,low_out,osem.at[0]); lc.start()
    def put_own(n,lt,v): own3[n,lt:lt+1,:]=v
    block_state(low,rate3,0,BLK-CTX,put_own)
    wcp.wait()
    half=packed.shape[1]//2
    packed[:,:half]=jnp.dot(low[...],w[:,:half],preferred_element_type=F32).astype(BF)
    pc=pltpu.make_async_copy(packed.at[:,pl.ds(0,half)],packed_out.at[:,pl.ds(0,half)],osem.at[1]); pc.start()
    @pl.when(q>0)
    def _(): tail.wait_recv()
    @pl.when(q==0)
    def _(): tail_x[...]=jnp.zeros_like(tail_x)
    norm_rows(tail_x,gain[...],tail_low,CTX)
    def put_tail(n,lt,v): s3[n,lt:lt+1,:]=v
    block_state(tail_low,rate3,0,CTX,put_tail)
    for n in range(nst):
        s3[n]=jnp.exp(-float(BLK-CTX)*rate3[n])*s3[n]+own3[n]
    ex=Scan(ns,nst,s3,gather,spread,h3,[e0,e1,e2,e3],True)
    ex.collect()
    split_lanes(tail_low,u3,CTX)
    packed[:,half:2*half-half//3]=jnp.dot(low[...],w[:,half:2*half-half//3],preferred_element_type=F32).astype(BF)
    ex.scan(dec3)
    packed[:,2*half-half//3:]=jnp.dot(low[...],w[:,2*half-half//3:],preferred_element_type=F32).astype(BF)
    pd=pltpu.make_async_copy(packed.at[:,pl.ds(half,half)],packed_out.at[:,pl.ds(half,half)],osem.at[2]); pd.start()
    ex.receive()
    a=[jnp.exp(-rate3[n]) for n in range(nst)]
    k=[weight3[n]*jnp.sqrt(rate3[n]) for n in range(nst)]
    def step(t,h):
        u=u3[t]
        h=tuple(p*v+u for p,v in zip(a,h))
        ys=[p*v for p,v in zip(k,h)]
        while len(ys)>1: ys=[ys[i]+ys[i+1] if i+1<len(ys) else ys[i] for i in range(0,len(ys),2)]
        y3[t]=ys[0]
        return h
    lax.fori_loop(0,CTX,step,tuple(h3[n] for n in range(nst)),unroll=4)
    join_lanes(y3,ctx,CTX)
    d=low.shape[1]
    pairs[...]=jnp.dot(ctx[...],w[:,d:],preferred_element_type=F32).astype(BF)
    ex.drain()
    @pl.when(q<ns-1)
    def _(): tail.wait_send()
    cc.wait(); lc.wait(); pc.wait(); pd.wait()

def front(ns, x, cot, gain, decay, weight, w):
    nst=decay.shape[0]; d=x.shape[1]
    V=pl.BlockSpec(memory_space=pltpu.VMEM); A=pl.BlockSpec(memory_space=pl.ANY)
    S=lambda *s,t=BF: jax.ShapeDtypeStruct(s,t)
    return pl.pallas_call(functools.partial(front_kernel,ns,x.shape[0]*ns),
        out_shape=[S(BLK,d),S(CTX,d),S(BLK,3*d),S(CTX,d),S(CTX,2*d),S(nst,8,128,t=F32),S(nst,8,128,t=F32),S(nst,8,128,t=F32),S(BLK,d)],
        in_specs=[V,A,V,V,V,A],out_specs=[A,V,A]+[V]*5+[A],
        scratch_shapes=[pltpu.VMEM((BLK,d),BF),pltpu.VMEM((BLK,3*d),BF),pltpu.SemaphoreType.DMA((3,)),pltpu.VMEM((d,3*d),BF),pltpu.VMEM((nst,8,128),F32),pltpu.VMEM((CTX,d),BF),pltpu.VMEM((nst,8,128),F32),pltpu.VMEM((nst,8,128),F32),
          pltpu.VMEM((CTX,8,128),F32),pltpu.VMEM((CTX,8,128),F32)]+scan_scratch(ns,nst)+[pltpu.SemaphoreType.DMA,pltpu.SemaphoreType.DMA((2,)),pltpu.SemaphoreType.DMA((2,))],
        compiler_params=pltpu.CompilerParams(collective_id=0,has_side_effects=True,vmem_limit_bytes=63*10**6),
        name="front")(x,cot,gain,decay,weight,w)

NEG=-1e30
NT=(((1,),(1,)),((),()))
TN=(((0,),(0,)),((),()))
NN=(((1,),(0,)),((),()))
def mm(a,b,dims=NN): return lax.dot_general(a,b,dims,preferred_element_type=F32)

def attention_kernel(q,k,v,ck,cv,seg,vis,x,wo,gain,probs,attended,residual,low2,bias):
    h=pl.program_id(0)
    @pl.when(h==0)
    def _():
        row=jnp.broadcast_to(seg[...].astype(F32),(128,BLK))
        col=jnp.transpose(row)
        for i in range(BLK//128):
            ci=col[i*128:(i+1)*128]
            for j in range(BLK//128):
                if j>i:
                    bias[i*128:(i+1)*128,j*128:(j+1)*128]=jnp.full((128,128),NEG,F32); continue
                ok=ci==row[:,j*128:(j+1)*128]
                if i==j: ok=ok&(lax.broadcasted_iota(jnp.int32,(128,128),0)>=lax.broadcasted_iota(jnp.int32,(128,128),1))
                bias[i*128:(i+1)*128,j*128:(j+1)*128]=jnp.where(ok,0.0,NEG)
        seen=jnp.where((vis[...]==1)&(lax.axis_index("seq")>0),0.0,NEG)
        bias[:,BLK:]=jnp.broadcast_to(seen,(BLK,CTX))
    scale=1.0/math.sqrt(HD)
    half=BLK//2
    for r in range(2):
        rows=slice(r*half,(r+1)*half); n=(r+1)*half
        s1=mm(q[rows,:],k[:n,:],NT)*scale+bias[rows,:n]
        s2=mm(q[rows,:],ck[...],NT)*scale+bias[rows,BLK:]
        top=jnp.maximum(jnp.max(s1,axis=-1,keepdims=True),jnp.max(s2,axis=-1,keepdims=True))
        e1=jnp.exp(s1-top); e2=jnp.exp(s2-top)
        inv=1.0/(jnp.sum(e1,axis=-1,keepdims=True)+jnp.sum(e2,axis=-1,keepdims=True))
        p1=(e1*inv).astype(BF); p2=(e2*inv).astype(BF)
        probs[0,rows,:n]=p1; probs[0,rows,BLK:]=p2
        if n<BLK: probs[0,rows,n:BLK]=jnp.zeros((half,BLK-n),BF)
        o=mm(p1,v[:n,:])+mm(p2,cv[...])
        attended[rows,pl.ds(pl.multiple_of(h*HD,HD),HD)]=o.astype(BF)
    @pl.when(h==HEADS-1)
    def _():
        def body(i,_):
            rr=pl.ds(pl.multiple_of(i*128,128),128)
            res=x[rr,:].astype(F32)+mm(attended[rr,:],wo[...])
            residual[rr,:]=res
            m=res-jnp.mean(res,axis=-1,keepdims=True)
            var=jnp.mean(m*m,axis=-1,keepdims=True)
            low2[rr,:]=(m*lax.rsqrt(var+EPS)*gain[...]).astype(BF)
            return 0
        lax.fori_loop(0,BLK//128,body,0)

def attention(packed,pairs,seg,vis,x,wo,gain):
    d=x.shape[1]
    S=lambda *s,t=BF: jax.ShapeDtypeStruct(s,t)
    full=lambda a: pl.BlockSpec(a.shape,lambda h:(0,)*a.ndim)
    return pl.pallas_call(attention_kernel,grid=(HEADS,),
      in_specs=[pl.BlockSpec((BLK,HD),lambda h:(0,h)),pl.BlockSpec((BLK,HD),lambda h:(0,HEADS+h)),pl.BlockSpec((BLK,HD),lambda h:(0,2*HEADS+h)),
        pl.BlockSpec((CTX,HD),lambda h:(0,h)),pl.BlockSpec((CTX,HD),lambda h:(0,HEADS+h)),full(seg),full(vis),full(x),full(wo),full(gain)],
      out_specs=[pl.BlockSpec((1,BLK,BLK+CTX),lambda h:(h,0,0)),pl.BlockSpec((BLK,d),lambda h:(0,0)),pl.BlockSpec((BLK,d),lambda h:(0,0)),pl.BlockSpec((BLK,d),lambda h:(0,0))],
      out_shape=[S(HEADS,BLK,BLK+CTX),S(BLK,d),S(BLK,d,t=F32),S(BLK,d)],
      scratch_shapes=[pltpu.VMEM((BLK,BLK+CTX),F32)],
      compiler_params=pltpu.CompilerParams(vmem_limit_bytes=63*10**6),
      cost_estimate=pl.CostEstimate(flops=4*10**9,bytes_accessed=2*10**7,transcendentals=3*10**6),
      name="attention")(packed,packed,packed,pairs,pairs,seg,vis,x,wo,gain)

G0=math.sqrt(2/math.pi); G1=0.044715
def gelu_pair(h):
    h2=h*h
    th=jnp.tanh(h*(G0+G0*G1*h2))
    p=0.5*(1.0+th)
    return h*p, p+h*(0.5*(1.0-th*th))*(G0+3*G0*G1*h2)


def norm_back(v, gain, dy):
    x=v-jnp.mean(v,axis=-1,keepdims=True)
    s=lax.rsqrt(jnp.mean(x*x,axis=-1,keepdims=True)+EPS)
    nrm=x*s
    dn=dy*gain
    dv=(dn-jnp.mean(dn,axis=-1,keepdims=True)-nrm*jnp.mean(dn*nrm,axis=-1,keepdims=True))*s
    return dv, dy*nrm
def fold(v):
    return jnp.sum(v.reshape(v.shape[0]//8,8,v.shape[1]),axis=0)


def S(*s,t=BF): return jax.ShapeDtypeStruct(s,t)


class Lane:
    def __init__(s, place, order, rows, cw, src, out, scratch):
        s.p,s.order,s.rows,s.cw,s.src,s.out=place,order,rows,cw,src,out
        s.recv=scratch[:3]; s.ss,s.rs=scratch[3],scratch[4]
        s.begun=[]
        s.mine=pl.ds(pl.multiple_of(place.i["x"]*cw,128),cw)
    def held(s, stage, fixed):
        if stage==0: return s.src(fixed)
        left=[a for a in "zyx" if a not in s.order[:stage]]
        cols=slice(None)
        if "x" in fixed and "x" in left: cols=pl.ds(pl.multiple_of(fixed["x"]*s.cw,128),s.cw)
        return s.recv[stage-1].at[(0,)+tuple(fixed.get(a,slice(None)) for a in "zy" if a in left)+(slice(None),cols)]
    def copy(s, stage, k):
        ax="x" if stage==3 else s.order[stage]
        if stage==3: src=s.out.at[:,s.mine]; dst=s.out.at[:,s.mine]
        else: src=s.held(stage,{ax:s.p.at(ax,k)}); dst=s.recv[stage].at[k-1]
        return pltpu.make_async_remote_copy(src_ref=src,dst_ref=dst,send_sem=s.ss.at[stage,k-1],recv_sem=s.rs.at[stage,k-1],device_id=s.p.device(ax,k),device_id_type=MESH)
    def start(s, stage):
        for k in range(1,s.p.n["x" if stage==3 else s.order[stage]]):
            s.copy(stage,k).start(); s.begun.append((stage,k))
    def drain(s):
        for stage,k in s.begun: s.copy(stage,k).wait_send()
    def finish(s, stage):
        for st,k in s.begun:
            if st==stage: s.copy(st,k).wait_recv()
        if stage==3: return
        ax=s.order[stage]; n=s.p.n
        left=[a for a in "zy" if a not in s.order[:stage+1]]
        R=s.recv[stage]; step=min(s.rows,32)
        for lead in itertools.product(*[range(n[a]) for a in left]):
            fixed=dict(zip(left,lead)); fixed[ax]=s.p.i[ax]
            own=s.held(stage,fixed)
            def body(r,_):
                rr=pl.ds(pl.multiple_of(r*step,16),step)
                v=own[rr,:].astype(F32)
                for k in range(n[ax]-1): v=v+R[(k,)+lead+(rr,slice(None))].astype(F32)
                if stage==2: s.out[rr,s.mine]=v.astype(BF)
                else: R[(0,)+lead+(rr,slice(None))]=v.astype(BF)
                return 0
            if s.rows==step: body(0,0)
            else: lax.fori_loop(0,s.rows//step,body,0)

def lane_scratch(n, order, rows, cw):
    most=max(n.values())-1
    return [pltpu.VMEM((n[ax]-1,)+sh,BF) for ax,sh in zip(order,stage_shapes(n,order,rows,cw))]+[pltpu.SemaphoreType.DMA((4,most)),pltpu.SemaphoreType.DMA((4,most))]

def cut(ref, place, row0, rows, col0, cw):
    def src(fixed):
        cols=pl.ds(pl.multiple_of(col0+fixed["x"]*cw,128),cw) if "x" in fixed else pl.ds(col0,cw*place.n["x"])
        return ref.at[tuple(fixed.get(a,slice(None)) for a in "zy")+(pl.ds(row0,rows),cols)]
    return src

def plan_of(n, rf, rb, rc, d, own):
    nx=n["x"]; J=max(1,rf//128); plan=[]
    parts=AP if rf//AP>=16 else rf//16
    for i in range(parts): plan.append(("A",0 if J>1 and i<parts//2 else 1,i*(rf//parts),rf//parts,0,d//nx))
    w=max(BW,128*nx)
    for c0 in range(0,own,w): plan.append(("B",c0//512,0,rb,c0,w//nx))
    w=max(CW,128*nx)
    for k in range(4):
        for c0 in range(0,d,w): plan.append(("C",k,0,rc,c0,w//nx))
    plan.append(("S",0,0,rc,0,128))
    seen={}; full=[]
    for p in plan:
        j=seen.get(p[0],0); seen[p[0]]=j+1
        full.append(p+(ORDERS[p[0]][j%len(ORDERS[p[0]])],))
    return full
ORDERS=dict(A=["xyz","zxy","xyz","yzx"],B=["yxz","yzx","xyz","xyz"],C=["yzx","xyz","xyz","yxz"],S=["xyz"])
AP=4; BW=512; CW=1024; HOLD=0
LINK=91e3; LAT=4.0; MARGIN=1.0; COST=.25

def steps():
    T=[5.0]
    for t in range(4):
        T+=[4.2,("B",t),None,1.4]
        if t%2: T+=[("A",t//2)]
        T+=[None]
    T+=[2.8,None]*4+[.5]+[1.3,None]*4+[1.5,None,1.3,("C",0),None]+[1.9,None]*4
    T+=[1.6,None,1.7,("C",1),None,1.7,("C",2),None,1.5,("C",3),None,1.,None]
    T+=[2.4,None]*4+[1.0,None]*4+[.6,None]*8+[1.8,None]*2+[2.,None,2.5,None,2.,("S",0),None]
    return T

def arrivals(n, plan):
    now=0.; free=dict(x=0.,y=0.,z=0.); wait=[]; count=itertools.count(); res=[]; T=steps()
    def start(i,s):
        _,_,_,r0,_,cw,order=plan[i]; r=plan[i][3]
        if s<3:
            ax=order[s]; vol=math.prod(stage_shapes(n,order,r,cw)[s])*4*(n[ax]**2/4 if n[ax]>2 else 1)
        else: ax="x"; vol=r*cw*4
        free[ax]=max(now,free[ax])+vol/LINK
        heapq.heappush(wait,(free[ax]+LAT,next(count),i,s))
    for at,v in enumerate(T):
        if v is None:
            got=[]
            while wait and len(res)>=HOLD and (wait[0][0]+MARGIN<=now or at==len(T)-1):
                a,_,i,s=heapq.heappop(wait); now=max(now,a)+COST; got.append((i,s))
                if s<3: start(i,s+1)
            res.append(got)
        elif isinstance(v,tuple):
            for i,p in enumerate(plan):
                if p[:2]==v: start(i,0)
        else: now+=v
    return res

def tree(ys):
    ys=list(ys)
    while len(ys)>1: ys=[ys[i]+ys[i+1] if i+1<len(ys) else ys[i] for i in range(0,len(ys),2)]
    return ys[0]

def main_kernel(n, ns, length, plan, packed_w, *refs):
    (low2,cot,cots,w1,w2,residual,gain2,attended,wo,packed,pairs,probs,low,tail_low,ctx,w_in,x,gain1,decay3,weight3,h3,
     out,igrad,OA,OBk,OBr,OC,OS,
     x2,cot2,A,B,Cf,crec,dx_rec,out_rec,OBf,small,small_rec,tailb,tail_in,
     wsem1,wsem2,lsem,xsem,dsem,osem,csem,bsem,tsem,psem,outsem,s3,gather,spread,hb,e0,e1,e2,e3)=refs[:60]
    scr=refs[60:]
    place=Place(n); c=place.c; sib=place.sibling(); q=lax.axis_index("seq"); g=lax.axis_index("grp")
    d=x2.shape[1]; nz,ny=n["z"],n["y"]; nzy=nz*ny; rf=A.shape[2]; rb=B.shape[2]; own=B.shape[3]; rc=crec.shape[3]
    nst=decay3.shape[0]; J=max(1,rf//128); rj=rf//J
    sem=pltpu.get_barrier_semaphore()
    def sg(i,_):
        @pl.when(i!=q)
        def _(): pl.semaphore_signal(sem,inc=1,device_id={"seq":i},device_id_type=MESH)
        return 0
    lax.fori_loop(0,ns,sg,0)
    for k in range(1,n["x"]): pl.semaphore_signal(sem,inc=1,device_id=place.device("x",k),device_id_type=MESH)
    due=arrivals(n,plan); at=[0]
    outs={"A":OA,"B":OBf,"C":OC,"S":OS}; srcs={"A":lambda k:A,"B":lambda k:B,"C":lambda k:crec.at[k],"S":lambda k:small_rec}
    lanes=[]
    for i,(t,k,r0,r,c0,cw,o) in enumerate(plan):
        oc=(k*d+c0 if t=="C" else c0)
        lanes.append(Lane(place,o,r,cw,cut(srcs[t](k),place,r0,r,c0,cw),outs[t].at[pl.ds(r0,r),pl.ds(oc,cw*n["x"])],scr[5*i:5*i+5]))
    index={}
    for i,p in enumerate(plan): index.setdefault(p[0],[]).append(i)
    bcopies=[]
    def bcopy(c0,w):
        h=rb//2; cs=pl.ds(c0,w)
        return pltpu.make_async_remote_copy(src_ref=OBf.at[pl.ds(pl.multiple_of((1-c)*h,16),h),cs],dst_ref=OBr.at[:,cs],send_sem=bsem.at[0,c0//256],recv_sem=bsem.at[1,c0//256],device_id=sib,device_id_type=MESH)
    def launch(group,k):
        for i in index[group]:
            if plan[i][1]==k: lanes[i].start(0)
    def point():
        for i,s in due[at[0]]:
            lanes[i].finish(s)
            if s<3: lanes[i].start(s+1)
            elif plan[i][0]=="B":
                c0,w=plan[i][4],plan[i][5]*n["x"]; cs=pl.ds(c0,w); h=rb//2
                bcopy(c0,w).start(); bcopies.append((c0,w))
                OBk[:,cs]=OBf[pl.ds(pl.multiple_of(c*h,16),h),cs]
        at[0]+=1

    def forward_part(w1s,w2s,act,dexp):
        tiles=own//512; wd=rj if rj%128==0 else 512; per=512//wd
        def wcopy(b):
            if packed_w: s1=s2=b*wd
            else: s1=s2=lax.rem(b,nzy)*(2*rf)+c*rf+lax.div(b,nzy)*rj
            return (pltpu.make_async_copy(w1.at[:,pl.ds(pl.multiple_of(s1,128),wd)],w1s.at[:,pl.ds(pl.multiple_of(b*wd,128),wd)],wsem1.at[b]),
                    pltpu.make_async_copy(w2.at[pl.ds(pl.multiple_of(s2,16),wd),:],w2s.at[pl.ds(pl.multiple_of(b*wd,16),wd),:],wsem2.at[b]))
        cc=[pltpu.make_async_copy(cot,cot2.at[pl.ds(0,BLK),:],lsem.at[0]),pltpu.make_async_copy(cots,cot2.at[pl.ds(BLK,BLK),:],lsem.at[1]),pltpu.make_async_copy(low2,x2.at[pl.ds(0,BLK),:],lsem.at[2])]
        for v in cc: v.start()
        def go(b,_):
            u,v=wcopy(b); v.start(); u.start(); return 0
        lax.fori_loop(0,own//wd,go,0)
        pl.semaphore_wait(sem,ns-1+n["x"]-1)
        xs=pltpu.make_async_remote_copy(src_ref=low2,dst_ref=x2.at[pl.ds(BLK,BLK),:],send_sem=xsem.at[0],recv_sem=xsem.at[1],device_id=sib,device_id_type=MESH)
        xs.start()
        for v in cc: v.wait()
        for t in range(tiles):
            for b in range(t*per,(t+1)*per): wcopy(b)[1].wait()
            cs=slice(t*512,(t+1)*512)
            u=mm(cot2[...],w2s[cs,:],NT)
            for b in range(t*per,(t+1)*per): wcopy(b)[0].wait()
            if t==0: xs.wait()
            h=mm(x2[...],w1s[:,cs])
            a,gp=gelu_pair(h)
            act[:,cs]=a.astype(BF); dexp[:,cs]=(u*gp).astype(BF)
            v=mm(x2[...],dexp[:,cs],TN).astype(BF)
            for b in range(nzy): B[b//ny,b%ny,:,cs]=v[b*rb:(b+1)*rb]
            launch("B",t)
            point()
            v=mm(act[:,cs],cot2[...],TN).astype(BF)
            for b in range(512//rj):
                e=t*(512//rj)+b; j,zy=e//nzy,e%nzy
                A[zy//ny,zy%ny,j*rj:(j+1)*rj,:]=v[b*rj:(b+1)*rj]
            if t%2: launch("A",t//2)
            point()
        cot2[0:BLK,:]=mm(dexp[BLK:,:],w1s[...],NT).astype(BF)
        dc=pltpu.make_async_remote_copy(src_ref=cot2.at[pl.ds(0,BLK),:],dst_ref=dx_rec,send_sem=dsem.at[0],recv_sem=dsem.at[1],device_id=sib,device_id_type=MESH); dc.start()
        point()
        cot2[BLK:,:]=mm(act[BLK:,:],w2s[...]).astype(BF)
        oc=pltpu.make_async_remote_copy(src_ref=cot2.at[pl.ds(BLK,BLK),:],dst_ref=out_rec,send_sem=osem.at[0],recv_sem=osem.at[1],device_id=sib,device_id_type=MESH); oc.start()
        point()
        x2[0:BLK,:]=mm(dexp[0:BLK,:],w1s[...],NT).astype(BF)
        point()
        x2[BLK:,:]=mm(act[0:BLK,:],w2s[...]).astype(BF)
        point()
        dc.wait(); oc.wait()
    pl.run_scoped(forward_part,pltpu.VMEM((d,own),BF),pltpu.VMEM((own,d),BF),pltpu.VMEM((2*BLK,own),BF),pltpu.VMEM((2*BLK,own),BF))

    def ccopy(k):
        return pltpu.make_async_remote_copy(src_ref=Cf.at[k%2,:,:,1-c],dst_ref=crec.at[k],send_sem=csem.at[0,k],recv_sem=csem.at[1,k],device_id=sib,device_id_type=MESH)
    joined=set()
    def send_half(k, part, slot):
        if k>=2: join_half(k-2); ccopy(k-2).wait_send()
        for r in range(2):
            v=part(slice(r*d//2,(r+1)*d//2)).astype(BF)
            for b in range(nzy):
                e=r*nzy+b
                Cf[slot,e//2//ny,e//2%ny,e%2]=v[b*rc:(b+1)*rc]
        ccopy(k).start()
    def join_half(k):
        if k in joined: return
        joined.add(k); slot=k%2
        ccopy(k).wait_recv()
        def add(z,_):
            for y in range(ny):
                for h in range(rc//16):
                    rr=slice(h*16,h*16+16)
                    crec[k,z,y,rr,:]=(crec[k,z,y,rr,:].astype(F32)+Cf[slot,z,y,c,rr,:].astype(F32)).astype(BF)
            return 0
        lax.fori_loop(0,nz,add,0)
        launch("C",k)

    def rest(res,dq,dk,dv,dck,dcv,lowv,ctxv,ggrad2):
        loads=[pltpu.make_async_copy(residual,res,lsem.at[0]),pltpu.make_async_copy(low,lowv,lsem.at[1]),pltpu.make_async_copy(ctx,ctxv,lsem.at[2])]
        for v in loads: v.start()
        def attention_part(attv,wov,pk,pr,pbuf,branch,agrad):
            more=[pltpu.make_async_copy(attended,attv,lsem.at[3]),pltpu.make_async_copy(wo,wov,lsem.at[4]),pltpu.make_async_copy(packed,pk,lsem.at[5]),pltpu.make_async_copy(pairs,pr,lsem.at[6])]
            for v in more: v.start()
            def pload(h): return pltpu.make_async_copy(probs.at[h],pbuf.at[lax.rem(h,2)],psem.at[lax.rem(h,2)])
            pload(0).start()
            for v in loads: v.wait()
            ggrad2[...]=jnp.zeros_like(ggrad2)
            for part in range(4):
                def body(i,_):
                    rr=pl.ds(pl.multiple_of(part*128+i*64,64),64)
                    dy=x2[rr,:].astype(F32)+dx_rec[rr,:].astype(F32)
                    dvv,gg=norm_back(res[rr,:],gain2[...],dy)
                    stage[rr,:]=(res[rr,:]+x2[pl.ds(pl.multiple_of(BLK+part*128+i*64,64),64),:].astype(F32)+out_rec[rr,:].astype(F32)).astype(BF)
                    r=cot_own[rr,:].astype(F32)+dvv
                    res[rr,:]=r; branch[rr,:]=r.astype(BF)
                    ggrad2[...]+=fold(gg)
                    return 0
                lax.fori_loop(0,2,body,0)
                point()
            oc=pltpu.make_async_copy(stage,out,outsem.at[0]); oc.start()
            for v in more: v.wait()
            send_half(0,lambda r: mm(attv[:,r],branch[...],TN),0)
            point()
            agrad[...]=mm(branch[...],wov[...],NT).astype(BF)
            join_half(0); point()
            scale=1.0/math.sqrt(HD); half=BLK//2
            def head(h,_):
                @pl.when(h<HEADS-1)
                def _(): pload(h+1).start()
                pload(h).wait()
                slot=lax.rem(h,2)
                ql=pl.ds(pl.multiple_of(h*HD,128),HD); kl=pl.ds(pl.multiple_of(d+h*HD,128),HD); vl=pl.ds(pl.multiple_of(2*d+h*HD,128),HD)
                for r in range(2):
                    rows=slice(r*half,(r+1)*half); m=(r+1)*half
                    gr=agrad[rows,ql]
                    dot=jnp.sum(gr.astype(F32)*attv[rows,ql].astype(F32),axis=-1,keepdims=True)
                    p1=pbuf[slot,rows,:m]; p2=pbuf[slot,rows,BLK:]
                    s1=(p1.astype(F32)*(mm(gr,pk[:m,vl],NT)-dot)).astype(BF)
                    s2=(p2.astype(F32)*(mm(gr,pr[:,kl],NT)-dot)).astype(BF)
                    dq[rows,ql]=((mm(s1,pk[:m,kl])+mm(s2,pr[:,ql]))*scale).astype(BF)
                    qr=pk[rows,ql]
                    a1=mm(s1,qr,TN)*scale; a2=mm(s2,qr,TN)*scale; b1=mm(p1,gr,TN); b2=mm(p2,gr,TN)
                    if r==0: first=(a1,a2,b1,b2)
                dk[0:half,ql]=(first[0]+a1[:half]).astype(BF); dk[half:,ql]=a1[half:].astype(BF)
                dv[0:half,ql]=(first[2]+b1[:half]).astype(BF); dv[half:,ql]=b1[half:].astype(BF)
                dck[:,ql]=(first[1]+a2).astype(BF); dcv[:,ql]=(first[3]+b2).astype(BF)
                return 0
            for part in range(4):
                lax.fori_loop(2*part,2*part+2,head,0)
                point()
            oc.wait()
        def bigger(cot_,stage_):
            nonlocal cot_own,stage
            cot_own=cot_; stage=stage_
            cl=pltpu.make_async_copy(cot,cot_,lsem.at[7]); cl.start(); cl.wait()
            pl.run_scoped(attention_part,pltpu.VMEM((BLK,d),BF),pltpu.VMEM((d,d),BF),pltpu.VMEM((BLK,3*d),BF),pltpu.VMEM((CTX,2*d),BF),pltpu.VMEM((2,BLK,BLK+CTX),BF),pltpu.VMEM((BLK,d),BF),pltpu.VMEM((BLK,d),BF))
        cot_own=stage=None
        pl.run_scoped(bigger,pltpu.VMEM((BLK,d),BF),pltpu.VMEM((BLK,d),BF))
        def conv_part(w,dn,sig,u3,g3,y3,G,rate3,dec3,sp3,d0,d1,xv,tl,ggrad1,sm):
            loads=[pltpu.make_async_copy(w_in,w,lsem.at[0]),pltpu.make_async_copy(x,xv,lsem.at[1]),pltpu.make_async_copy(tail_low,tl,lsem.at[2])]
            for v in loads: v.start()
            def g1(): send_half(1,lambda r: mm(lowv[:,r],dq[...],TN),1)
            def g2(): send_half(2,lambda r: mm(lowv[:,r],dk[...],TN)+mm(ctxv[:,r],dck[...],TN),0)
            def g3_(): send_half(3,lambda r: mm(lowv[:,r],dv[...],TN)+mm(ctxv[:,r],dcv[...],TN),1)
            g1(); point(); g2(); join_half(1); point(); g3_(); join_half(2); point()
            for v in loads: v.wait()
            G[...]=(mm(dck[...],w[:,d:2*d],NT)+mm(dcv[...],w[:,2*d:],NT)).astype(BF)
            join_half(3); point()
            rate3[...]=rates(decay3[...],length)
            dec3[...]=jnp.exp(-float(BLK)*rate3[...])
            split_lanes(G,g3,CTX)
            a=lambda k: jnp.exp(-rate3[k]); kk=lambda k: weight3[k]*jnp.sqrt(rate3[k])
            av=[a(k) for k in range(nst)]; kv=[kk(k) for k in range(nst)]
            def back(i,gs):
                t=CTX-1-i; v=g3[t]
                gs=tuple(p*z+v for p,z in zip(av,gs))
                y3[t]=tree(p*z for p,z in zip(kv,gs))
                return gs
            gs=lax.fori_loop(0,CTX,back,tuple(jnp.zeros((8,128),F32) for _ in range(nst)),unroll=2)
            for k in range(nst): s3[k]=gs[k]
            ex=Scan(ns,nst,s3,gather,spread,hb,[e0,e1,e2,e3],False)
            ex.collect()
            point()
            split_lanes(tl,u3,CTX)
            up=lax.broadcasted_iota(jnp.int32,(8,128),0).astype(F32)
            for lt in range(d//128):
                ls=slice(lt*128,(lt+1)*128)
                for part in range(0,nst,8):
                    r=[jnp.broadcast_to(rate3[k,lt:lt+1,:],(8,128)) for k in range(part,part+8)]
                    a8=[jnp.exp(-8.0*v) for v in r]
                    def body(i,cr):
                        acc,der=cr
                        u=lowv[pl.ds(pl.multiple_of(i*16,16),16),ls].astype(F32)
                        for w_ in (u[:8],u[8:]):
                            der=tuple(p*(z+y) for p,z,y in zip(a8,der,acc))
                            acc=tuple(p*y+w_ for p,y in zip(a8,acc))
                        return acc,der
                    zz=tuple(jnp.zeros((8,128),F32) for _ in range(8))
                    acc,der=lax.fori_loop(0,(BLK-CTX)//16,body,(zz,zz))
                    for i,k in enumerate(range(part,part+8)):
                        j=7.0-up
                        sp3[k,lt:lt+1,:]=jnp.sum(jnp.exp(-j*r[i])*(8.0*der[i]+j*acc[i]),axis=0,keepdims=True)
                if lt==2: ex.scan(dec3)
                if lt%2==1: point()
            for part in range(0,nst,4):
                zz=tuple(jnp.zeros((8,128),F32) for _ in range(4))
                aa=[a(k) for k in range(part,part+4)]
                def fwd(t,cr):
                    h,hp,q0,q1=cr
                    u=u3[t]; gg=g3[t]
                    hp=tuple(p*(z+y) for p,z,y in zip(aa,hp,h))
                    h=tuple(p*z+u for p,z in zip(aa,h))
                    return h,hp,tuple(z+gg*y for z,y in zip(q0,h)),tuple(z+gg*y for z,y in zip(q1,hp))
                h,hp,q0,q1=lax.fori_loop(0,CTX,fwd,(tuple(h3[k] for k in range(part,part+4)),zz,zz,zz),unroll=2)
                for i,k in enumerate(range(part,part+4)):
                    d0[k]=q0[i]; d1[k]=q1[i]
                    m=float(BLK-CTX); am=jnp.exp(-m*rate3[k])
                    sp3[k]=aa[i]*(am*hp[i]+m*am*h[i]+sp3[k])
                point()
            ex.receive()
            for lt in range(d//128):
                ls=slice(lt*128,(lt+1)*128)
                r=[jnp.broadcast_to(rate3[k,lt:lt+1,:],(8,128)) for k in range(nst)]
                a8=[jnp.exp(-8.0*z) for z in r]
                v=tuple(jnp.broadcast_to((weight3[k,lt:lt+1,:]*jnp.sqrt(rate3[k,lt:lt+1,:]))*hb[k,lt:lt+1,:],(8,128))*jnp.exp(-(8.0-up)*r[k]) for k in range(nst))
                def two(v):
                    b=tree(v); v=tuple(p*z for p,z in zip(a8,v))
                    t=tree(v); v=tuple(p*z for p,z in zip(a8,v))
                    return jnp.concatenate([t,b],axis=0),v
                def ownrows(i,v):
                    tb,v=two(v)
                    sig[pl.ds(pl.multiple_of(BLK-CTX-16-i*16,16),16),ls]=tb.astype(BF)
                    return v
                v=lax.fori_loop(0,(BLK-CTX)//16,ownrows,v)
                def tailrows(i,v):
                    tb,v=two(v)
                    row=pl.multiple_of(CTX-16-i*16,16)
                    tailb[pl.ds(row,16),ls]=(tb+y3[pl.ds(row,16),lt,:]).astype(BF)
                    return v
                lax.fori_loop(0,CTX//16,tailrows,v)
                point()
            bc=pltpu.make_async_remote_copy(src_ref=tailb,dst_ref=tail_in,send_sem=tsem.at[0],recv_sem=tsem.at[1],device_id={"seq":jnp.maximum(q-1,0)},device_id_type=MESH)
            @pl.when(q>0)
            def _(): bc.start()
            def dnr(r):
                rr=slice(r*256,(r+1)*256)
                dn[rr,:]=mm(dq[rr,:],w[:,:d],NT)+mm(dk[rr,:],w[:,d:2*d],NT)+mm(dv[rr,:],w[:,2*d:],NT)
            dnr(0); point(); dnr(1); point()
            ggrad1[...]=jnp.zeros_like(ggrad1)
            def lastrows(i,_):
                rr=pl.ds(pl.multiple_of(i*64,64),64)
                dvv,gg=norm_back(xv[rr,:].astype(F32),gain1[...],dn[rr,:]+sig[rr,:].astype(F32))
                res[rr,:]=res[rr,:]+dvv
                ggrad1[...]+=fold(gg)
                return 0
            lax.fori_loop(0,(BLK-CTX)//64,lastrows,0)
            point()
            @pl.when(q==ns-1)
            def _(): tail_in[...]=jnp.zeros_like(tail_in)
            @pl.when(q<ns-1)
            def _(): bc.wait_recv()
            sig[BLK-CTX:,:]=tail_in[...]
            lax.fori_loop((BLK-CTX)//64,BLK//64,lastrows,0)
            ic=pltpu.make_async_copy(res,igrad,outsem.at[1]); ic.start()
            sm[...]=jnp.zeros_like(sm)
            for k in range(nst):
                r=rate3[k]; D1=d1[k]+hb[k]*sp3[k]; sq=jnp.sqrt(r)
                kw=sq*d0[k]; kd=weight3[k]*sq*(0.5*d0[k]-r*D1)
                for lt in range(d//128):
                    sm[k:k+1,lt*128:(lt+1)*128]=kw[lt:lt+1,:]; sm[nst+k:nst+k+1,lt*128:(lt+1)*128]=kd[lt:lt+1,:]
            sm[2*nst:2*nst+1,:]=jnp.sum(ggrad1[...],axis=0,keepdims=True)
            sm[2*nst+1:2*nst+2,:]=jnp.sum(ggrad2[...],axis=0,keepdims=True)
            for j in range(d//128):
                v=jnp.transpose(sm[:,j*128:(j+1)*128]).astype(BF)
                for b in range(128//rc):
                    e=j*(128//rc)+b
                    small[e//2//ny,e//2%ny,e%2,:,0:128]=v[b*rc:(b+1)*rc]
                    small[e//2//ny,e//2%ny,e%2,:,128:]=jnp.zeros((rc,small.shape[4]-128),BF)
            def scopy(): return pltpu.make_async_remote_copy(src_ref=small.at[:,:,1-c],dst_ref=small_rec,send_sem=csem.at[0,4],recv_sem=csem.at[1,4],device_id=sib,device_id_type=MESH)
            scopy().start()
            def join_small():
                scopy().wait_recv()
                for z in range(nz):
                    for y in range(ny):
                        small_rec[z,y]=(small_rec[z,y].astype(F32)+small[z,y,c].astype(F32)).astype(BF)
                launch("S",0)
            point()
            join_small()
            ic.wait(); scopy().wait_send(); ex.drain()
            @pl.when(q>0)
            def _(): bc.wait_send()
        M=pltpu.VMEM; st=(nst,8,128)
        pl.run_scoped(conv_part,M((d,3*d),BF),M((BLK,d),F32),M((BLK,d),BF),M((CTX,8,128),F32),M((CTX,8,128),F32),M((CTX,8,128),F32),M((CTX,d),BF),M(st,F32),M(st,F32),M(st,F32),M(st,F32),M(st,F32),M((BLK,d),BF),M((CTX,d),BF),M((8,d),F32),M((128,d),F32))
    M=pltpu.VMEM
    pl.run_scoped(rest,M((BLK,d),F32),M((BLK,d),BF),M((BLK,d),BF),M((BLK,d),BF),M((CTX,d),BF),M((CTX,d),BF),M((BLK,d),BF),M((CTX,d),BF),M((8,d),F32))
    point()
    assert at[0]==len(due)
    for v in bcopies: bcopy(*v).wait()
    for v in lanes: v.drain()
    for k in (2,3): ccopy(k).wait_send()

def main(n, ns, low2,cot,cots,w1,w2,residual,gain2,attended,wo,packed,pairs,probs,low,tail_low,ctx,w_in,x,gain1,decay3,weight3,h3):
    d=x.shape[1]; ff=w1.shape[1]; nz,ny,nx=n["z"],n["y"],n["x"]; nzy=nz*ny; own=ff//2; rf=own//nzy; rb=d//nzy; rc=d//ns; nst=decay3.shape[0]
    J=max(1,rf//128); rj=rf//J
    packed_w=rj%128!=0
    if packed_w:
        c=lax.rem(lax.axis_index("seq"),2)
        w1=lax.dynamic_index_in_dim(w1.reshape(d,nzy,2,rf),c,2,keepdims=False).reshape(d,own)
        w2=lax.dynamic_index_in_dim(w2.reshape(nzy,2,rf,d),c,1,keepdims=False).reshape(own,d)
    plan=plan_of(n,rf,rb,rc,d,own)
    V=pl.BlockSpec(memory_space=pltpu.VMEM); Y=pl.BlockSpec(memory_space=pl.ANY); M=pltpu.VMEM; D=pltpu.SemaphoreType.DMA
    wd=rj if not packed_w else 512
    scr=[M((2*BLK,d),BF),M((2*BLK,d),BF),M((nz,ny,rf,d),BF),M((nz,ny,rb,own),BF),M((2,nz,ny,2,rc,d),BF),M((4,nz,ny,rc,d),BF),M((BLK,d),BF),M((BLK,d),BF),
         M((rb,own),BF),M((nz,ny,2,rc,128*nx),BF),M((nz,ny,rc,128*nx),BF),M((CTX,d),BF),M((CTX,d),BF),
         D((own//wd,)),D((own//wd,)),D((8,)),D((2,)),D((2,)),D((2,)),D((2,5)),D((2,8)),D((2,)),D((2,)),D((2,))]
    sc=scan_scratch(ns,nst)
    scr+=[sc[0],sc[1],sc[2],M((nst,8,128),F32)]+sc[3:]
    for (t,k,r0,r,c0,cw,o) in plan: scr+=lane_scratch(n,o,r,cw)
    ins=[low2,cot,cots,w1,w2,residual,gain2,attended,wo,packed,pairs,probs,low,tail_low,ctx,w_in,x,gain1,decay3,weight3,h3]
    small_in={6,17,18,19,20}
    return pl.pallas_call(functools.partial(main_kernel,n,ns,BLK*ns,plan,packed_w),
        out_shape=[S(BLK,d),S(BLK,d,t=F32),S(rf,d),S(rc,own),S(rc,own),S(rc,4*d),S(rc,128*nx)],
        in_specs=[V if i in small_in else Y for i in range(len(ins))],out_specs=[Y,Y]+[V]*5,scratch_shapes=scr,
        compiler_params=pltpu.CompilerParams(collective_id=1,has_side_effects=True,vmem_limit_bytes=63*10**6),
        cost_estimate=pl.CostEstimate(flops=45*10**9,bytes_accessed=6*10**7,transcendentals=2*10**6),name="main")(*ins)


def closing_kernel(n, out0, igrad0, OA, OBk, OBr, OC, OS, out, igrad, g1, qkv, kw, kd, ao, g2, eg, ra):
    c=lax.rem(lax.axis_index("seq"),2)
    igrad[...]=igrad0[...]; out[...]=out0[...]
    d=OA.shape[1]; nst=kw.shape[0]
    ra[...]=OA[...].astype(F32)
    ao[...]=OC[:,:d].astype(F32)
    qkv[...]=OC[:,d:].astype(F32)
    s=OS[:,:128].astype(F32)
    t=jnp.transpose(s)
    kw[...]=t[:nst,:]; kd[...]=t[nst:2*nst,:]
    g1[...]=t[2*nst:2*nst+1,:]; g2[...]=t[2*nst+1:2*nst+2,:]
    nzy=n["z"]*n["y"]; rf=OBk.shape[1]//nzy; J=max(1,rf//128); rj=rf//J
    if rj%128==0:
        for j in range(J):
            for b in range(nzy):
                o=slice((j*nzy+b)*rj,(j*nzy+b+1)*rj)
                eg[:,pl.ds(pl.multiple_of((2*b+c)*rf+j*rj,128),rj)]=OBk[:,o].astype(F32)
                eg[:,pl.ds(pl.multiple_of((2*b+1-c)*rf+j*rj,128),rj)]=OBr[:,o].astype(F32)

def closing(n, out, igrad, OA, OBk, OBr, OC, OS, nst):
    V=pl.BlockSpec(memory_space=pltpu.VMEM); d=OA.shape[1]; rc=OC.shape[0]
    nzy=n["z"]*n["y"]; rf=OBk.shape[1]//nzy; J=max(1,rf//128); rj=rf//J
    res=list(pl.pallas_call(functools.partial(closing_kernel,n),
      out_shape=[S(*out.shape),S(*igrad.shape,t=F32),S(1,rc,t=F32),S(rc,3*d,t=F32),S(nst,rc,t=F32),S(nst,rc,t=F32),S(rc,d,t=F32),S(1,rc,t=F32),S(rc,2*OBk.shape[1],t=F32),S(*OA.shape,t=F32)],
      in_specs=[V]*7,out_specs=[V]*10,
      compiler_params=pltpu.CompilerParams(vmem_limit_bytes=63*10**6),name="closing")(out,igrad,OA,OBk,OBr,OC,OS))
    if rj%128:
        c=lax.rem(lax.axis_index("seq"),2)
        keep=OBk.reshape(rc,J,nzy,rj); other=OBr.reshape(rc,J,nzy,rj)
        e=jnp.stack([jnp.where(c==0,keep,other),jnp.where(c==0,other,keep)],3)
        res[8]=e.transpose(0,2,3,1,4).reshape(rc,2*OBk.shape[1]).astype(F32)
    res[0]=res[0][None]; res[1]=res[1][None]; res[4]=res[4].T; res[5]=res[5].T; res[2]=res[2].reshape(rc); res[7]=res[7].reshape(rc)
    return tuple(res)

def local(layer_input,segment_ids,context_mask,first_gain,attention_in,kernel_weight,kernel_decay,attention_out,second_gain,expand_weight,reduce_weight,cotangent):
    ns=lax.axis_size("seq"); nx=lax.axis_size("grp"); nst=kernel_decay.shape[1]; n=sizes(nx,ns)
    x=layer_input[0]; cot=cotangent[0]
    low,tail_low,packed,ctx,pairs,h3,decay3,weight3,cot_sib=front(ns,x,cot,first_gain[None],kernel_decay.T,kernel_weight.T,attention_in)
    probs,attended,residual,low2=attention(packed,pairs,segment_ids,context_mask[0],x,attention_out,second_gain[None])
    got=main(n,ns,low2,cot,cot_sib,expand_weight,reduce_weight,residual,second_gain[None],attended,attention_out,packed,pairs,probs,low,tail_low,ctx,attention_in,x,first_gain[None],decay3,weight3,h3)
    return closing(n,*got,nst)

def solution(mesh):
    ins=(P("grp","seq",None),P("grp","seq"),P("grp","seq",None))+(P(),)*8+(P("grp","seq",None),)
    outs=(P("grp","seq",None),)*2+(P("seq"),)+(P("seq",None),)*4+(P("seq"),)+(P("seq",None),)*2
    return jax.shard_map(local,mesh=mesh,in_specs=ins,out_specs=outs,check_vma=False)
```
